256 devices in a mesh: batch: 4 (over y), ctx: 16 (over z, core), tower: 4 (over x).
Axes of the slice: x: 4, y: 4, z: 8, core: 2. Of those that a mesh axis runs over, the one named last changes fastest.
Arguments:
- video_q: bfloat16 [4, 8192, 1536], P('batch', ('ctx', 'tower')), may hold values from -20 to 20
- video_k: bfloat16 [4, 8192, 1536], P('batch', ('ctx', 'tower')), may hold values from -20 to 20
- video_v: bfloat16 [4, 8192, 1536], P('batch', ('ctx', 'tower')), may hold values from -6 to 6
- audio_q: bfloat16 [4, 1536, 1536], P('batch', 'tower'), may hold values from -20 to 20
- audio_k: bfloat16 [4, 1536, 1536], P('batch', 'tower'), may hold values from -20 to 20
- audio_v: bfloat16 [4, 1536, 1536], P('batch', 'tower'), may hold values from -6 to 6
- margin: int32 [4, 64, 3], P('batch'), may hold values from 0 to 63, as said below
- out_weight: bfloat16 [3, 12, 128, 3072], P(None, 'tower', 'batch'), may hold values from -0.21875 to 0.21875
- gate_gains: float32 [4, 2, 3072], P('batch'), may hold values from 0.5 to 1.5
Outputs:
- video_out: bfloat16 [4, 8192, 3072], P('batch', ('ctx', 'tower'))
- audio_out: bfloat16 [4, 1536, 3072], P('batch', ('ctx', 'tower'))
The draws below stay inside these ranges and needn't reach their ends.
Inputs may be any that keep to these rules, and one draw needn't show every extreme that they name: margin[c, i, 0] = i, and every entry of margin[c, i, :] lies within 2 of i.
All inputs are finite; a program needn't handle non-finite values.
Results may differ from the reference program's by a relative error of at most 0.017.
Values may be sent and summed in bfloat16 or wider, within the bound.
No kernel may reach another device: no remote copies, remote signals or barrier semaphores. Data moves between devices by JAX's collectives and lax.ppermute only.
A program may use at most 128 MiB of HBM per device.

```python
import math
import jax
import jax.numpy as jnp
from jax import lax

D = 3072
H = 12
HD = 128
VBLK = 128
LIST = 3
CLIPS = 4
VT = 8192
AT = 1536
HW = 1536
NB = 64
ABLK = 24
N_TOWER = 4


def drawn_normal(key, row_total, noise_scale):
    values = noise_scale * jax.random.normal(key, (CLIPS, row_total, HW))
    return jnp.clip(values, -20.0, 20.0).astype(jnp.bfloat16)


def draw_video_q(key, part):
    key = jax.random.fold_in(key, 1)
    return drawn_normal(key, VT, 2.0)


def draw_video_k(key, part):
    key = jax.random.fold_in(key, 2)
    return drawn_normal(key, VT, 1.0)


def draw_audio_q(key, part):
    key = jax.random.fold_in(key, 3)
    return drawn_normal(key, AT, 2.0)


def draw_audio_k(key, part):
    key = jax.random.fold_in(key, 4)
    return drawn_normal(key, AT, 1.0)


def draw_margin(key, part):
    key = jax.random.fold_in(key, 5)
    centres = jnp.broadcast_to(jnp.arange(NB, dtype=jnp.int32)[None, :, None], (CLIPS, NB, LIST - 1))
    offsets = jax.random.randint(key, (CLIPS, NB, LIST - 1), -2, 3, dtype=jnp.int32)
    others = jnp.clip(centres + offsets, 0, NB - 1)
    first_column = jnp.broadcast_to(jnp.arange(NB, dtype=jnp.int32)[None, :, None], (CLIPS, NB, 1))
    return jnp.concatenate([first_column, others], axis=2).astype(jnp.int32)


def steps_of(key, extent, pieces, low, high):
    level, own = 1.0, jax.random.fold_in(key, 6)
    for dim, shards_of in pieces:
        draws = jnp.exp(jax.random.uniform(jax.random.fold_in(own, dim), (shards_of,), jnp.float32, low / len(pieces), high / len(pieces)))
        level = level * jnp.repeat(draws, extent[dim] // shards_of).reshape([-1 if axis == dim else 1 for axis in range(len(extent))])
    return level


def gaussian(key, dims, deviation, reach, cuts=(), held_as=jnp.bfloat16):
    loudness = steps_of(key, dims, cuts, -0.22, 0.18) if cuts else 1.0
    values = jax.random.normal(key, dims, jnp.float32) * deviation * loudness
    return jnp.minimum(jnp.maximum(values, -reach), reach).astype(held_as)


def setup_inputs(seed: int = 0) -> dict:
    keys = jax.random.split(jax.random.key(seed), 10)
    return {
        "video_q": draw_video_q(jax.random.fold_in(keys[9], 71), 0),
        "video_k": draw_video_k(jax.random.fold_in(keys[9], 71), 0),
        "video_v": gaussian(keys[2], (CLIPS, VT, HW), 1.0, 6.0, ((0, 4), (1, 64))),
        "audio_q": draw_audio_q(jax.random.fold_in(keys[9], 71), 0),
        "audio_k": draw_audio_k(jax.random.fold_in(keys[9], 71), 0),
        "audio_v": gaussian(keys[5], (CLIPS, AT, HW), 1.0, 6.0, ((0, 4), (1, 4))),
        "margin": draw_margin(jax.random.fold_in(keys[9], 71), 0),
        "out_weight": gaussian(keys[7], (3, H, HD, D), (HW // 2) ** -0.5, 0.21875, ((1, 4), (2, 4))),
        "gate_gains": jnp.clip(1.0 + 0.1 * jax.random.normal(keys[8], (CLIPS, 2, D), jnp.float32), 0.5, 1.5),
    }


NEGATIVE = -1.0e30


def attend_rows(query_matrix, key_row_matrix, value_row_matrix, allowed):
    softmax_scale = query_matrix.shape[-1] ** -0.5
    scores = jnp.dot(query_matrix, key_row_matrix.T, preferred_element_type=jnp.float32) * softmax_scale
    scores = jnp.where(allowed > 0, scores, NEGATIVE)
    maxima = jnp.max(scores, axis=-1, keepdims=True)
    attention_weights = jnp.exp(scores - maxima)
    totals = jnp.sum(attention_weights, axis=-1, keepdims=True)
    summed = jnp.dot(attention_weights.astype(jnp.bfloat16), value_row_matrix, preferred_element_type=jnp.float32)
    return (summed / totals).astype(jnp.bfloat16)


def attend_heads(query_matrix, key_row_matrix, value_row_matrix, allowed):
    row_total = query_matrix.shape[0]
    step_rows = math.gcd(row_total, 512)
    blocks_count = row_total // step_rows
    mask_blocks = allowed.reshape(blocks_count, step_rows, allowed.shape[1])
    head_queries = jnp.transpose(query_matrix, (1, 0, 2))
    head_keys = jnp.transpose(key_row_matrix, (1, 0, 2))
    head_values = jnp.transpose(value_row_matrix, (1, 0, 2))

    def one_head(triple):
        query_head, key_head, value_head = triple
        query_blocks = query_head.reshape(blocks_count, step_rows, query_head.shape[1])

        def one_block(pair):
            return attend_rows(pair[0], key_head, value_head, pair[1])

        result = lax.map(one_block, (query_blocks, mask_blocks))
        return result.reshape(row_total, query_head.shape[1])

    heads_out = lax.map(one_head, (head_queries, head_keys, head_values))
    return jnp.transpose(heads_out, (1, 0, 2))


def reference(video_q, video_k, video_v, audio_q, audio_k, audio_v, margin, out_weight, gate_gains):
    group_heads = H // N_TOWER
    video_outs = []
    audio_outs = []
    for clip_index in range(CLIPS):
        video_queries = video_q[clip_index].reshape(VT, H, HD)
        video_keys = video_k[clip_index].reshape(VT, H, HD)
        video_values = video_v[clip_index].reshape(VT, H, HD)
        audio_queries = audio_q[clip_index].reshape(AT, H, HD)
        audio_keys = audio_k[clip_index].reshape(AT, H, HD)
        audio_values = audio_v[clip_index].reshape(AT, H, HD)
        linked_blocks = jnp.any(margin[clip_index][:, :, None] == jnp.arange(NB, dtype=jnp.int32)[None, None, :], axis=1)
        token_links = jnp.repeat(jnp.repeat(linked_blocks, VBLK, axis=0), ABLK, axis=1).astype(jnp.int32)
        every_pair = jnp.ones((VT, VT), dtype=jnp.int32)
        video_self = attend_heads(video_queries, video_keys, video_values, every_pair)
        video_cross = attend_heads(video_queries, audio_keys, audio_values, token_links)
        audio_mix = attend_heads(audio_queries, video_keys, video_values, jnp.transpose(token_links))
        video_total_sum = jnp.zeros((VT, D), jnp.float32)
        audio_sum = jnp.zeros((AT, D), jnp.float32)
        for group_index in range(N_TOWER):
            low = group_index * group_heads
            high = low + group_heads
            video_part = jnp.einsum("nhd,hde->ne", video_self[:, low:high].astype(jnp.float32), out_weight[0, low:high].astype(jnp.float32))
            video_part = video_part + jnp.einsum("nhd,hde->ne", video_cross[:, low:high].astype(jnp.float32), out_weight[1, low:high].astype(jnp.float32))
            video_part = lax.optimization_barrier(video_part.astype(jnp.bfloat16))
            video_total_sum = video_total_sum + video_part.astype(jnp.float32)
            audio_part = jnp.einsum("nhd,hde->ne", audio_mix[:, low:high].astype(jnp.float32), out_weight[2, low:high].astype(jnp.float32))
            audio_part = lax.optimization_barrier(audio_part.astype(jnp.bfloat16))
            audio_sum = audio_sum + audio_part.astype(jnp.float32)
        video_outs.append((gate_gains[clip_index, 0][None, :] * video_total_sum).astype(jnp.bfloat16))
        audio_outs.append((gate_gains[clip_index, 1][None, :] * audio_sum).astype(jnp.bfloat16))
    return jnp.stack(video_outs), jnp.stack(audio_outs)
```

```python
import functools

import jax
import jax.numpy as jnp
from jax import lax
from jax.experimental import pallas as pl
from jax.experimental.pallas import tpu as pltpu
from jax.sharding import PartitionSpec as P

H = 12
HD = 128
VBLK = 128
ABLK = 24
TOWERS = 4
CHIPS = 8
LOCAL = H // TOWERS
GW = LOCAL * HD
NEG = -1e30
SCALE2 = HD**-0.5 * 1.4426950408889634
MIB = 1024 * 1024


def nt_dot(a, b):
    return lax.dot_general(a, b, (((1,), (1,)), ((), ())), preferred_element_type=jnp.float32)


def nn_dot(a, b):
    return jnp.dot(a, b, preferred_element_type=jnp.float32)


def full(shape):
    return pl.BlockSpec(shape, lambda *_: (0,) * len(shape))


def pack_video_kernel(place, q_ref, k_ref, v_ref, *outs):
    tower = place[1]
    for step in range(TOWERS):
        first = pl.multiple_of(lax.rem(tower + step, TOWERS) * GW, 128)
        columns = pl.ds(first, GW)
        outs[step][0] = k_ref[:, columns]
        outs[step][1] = v_ref[:, columns]
        outs[TOWERS + step][...] = q_ref[:, columns]


def pack_video(place, q, k, v):
    rows = q.shape[0]
    kv = jax.ShapeDtypeStruct((2, rows, GW), jnp.bfloat16)
    qs = jax.ShapeDtypeStruct((rows, GW), jnp.bfloat16)
    outs = pl.pallas_call(
        pack_video_kernel,
        out_shape=[kv] * TOWERS + [qs] * TOWERS,
        grid_spec=pltpu.PrefetchScalarGridSpec(
            num_scalar_prefetch=1,
            grid=(1,),
            in_specs=[full(q.shape)] * 3,
            out_specs=[full(kv.shape)] * TOWERS + [full(qs.shape)] * TOWERS,
        ),
        compiler_params=pltpu.CompilerParams(vmem_limit_bytes=24 * MIB),
        name="pack_video",
    )(place, q, k, v)
    return outs[:TOWERS], outs[TOWERS:]


WIN = 192
HALO = 48
QROWS = 96


def main_first(ctx):
    return jnp.clip(lax.rem(ctx, 4) * QROWS - HALO, 0, 384 - WIN)


def pack_audio_kernel(place, q_ref, k_ref, v_ref, *outs):
    ctx, tower = place[0], place[1]
    phase = lax.rem(ctx, 4)
    main = pl.multiple_of(main_first(ctx), 16)
    mine = pl.multiple_of(phase * QROWS, 16)
    halo = pl.multiple_of(jnp.where(phase == 0, 384 - HALO, 0), 16)
    for step in range(TOWERS):
        first = pl.multiple_of(lax.rem(tower + step, TOWERS) * GW, 128)
        columns = pl.ds(first, GW)
        outs[step][pl.ds(0, WIN), :] = k_ref[pl.ds(main, WIN), columns]
        outs[step][pl.ds(WIN, WIN), :] = v_ref[pl.ds(main, WIN), columns]
        outs[step][pl.ds(2 * WIN, QROWS), :] = q_ref[pl.ds(mine, QROWS), columns]
        outs[TOWERS + step][pl.ds(0, HALO), :] = k_ref[pl.ds(halo, HALO), columns]
        outs[TOWERS + step][pl.ds(HALO, HALO), :] = v_ref[pl.ds(halo, HALO), columns]


def pack_audio(place, q, k, v):
    main = jax.ShapeDtypeStruct((2 * WIN + QROWS, GW), jnp.bfloat16)
    halo = jax.ShapeDtypeStruct((2 * HALO, GW), jnp.bfloat16)
    outs = pl.pallas_call(
        pack_audio_kernel,
        out_shape=[main] * TOWERS + [halo] * TOWERS,
        grid_spec=pltpu.PrefetchScalarGridSpec(
            num_scalar_prefetch=1,
            grid=(1,),
            in_specs=[full(q.shape)] * 3,
            out_specs=[full(main.shape)] * TOWERS + [full(halo.shape)] * TOWERS,
        ),
        compiler_params=pltpu.CompilerParams(vmem_limit_bytes=32 * MIB),
        name="pack_audio",
    )(place, q, k, v)
    return outs[:TOWERS], outs[TOWERS:]


def flash_kernel(kv_count, first, last, *refs):
    q_refs = refs[:TOWERS]
    kv_refs = refs[TOWERS : TOWERS + kv_count]
    rest = refs[TOWERS + kv_count :]
    if first:
        acc_in = stat_in = None
        outs = rest
    else:
        acc_in, stat_in = rest[:2]
        outs = rest[2:]
    for pair in range(TOWERS // 2):
        rows = pl.ds(pair * 2 * VBLK, 2 * VBLK)
        query = jnp.concatenate([q_refs[2 * pair][...], q_refs[2 * pair + 1][...]], axis=0)
        scores = [nt_dot(query, kv[0]) for kv in kv_refs]
        top = functools.reduce(
            jnp.maximum, [jnp.max(s, axis=1, keepdims=True) for s in scores]
        ) * SCALE2
        if not first:
            stat = stat_in[rows, :]
            old_top, old_total = stat[:, 0:1], stat[:, 64:65]
            top = jnp.maximum(top, old_top)
            factor = jnp.exp2(old_top - top)
        total = None
        acc = None
        for s, kv in zip(scores, kv_refs):
            weights = jnp.exp2(s * SCALE2 - top)
            part = jnp.sum(weights, axis=1, keepdims=True)
            total = part if total is None else total + part
            part = nn_dot(weights.astype(jnp.bfloat16), kv[1])
            acc = part if acc is None else acc + part
        if not first:
            total = total + old_total * factor
            acc = acc + acc_in[rows, :] * factor
        if last:
            out = (acc / total).astype(jnp.bfloat16)
            outs[2 * pair][...] = out[:VBLK]
            outs[2 * pair + 1][...] = out[VBLK:]
        else:
            outs[0][rows, :] = acc
            lane = lax.broadcasted_iota(jnp.int32, (2 * VBLK, HD), 1)
            outs[1][rows, :] = jnp.where(lane < 64, top, total)


def flash(queries, kvs, state, last):
    rows = TOWERS * VBLK
    keys = sum(kv.shape[1] for kv in kvs)
    wide = jax.ShapeDtypeStruct((rows, GW), jnp.float32)
    head = pl.BlockSpec((rows, HD), lambda h: (0, h))
    small = pl.BlockSpec((VBLK, HD), lambda h: (0, h))
    if last:
        out_shape = [jax.ShapeDtypeStruct((VBLK, GW), jnp.bfloat16)] * TOWERS
        out_specs = [small] * TOWERS
    else:
        out_shape = [wide, wide]
        out_specs = [head, head]
    return pl.pallas_call(
        functools.partial(flash_kernel, len(kvs), state is None, last),
        out_shape=out_shape,
        grid=(LOCAL,),
        in_specs=[small] * TOWERS
        + [pl.BlockSpec((2, kv.shape[1], HD), lambda h: (0, 0, h)) for kv in kvs]
        + ([] if state is None else [head, head]),
        out_specs=out_specs,
        compiler_params=pltpu.CompilerParams(vmem_limit_bytes=48 * MIB),
        cost_estimate=pl.CostEstimate(
            flops=8 * rows * keys * GW,
            bytes_accessed=4 * keys * GW + 16 * rows * GW,
            transcendentals=rows * keys * LOCAL,
        ),
        name="flash",
    )(*queries, *kvs, *(() if state is None else state))


def masked_rows(query, key_rows, value_rows, biases):
    scores = [nt_dot(query, k) * SCALE2 + b for k, b in zip(key_rows, biases)]
    top = functools.reduce(jnp.maximum, [jnp.max(s, axis=1, keepdims=True) for s in scores])
    weights = [jnp.exp2(s - top) for s in scores]
    total = functools.reduce(jnp.add, [jnp.sum(w, axis=1, keepdims=True) for w in weights])
    acc = functools.reduce(
        jnp.add, [nn_dot(w.astype(jnp.bfloat16), v) for w, v in zip(weights, value_rows)]
    )
    return (acc / total).astype(jnp.bfloat16)


def cross_kernel(place, margin, *refs):
    q_refs, (main, halo), outs = refs[:TOWERS], refs[TOWERS : TOWERS + 2], refs[TOWERS + 2 :]
    ctx, tower = place[0], place[1]
    phase = lax.rem(ctx, 4)
    base = (ctx - phase) * 4
    lane = lax.broadcasted_iota(jnp.int32, (1, WIN), 1) // ABLK
    main_ids = lane + base + lax.div(main_first(ctx), ABLK)
    small_lane = lax.broadcasted_iota(jnp.int32, (1, HALO), 1) // ABLK
    halo_base = jnp.where(phase == 0, base - 2, jnp.where(phase == 3, base + 16, -100))
    halo_ids = small_lane + halo_base
    keys = [main[pl.ds(0, WIN), :], halo[pl.ds(0, HALO), :]]
    values = [main[pl.ds(WIN, WIN), :], halo[pl.ds(HALO, HALO), :]]
    for step in range(TOWERS):
        block = ctx * 4 + lax.rem(tower - step + TOWERS, TOWERS)
        entries = [margin[block, j] for j in range(3)]
        biases = []
        for ids in (main_ids, halo_ids):
            hit = (ids == entries[0]) | (ids == entries[1]) | (ids == entries[2])
            biases.append(jnp.where(hit, 0.0, NEG).astype(jnp.float32))
        outs[step][...] = masked_rows(q_refs[step][...], keys, values, biases)


def cross(place, margin, queries, main, halo):
    small = pl.BlockSpec((VBLK, HD), lambda h, *_: (0, h))
    return pl.pallas_call(
        cross_kernel,
        out_shape=[jax.ShapeDtypeStruct((VBLK, GW), jnp.bfloat16)] * TOWERS,
        grid_spec=pltpu.PrefetchScalarGridSpec(
            num_scalar_prefetch=2,
            grid=(LOCAL,),
            in_specs=[small] * TOWERS
            + [pl.BlockSpec((a.shape[0], HD), lambda h, *_: (0, h)) for a in (main, halo)],
            out_specs=[small] * TOWERS,
        ),
        compiler_params=pltpu.CompilerParams(vmem_limit_bytes=32 * MIB),
        cost_estimate=pl.CostEstimate(
            flops=8 * 512 * 256 * GW, bytes_accessed=2 * MIB, transcendentals=512 * 256 * 3
        ),
        name="cross",
    )(place, margin, *queries, main, halo)


def audio_kernel(sources, place, margin, *refs):
    q_ref = refs[0]
    kv_refs = refs[1 : 1 + len(sources)]
    outs = refs[1 + len(sources) :]
    ctx, tower = place[0], place[1]
    core = lax.rem(ctx, 2)
    sibling = ctx + 1 - 2 * core
    for step in range(TOWERS):
        wanted = lax.rem(tower - step + TOWERS, TOWERS)
        audio_block = ctx * 4 + wanted
        biases = []
        for (shift, swap, steps), kv in zip(sources, kv_refs):
            owner = lax.rem((sibling if swap else ctx) + shift + 16, 16)
            parts = []
            for other in steps:
                block = owner * 4 + lax.rem(tower - other + TOWERS, TOWERS)
                hit = (
                    (margin[block, 0] == audio_block)
                    | (margin[block, 1] == audio_block)
                    | (margin[block, 2] == audio_block)
                )
                parts.append(jnp.full((1, VBLK), jnp.where(hit, 0.0, NEG), jnp.float32))
            biases.append(jnp.concatenate(parts, axis=1) if len(parts) > 1 else parts[0])
        outs[step][...] = masked_rows(
            q_ref[wanted], [kv[0] for kv in kv_refs], [kv[1] for kv in kv_refs], biases
        )


def audio_mix(place, margin, query, sources, kvs):
    small = pl.BlockSpec((ABLK, HD), lambda h, *_: (0, h))
    return pl.pallas_call(
        functools.partial(audio_kernel, sources),
        out_shape=[jax.ShapeDtypeStruct((ABLK, GW), jnp.bfloat16)] * TOWERS,
        grid_spec=pltpu.PrefetchScalarGridSpec(
            num_scalar_prefetch=2,
            grid=(LOCAL,),
            in_specs=[pl.BlockSpec((TOWERS, ABLK, HD), lambda h, *_: (0, 0, h))]
            + [pl.BlockSpec((2, kv.shape[1], HD), lambda h, *_: (0, 0, h)) for kv in kvs],
            out_specs=[small] * TOWERS,
        ),
        compiler_params=pltpu.CompilerParams(vmem_limit_bytes=32 * MIB),
        cost_estimate=pl.CostEstimate(
            flops=8 * 128 * 2048 * GW, bytes_accessed=4 * MIB, transcendentals=128 * 2048 * 3
        ),
        name="audio_mix",
    )(place, margin, query, *kvs)


def shift_tower(value, step):
    return lax.ppermute(value, "tower", [(i, (i + step) % TOWERS) for i in range(TOWERS)])


def shift_chip(value, step):
    total = 2 * CHIPS
    return lax.ppermute(value, "ctx", [(i, (i + 2 * step) % total) for i in range(total)])


def swap_core(value):
    return lax.ppermute(value, "ctx", [(i, i ^ 1) for i in range(2 * CHIPS)])


def ctx_towers(pairs):
    return [(c * TOWERS + s, c * TOWERS + d) for c, s, d in pairs]


def spread_audio(mains, halos, ctx, tower):
    main = jnp.where(tower == ctx // 4, mains[0], jnp.zeros_like(mains[0]))
    edge = jnp.where(lax.rem(ctx, 4) == 0, ctx // 4 - 1, ctx // 4 + 1)
    has_edge = (lax.rem(ctx, 4) == 0) | (lax.rem(ctx, 4) == 3)
    halo = jnp.where(has_edge & (tower == edge), halos[0], jnp.zeros_like(halos[0]))
    for step in range(1, TOWERS):
        pairs = [(c, c // 4, (c // 4 + step) % TOWERS) for c in range(16)]
        main = main + lax.ppermute(mains[step], ("ctx", "tower"), ctx_towers(pairs))
        pairs = []
        for c in range(16):
            source = c // 4 - 1 if c % 4 == 0 else c // 4 + 1
            if c % 4 in (0, 3) and 0 <= source < TOWERS:
                pairs.append((c, source, (source + step) % TOWERS))
        halo = halo + lax.ppermute(halos[step], ("ctx", "tower"), ctx_towers(pairs))
    return main, halo


def ring(shard, tail):
    steps = [[shard, swap_core(shard)]]
    up = down = shard
    for _ in range(3):
        up, down = shift_chip(up, 1), shift_chip(down, -1)
        steps.append([up, down, swap_core(up), swap_core(down)])
    last = []
    for piece, way in tail(up, down):
        piece = shift_chip(piece, way)
        last += [piece, swap_core(piece)]
    steps.append(last)
    return steps


def shards(video_q, video_k, video_v, audio_q, audio_k, audio_v, margin, out_weight, gate_gains):
    ctx = lax.axis_index("ctx")
    tower = lax.axis_index("tower")
    place = jnp.stack([ctx, tower]).astype(jnp.int32)
    weights = lax.all_gather(out_weight, "batch", axis=2, tiled=True)

    kv_parts, q_parts = pack_video(place, video_q[0], video_k[0], video_v[0])
    near = kv_parts[0]
    far_parts = [shift_tower(kv_parts[step], step) for step in range(1, TOWERS)]
    far = jnp.concatenate(far_parts, axis=1)
    queries = [q_parts[0]] + [shift_tower(q_parts[step], step) for step in range(1, TOWERS)]

    near_ring = ring(near, lambda up, down: [(up, 1)])
    far_ring = ring(far, lambda up, down: [(up[:, :VBLK], 1), (down[:, VBLK:], -1)])

    aq, ak, av, far0 = lax.optimization_barrier((audio_q[0], audio_k[0], audio_v[0], far))
    mains, halos = pack_audio(place, aq, ak, av)
    main, halo = spread_audio(mains, halos, ctx, tower)
    video_cross = cross(place, margin[0], queries, main, halo)

    state = None
    for step, (a, b) in enumerate(zip(near_ring, far_ring)):
        last = step == len(near_ring) - 1
        state = flash(queries, list(a) + list(b), state, last)
    video_self = state

    sources = []
    kvs = []
    for pieces, kinds in ((near_ring, (0,)), (far_ring, (1, 2, 3))):
        own, sibling = pieces[0]
        up, down, up_other, down_other = pieces[1]
        kvs += [own, sibling, up_other, down_other]
        sources += [(0, False, kinds), (0, True, kinds), (-2, True, kinds), (2, True, kinds)]
    audio_query = main[2 * WIN :].reshape(TOWERS, ABLK, GW)
    mixed = audio_mix(place, margin[0], audio_query, tuple(sources), kvs)

    flat = weights.reshape(3, GW, weights.shape[-1])
    gains = gate_gains[0]
    audio_sum = nn_dot(mixed[0], flat[2]).astype(jnp.bfloat16).astype(jnp.float32)
    for step in range(1, TOWERS):
        part = nn_dot(mixed[step], flat[2]).astype(jnp.bfloat16)
        audio_sum = audio_sum + shift_tower(part, -step).astype(jnp.float32)
    audio_out = (gains[1][None] * audio_sum).astype(jnp.bfloat16)[None]

    cross_terms = [nn_dot(video_cross[step], flat[1]) for step in range(TOWERS)]
    video_sum = jnp.zeros_like(cross_terms[0])
    for step in (2, 1, 3, 0):
        part = (nn_dot(video_self[step], flat[0]) + cross_terms[step]).astype(jnp.bfloat16)
        part = shift_tower(part, -step) if step else part
        video_sum = video_sum + part.astype(jnp.float32)
    video_out = (gains[0][None] * video_sum).astype(jnp.bfloat16)[None]
    return (video_out, audio_out)


def solution(mesh):
    return jax.shard_map(
        shards,
        mesh=mesh,
        in_specs=(
            P("batch", ("ctx", "tower"), None),
            P("batch", ("ctx", "tower"), None),
            P("batch", ("ctx", "tower"), None),
            P("batch", "tower", None),
            P("batch", "tower", None),
            P("batch", "tower", None),
            P("batch", None, None),
            P(None, "tower", "batch", None),
            P("batch", None, None),
        ),
        out_specs=(P("batch", ("ctx", "tower"), None), P("batch", ("ctx", "tower"), None)),
        check_vma=False,
    )
```

```python
import functools

import jax
import jax.numpy as jnp
from jax import lax
from jax.experimental import pallas as pl
from jax.experimental.pallas import tpu as pltpu
from jax.sharding import PartitionSpec as P

H = 12
HD = 128
VBLK = 128
ABLK = 24
TOWERS = 4
CHIPS = 8
LOCAL = H // TOWERS
GW = LOCAL * HD
NEG = -1e30
SCALE2 = HD**-0.5 * 1.4426950408889634
MIB = 1024 * 1024
VMEM = 60 * MIB


def nt_dot(a, b):
    return lax.dot_general(a, b, (((1,), (1,)), ((), ())), preferred_element_type=jnp.float32)


def nn_dot(a, b):
    return jnp.dot(a, b, preferred_element_type=jnp.float32)


def full(shape):
    return pl.BlockSpec(shape, lambda *_: (0,) * len(shape))


def pack_video_kernel(q_ref, k_ref, v_ref, kv_out, q_out):
    kv_out[0, 0] = k_ref[...]
    kv_out[0, 1] = v_ref[...]
    q_out[0] = q_ref[...]


def pack_video(q, k, v):
    rows = q.shape[0]
    group = pl.BlockSpec((rows, GW), lambda g: (0, g))
    return pl.pallas_call(
        pack_video_kernel,
        out_shape=[
            jax.ShapeDtypeStruct((TOWERS, 2, rows, GW), jnp.bfloat16),
            jax.ShapeDtypeStruct((TOWERS, rows, GW), jnp.bfloat16),
        ],
        grid=(TOWERS,),
        in_specs=[group] * 3,
        out_specs=[
            pl.BlockSpec((1, 2, rows, GW), lambda g: (g, 0, 0, 0)),
            pl.BlockSpec((1, rows, GW), lambda g: (g, 0, 0)),
        ],
        compiler_params=pltpu.CompilerParams(vmem_limit_bytes=VMEM),
        name="pack_video",
    )(q, k, v)


WIN = 192
HALO = 48
QROWS = 96
QAT = 2 * WIN
HAT = QAT + QROWS
AROWS = HAT + 2 * HALO


def main_first(ctx):
    return jnp.clip(lax.rem(ctx, 4) * QROWS - HALO, 0, 384 - WIN)


def edge_tower(ctx):
    return jnp.clip(jnp.where(lax.rem(ctx, 4) == 0, ctx // 4 - 1, ctx // 4 + 1), 0, TOWERS - 1)


def pack_audio_kernel(place, q_ref, k_ref, v_ref, out):
    ctx = place[0]
    phase = lax.rem(ctx, 4)
    main = pl.multiple_of(main_first(ctx), 16)
    mine = pl.multiple_of(phase * QROWS, 16)
    halo = pl.multiple_of(jnp.where(phase == 0, 384 - HALO, 0), 16)
    out[0, pl.ds(0, WIN), :] = k_ref[pl.ds(main, WIN), :]
    out[0, pl.ds(WIN, WIN), :] = v_ref[pl.ds(main, WIN), :]
    out[0, pl.ds(QAT, QROWS), :] = q_ref[pl.ds(mine, QROWS), :]
    out[0, pl.ds(HAT, HALO), :] = k_ref[pl.ds(halo, HALO), :]
    out[0, pl.ds(HAT + HALO, HALO), :] = v_ref[pl.ds(halo, HALO), :]


def pack_audio(place, q, k, v):
    group = pl.BlockSpec((q.shape[0], GW), lambda g, *_: (0, g))
    return pl.pallas_call(
        pack_audio_kernel,
        out_shape=jax.ShapeDtypeStruct((TOWERS, AROWS, GW), jnp.bfloat16),
        grid_spec=pltpu.PrefetchScalarGridSpec(
            num_scalar_prefetch=1,
            grid=(TOWERS,),
            in_specs=[group] * 3,
            out_specs=pl.BlockSpec((1, AROWS, GW), lambda g, *_: (g, 0, 0)),
        ),
        compiler_params=pltpu.CompilerParams(vmem_limit_bytes=VMEM),
        name="pack_audio",
    )(place, q, k, v)


def rows_of(kv_ref, which):
    return jnp.concatenate([kv_ref[r, which] for r in range(TOWERS)], axis=0)


def flash_kernel(kv_count, first, last, *refs):
    q_ref = refs[0]
    kv_refs = refs[1 : 1 + kv_count]
    rest = refs[1 + kv_count :]
    if first:
        outs = rest
    else:
        acc_in, stat_in = rest[:2]
        outs = rest[2:]
    size = 2 * VBLK
    for tile in range(TOWERS // 2):
        rows = pl.ds(tile * size, size)
        query = q_ref[rows, :]
        scores = [nt_dot(query, rows_of(kv, 0)) for kv in kv_refs]
        top = functools.reduce(
            jnp.maximum, [jnp.max(s, axis=1, keepdims=True) for s in scores]
        ) * SCALE2
        if not first:
            stat = stat_in[rows, :]
            old_top, old_total = stat[:, 0:1], stat[:, 64:65]
            top = jnp.maximum(top, old_top)
            factor = jnp.exp2(old_top - top)
        total = None
        acc = None
        for s, kv in zip(scores, kv_refs):
            weights = jnp.exp2(s * SCALE2 - top)
            part = jnp.sum(weights, axis=1, keepdims=True)
            total = part if total is None else total + part
            part = nn_dot(weights.astype(jnp.bfloat16), rows_of(kv, 1))
            acc = part if acc is None else acc + part
        if not first:
            total = total + old_total * factor
            acc = acc + acc_in[rows, :] * factor
        if last:
            outs[0][rows, :] = (acc / total).astype(jnp.bfloat16)
        else:
            outs[0][rows, :] = acc
            lane = lax.broadcasted_iota(jnp.int32, (size, HD), 1)
            outs[1][rows, :] = jnp.where(lane < 64, top, total)


def flash(query, kvs, state, last):
    rows = TOWERS * VBLK
    keys = rows * len(kvs)
    wide = jax.ShapeDtypeStruct((rows, GW), jnp.float32)
    head = pl.BlockSpec((rows, HD), lambda h: (0, h))
    if last:
        out_shape = jax.ShapeDtypeStruct((rows, GW), jnp.bfloat16)
        out_specs = head
    else:
        out_shape = [wide, wide]
        out_specs = [head, head]
    shard = pl.BlockSpec((TOWERS, 2, VBLK, HD), lambda h: (0, 0, 0, h))
    return pl.pallas_call(
        functools.partial(flash_kernel, len(kvs), state is None, last),
        out_shape=out_shape,
        grid=(LOCAL,),
        in_specs=[head] + [shard] * len(kvs) + ([] if state is None else [head, head]),
        out_specs=out_specs,
        compiler_params=pltpu.CompilerParams(vmem_limit_bytes=VMEM),
        cost_estimate=pl.CostEstimate(
            flops=8 * rows * keys * GW,
            bytes_accessed=4 * keys * GW + 16 * rows * GW,
            transcendentals=rows * keys * LOCAL,
        ),
        name="flash",
    )(query, *kvs, *(() if state is None else state))


def cross_kernel(place, margin, q_ref, main, edge, out):
    ctx = place[0]
    phase = lax.rem(ctx, 4)
    base = (ctx - phase) * 4
    lane = lax.broadcasted_iota(jnp.int32, (1, 256), 1)
    halo_base = jnp.where(phase == 0, base - 2, jnp.where(phase == 3, base + 16, -100))
    main_base = base + lax.div(main_first(ctx), ABLK)
    ids = jnp.where(lane < WIN, lane // ABLK + main_base, lane // ABLK - WIN // ABLK + halo_base)
    ids = jnp.where(lane < WIN + HALO, ids, -100)
    spare = jnp.zeros((256 - WIN - HALO, HD), jnp.bfloat16)
    keys = jnp.concatenate([main[0, pl.ds(0, WIN), :], edge[0, pl.ds(HAT, HALO), :], spare], axis=0)
    values = jnp.concatenate(
        [main[0, pl.ds(WIN, WIN), :], edge[0, pl.ds(HAT + HALO, HALO), :], spare], axis=0
    )
    scores = nt_dot(q_ref[...], keys) * SCALE2
    parts = []
    for r in range(TOWERS):
        block = ctx * 4 + r
        hit = (ids == margin[block, 0]) | (ids == margin[block, 1]) | (ids == margin[block, 2])
        parts.append(jnp.where(hit, scores[r * VBLK : (r + 1) * VBLK], NEG))
    scores = jnp.concatenate(parts, axis=0)
    weights = jnp.exp2(scores - jnp.max(scores, axis=1, keepdims=True))
    total = jnp.sum(weights, axis=1, keepdims=True)
    out[...] = (nn_dot(weights.astype(jnp.bfloat16), values) / total).astype(jnp.bfloat16)


def cross(place, margin, query, audio):
    rows = query.shape[0]
    head = pl.BlockSpec((rows, HD), lambda h, *_: (0, h))
    return pl.pallas_call(
        cross_kernel,
        out_shape=jax.ShapeDtypeStruct((rows, GW), jnp.bfloat16),
        grid_spec=pltpu.PrefetchScalarGridSpec(
            num_scalar_prefetch=2,
            grid=(LOCAL,),
            in_specs=[
                head,
                pl.BlockSpec((1, AROWS, HD), lambda h, place, margin: (place[2], 0, h)),
                pl.BlockSpec((1, AROWS, HD), lambda h, place, margin: (place[3], 0, h)),
            ],
            out_specs=head,
        ),
        compiler_params=pltpu.CompilerParams(vmem_limit_bytes=VMEM),
        cost_estimate=pl.CostEstimate(
            flops=8 * rows * 256 * GW, bytes_accessed=2 * MIB, transcendentals=rows * 256 * 3
        ),
        name="cross",
    )(place, margin, query, audio, audio)


def audio_kernel(place, margin, audio, own, sibling, third, out):
    ctx = place[0]
    core = lax.rem(ctx, 2)
    owners = (ctx, ctx + 1 - 2 * core, lax.rem(ctx - 1 + 2 * core + 16, 16))
    row_block = lax.broadcasted_iota(jnp.int32, (QROWS, 1), 0) // ABLK + ctx * 4
    query = audio[0, pl.ds(QAT, QROWS), :]
    scores = []
    for owner, kv in zip(owners, (own, sibling, third)):
        s = nt_dot(query, rows_of(kv, 0)) * SCALE2
        for r in range(TOWERS):
            block = owner * 4 + r
            hit = (
                (row_block == margin[block, 0])
                | (row_block == margin[block, 1])
                | (row_block == margin[block, 2])
            )
            scores.append(jnp.where(hit, s[:, r * VBLK : (r + 1) * VBLK], NEG))
    scores = jnp.concatenate(scores, axis=1)
    weights = jnp.exp2(scores - jnp.max(scores, axis=1, keepdims=True))
    total = jnp.sum(weights, axis=1, keepdims=True)
    values = jnp.concatenate([rows_of(kv, 1) for kv in (own, sibling, third)], axis=0)
    out[...] = (nn_dot(weights.astype(jnp.bfloat16), values) / total).astype(jnp.bfloat16)


def audio_mix(place, margin, audio, kvs):
    shard = pl.BlockSpec((TOWERS, 2, VBLK, HD), lambda h, *_: (0, 0, 0, h))
    return pl.pallas_call(
        audio_kernel,
        out_shape=jax.ShapeDtypeStruct((QROWS, GW), jnp.bfloat16),
        grid_spec=pltpu.PrefetchScalarGridSpec(
            num_scalar_prefetch=2,
            grid=(LOCAL,),
            in_specs=[pl.BlockSpec((1, AROWS, HD), lambda h, place, margin: (place[2], 0, h))]
            + [shard] * 3,
            out_specs=pl.BlockSpec((QROWS, HD), lambda h, *_: (0, h)),
        ),
        compiler_params=pltpu.CompilerParams(vmem_limit_bytes=VMEM),
        cost_estimate=pl.CostEstimate(
            flops=8 * 96 * 1536 * GW, bytes_accessed=3 * MIB, transcendentals=96 * 1536 * 3
        ),
        name="audio_mix",
    )(place, margin, audio, *kvs)


def project_kernel(has_base, place, a_ref, mine, other, *refs):
    step = pl.program_id(0)

    def part(w_ref):
        acc = None
        for t in range(TOWERS):
            w = jnp.concatenate(
                [w_ref[b * TOWERS + t, 0, h] for h in range(LOCAL) for b in range(4)], axis=0
            )
            term = nn_dot(a_ref[t], w)
            acc = term if acc is None else acc + term
        if has_base:
            base, gain, out = refs
            out[...] = (gain[...] * (acc + base[...])).astype(out.dtype)
        else:
            refs[0][...] = acc

    @pl.when(step < 3)
    def _():
        part(mine)

    @pl.when(step >= 3)
    def _():
        part(other)


def project(place, a, mine, other, kind, base=None, gain=None):
    width = mine.shape[-1]
    tile = width // 3

    def column(i, place):
        return jnp.where(i < 3, place[4] * 3 + i, (1 - place[4]) * 3 + i - 3)

    block = (16, 1, LOCAL, HD // 4, tile)
    rows = pl.BlockSpec((VBLK, tile), lambda i, place: (0, column(i, place)))
    extra = [] if base is None else [rows, pl.BlockSpec((1, tile), lambda i, place: (0, column(i, place)))]
    dtype = jnp.float32 if base is None else jnp.bfloat16
    return pl.pallas_call(
        functools.partial(project_kernel, base is not None),
        out_shape=jax.ShapeDtypeStruct((VBLK, 2 * width), dtype),
        grid_spec=pltpu.PrefetchScalarGridSpec(
            num_scalar_prefetch=1,
            grid=(6,),
            in_specs=[
                full(a.shape),
                pl.BlockSpec(block, lambda i, place: (0, kind, 0, 0, jnp.minimum(i, 2))),
                pl.BlockSpec(block, lambda i, place: (0, kind, 0, 0, jnp.maximum(i - 3, 0))),
            ]
            + extra,
            out_specs=rows,
        ),
        compiler_params=pltpu.CompilerParams(vmem_limit_bytes=VMEM),
        cost_estimate=pl.CostEstimate(
            flops=2 * VBLK * 1536 * 3072, bytes_accessed=12 * MIB, transcendentals=0
        ),
        name="project",
    )(place, a, mine, other, *(() if base is None else (base, gain)))


def gate_kernel(*refs):
    pass


def gate(value, *after):
    anywhere = pl.BlockSpec(memory_space=pl.ANY)
    return pl.pallas_call(
        gate_kernel,
        out_shape=jax.ShapeDtypeStruct(value.shape, value.dtype),
        in_specs=[anywhere] * (1 + len(after)),
        out_specs=anywhere,
        input_output_aliases={0: 0},
        name="gate",
    )(value, *after)


def exchange_towers(value):
    return lax.all_to_all(value, "tower", split_axis=0, concat_axis=0, tiled=True)


def hop(value):
    total = 2 * CHIPS
    return lax.ppermute(value, "ctx", [(i, (i + 2 - 4 * (i % 2)) % total) for i in range(total)])


def swap_core(value):
    return lax.ppermute(value, "ctx", [(i, i ^ 1) for i in range(2 * CHIPS)])


def shards(video_q, video_k, video_v, audio_q, audio_k, audio_v, margin, out_weight, gate_gains):
    ctx = lax.axis_index("ctx")
    tower = lax.axis_index("tower")
    core = lax.rem(ctx, 2)
    place = jnp.stack([ctx, tower, ctx // 4, edge_tower(ctx), core]).astype(jnp.int32)
    gains = gate_gains[0]
    margins = margin[0]

    kv_parts, q_parts = pack_video(video_q[0], video_k[0], video_v[0])
    own = exchange_towers(kv_parts)
    sibling = swap_core(own)
    near, far = hop(own), hop(sibling)

    half = out_weight.shape[-1] // 2
    narrow = lax.dynamic_slice_in_dim(out_weight[:2], core * half, half, 3)
    w_mine = lax.all_gather(narrow, ("batch", "tower"), axis=0, tiled=False)
    w_audio = lax.all_gather(out_weight[2], "batch", axis=1, tiled=True)

    query = exchange_towers(q_parts).reshape(TOWERS * VBLK, GW)
    state = flash(query, [own, sibling], None, False)
    audio = exchange_towers(pack_audio(place, audio_q[0], audio_k[0], audio_v[0]))
    video_cross = cross(place, margins, query, audio)
    mixed = audio_mix(place, margins, audio, (own, sibling, far))
    near = gate(near, state[1])

    for step in range(1, 4):
        now = [near, far, swap_core(near), swap_core(far)]
        near, far = hop(near), (hop(far) if step < 3 else None)
        state = flash(query, now, state, False)
        if step == 1:
            near = gate(near, state[1], video_cross, mixed)
        if step == 2:
            near = gate(near, state[1])
            w_mine = gate(w_mine, state[1])
    video_self = flash(query, [near, swap_core(near)], state, True)

    w_other = swap_core(w_mine)
    cross_all = exchange_towers(video_cross.reshape(TOWERS, VBLK, GW))
    base = project(place, cross_all, w_mine, w_other, 1)
    self_all = exchange_towers(video_self.reshape(TOWERS, VBLK, GW))
    video_out = project(place, self_all, w_mine, w_other, 0, base, gains[0][None])

    audio_part = nn_dot(mixed, w_audio.reshape(GW, -1)).astype(jnp.bfloat16)
    audio_part = exchange_towers(audio_part.reshape(TOWERS, ABLK, -1))
    audio_sum = jnp.sum(audio_part.astype(jnp.float32), axis=0)
    audio_out = (gains[1][None] * audio_sum).astype(jnp.bfloat16)
    return (video_out[None], audio_out[None])


def solution(mesh):
    return jax.shard_map(
        shards,
        mesh=mesh,
        in_specs=(
            P("batch", ("ctx", "tower"), None),
            P("batch", ("ctx", "tower"), None),
            P("batch", ("ctx", "tower"), None),
            P("batch", "tower", None),
            P("batch", "tower", None),
            P("batch", "tower", None),
            P("batch", None, None),
            P(None, "tower", "batch", None),
            P("batch", None, None),
        ),
        out_specs=(P("batch", ("ctx", "tower"), None), P("batch", ("ctx", "tower"), None)),
        check_vma=False,
    )
```

```python
import functools

import jax
import jax.numpy as jnp
from jax import lax
from jax.experimental import pallas as pl
from jax.experimental.pallas import tpu as pltpu
from jax.sharding import PartitionSpec as P

H = 12
HD = 128
VBLK = 128
ABLK = 24
TOWERS = 4
CHIPS = 8
LOCAL = H // TOWERS
GW = LOCAL * HD
NEG = -1e30
SCALE2 = HD**-0.5 * 1.4426950408889634
MIB = 1024 * 1024


def nt_dot(a, b):
    return lax.dot_general(a, b, (((1,), (1,)), ((), ())), preferred_element_type=jnp.float32)


def nn_dot(a, b):
    return jnp.dot(a, b, preferred_element_type=jnp.float32)


def full(shape):
    return pl.BlockSpec(shape, lambda *_: (0,) * len(shape))


ANY = pl.BlockSpec(memory_space=pl.ANY)


def start_copies(pairs, sem, first):
    copies = [pltpu.make_async_copy(a, b, sem.at[first + i]) for i, (a, b) in enumerate(pairs)]
    for copy in copies:
        copy.start()
    return copies


def pack_video_kernel(place, k_ref, v_ref, q_ref, w_ref, kv_out, q_out, self_out, rest_out, rows, w_rows, sem):
    half = w_ref.shape[3] // 2
    columns = pl.ds(pl.multiple_of(place[4] * half, 128), half)
    coming = start_copies([(ref, rows.at[i]) for i, ref in enumerate((k_ref, v_ref, q_ref))], sem, 0)
    coming += start_copies([(w_ref.at[:, :, :, columns], w_rows)], sem, 3)
    going = []
    for i in range(3):
        coming[i].wait()
        pairs = []
        for g in range(TOWERS):
            target = q_out.at[g] if i == 2 else kv_out.at[g, i]
            pairs.append((rows.at[i, :, pl.ds(g * GW, GW)], target))
        going += start_copies(pairs, sem, 4 + i * TOWERS)
    coming[3].wait()
    going += start_copies([(w_rows.at[0], self_out), (w_rows.at[pl.ds(1, 2)], rest_out)], sem, 16)
    for copy in going:
        copy.wait()


def pack_video(place, k, v, q, w):
    rows = k.shape[0]
    narrow = (LOCAL, w.shape[2], w.shape[3] // 2)
    shapes = [(TOWERS, 2, rows, GW), (TOWERS, rows, GW), narrow, (2,) + narrow]
    return pl.pallas_call(
        pack_video_kernel,
        out_shape=[jax.ShapeDtypeStruct(shape, jnp.bfloat16) for shape in shapes],
        grid_spec=pltpu.PrefetchScalarGridSpec(
            num_scalar_prefetch=1,
            grid=(1,),
            in_specs=[ANY] * 4,
            out_specs=[ANY] * 4,
            scratch_shapes=[
                pltpu.VMEM((3,) + k.shape, jnp.bfloat16),
                pltpu.VMEM((3,) + narrow, jnp.bfloat16),
                pltpu.SemaphoreType.DMA((18,)),
            ],
        ),
        compiler_params=pltpu.CompilerParams(vmem_limit_bytes=60 * MIB),
        name="pack_video",
    )(place, k, v, q, w)


WIN = 192
HALO = 48
QROWS = 96
QAT = 2 * WIN
HAT = QAT + QROWS
AROWS = HAT + 2 * HALO


def main_first(ctx):
    return jnp.clip(lax.rem(ctx, 4) * QROWS - HALO, 0, 384 - WIN)


def edge_tower(ctx):
    return jnp.clip(jnp.where(lax.rem(ctx, 4) == 0, ctx // 4 - 1, ctx // 4 + 1), 0, TOWERS - 1)


def pack_audio_kernel(place, q_ref, k_ref, v_ref, out, rows, sem):
    ctx = place[0]
    phase = lax.rem(ctx, 4)
    main = pl.ds(pl.multiple_of(main_first(ctx), 16), WIN)
    mine = pl.ds(pl.multiple_of(phase * QROWS, 16), QROWS)
    halo = pl.ds(pl.multiple_of(jnp.where(phase == 0, 384 - HALO, 0), 16), HALO)
    coming = start_copies(
        [
            (k_ref.at[main], rows.at[pl.ds(0, WIN)]),
            (v_ref.at[main], rows.at[pl.ds(WIN, WIN)]),
            (q_ref.at[mine], rows.at[pl.ds(QAT, QROWS)]),
            (k_ref.at[halo], rows.at[pl.ds(HAT, HALO)]),
            (v_ref.at[halo], rows.at[pl.ds(HAT + HALO, HALO)]),
        ],
        sem,
        0,
    )
    for copy in coming:
        copy.wait()
    going = start_copies(
        [(rows.at[:, pl.ds(g * GW, GW)], out.at[g]) for g in range(TOWERS)], sem, 5
    )
    for copy in going:
        copy.wait()


def pack_audio(place, q, k, v):
    return pl.pallas_call(
        pack_audio_kernel,
        out_shape=jax.ShapeDtypeStruct((TOWERS, AROWS, GW), jnp.bfloat16),
        grid_spec=pltpu.PrefetchScalarGridSpec(
            num_scalar_prefetch=1,
            grid=(1,),
            in_specs=[ANY] * 3,
            out_specs=ANY,
            scratch_shapes=[
                pltpu.VMEM((AROWS, q.shape[1]), jnp.bfloat16),
                pltpu.SemaphoreType.DMA((9,)),
            ],
        ),
        compiler_params=pltpu.CompilerParams(vmem_limit_bytes=60 * MIB),
        name="pack_audio",
    )(place, q, k, v)


def rows_of(kv_ref, which):
    return jnp.concatenate([kv_ref[r, which] for r in range(TOWERS)], axis=0)


def flash_kernel(kv_count, first, last, *refs):
    q_ref = refs[0]
    kv_refs = refs[1 : 1 + kv_count]
    rest = refs[1 + kv_count :]
    if first:
        outs = rest
    else:
        acc_in, stat_in = rest[:2]
        outs = rest[2:]
    size = TOWERS * VBLK
    scaled = q_ref[...].astype(jnp.float32) * SCALE2
    high = scaled.astype(jnp.bfloat16)
    low = (scaled - high.astype(jnp.float32)).astype(jnp.bfloat16)
    query = jnp.concatenate([high, low], axis=1)
    scores = []
    for kv in kv_refs:
        keys = rows_of(kv, 0)
        scores.append(nt_dot(query, jnp.concatenate([keys, keys], axis=1)))
    top = functools.reduce(jnp.maximum, [jnp.max(s, axis=1, keepdims=True) for s in scores])
    if not first:
        stat = stat_in[...]
        old_top, old_total = stat[:, 0:1], stat[:, 64:65]
        top = jnp.maximum(top, old_top)
        factor = jnp.exp2(old_top - top)
    acc = None
    for s, kv in zip(scores, kv_refs):
        weights = jnp.exp2(s - top).astype(jnp.bfloat16)
        values = rows_of(kv, 1)
        part = nn_dot(weights, jnp.concatenate([values, jnp.ones_like(values)], axis=1))
        acc = part if acc is None else acc + part
    acc, total = acc[:, :HD], acc[:, HD:]
    if not first:
        total = total + old_total * factor
        acc = acc + acc_in[...] * factor
    if last:
        outs[0][...] = (acc / total).astype(jnp.bfloat16)
    else:
        outs[0][...] = acc
        lane = lax.broadcasted_iota(jnp.int32, (size, HD), 1)
        outs[1][...] = jnp.where(lane < 64, top, total)
        outs[2][...] = total[:8]


def flash(query, kvs, state, last):
    rows = TOWERS * VBLK
    keys = rows * len(kvs)
    wide = jax.ShapeDtypeStruct((rows, GW), jnp.float32)
    head = pl.BlockSpec((rows, HD), lambda h: (0, h))
    if last:
        out_shape = jax.ShapeDtypeStruct((rows, GW), jnp.bfloat16)
        out_specs = head
    else:
        out_shape = [wide, wide, jax.ShapeDtypeStruct((8, HD), jnp.float32)]
        out_specs = [head, head, pl.BlockSpec((8, HD), lambda h: (0, 0))]
    shard = pl.BlockSpec((TOWERS, 2, VBLK, HD), lambda h: (0, 0, 0, h))
    return pl.pallas_call(
        functools.partial(flash_kernel, len(kvs), state is None, last),
        out_shape=out_shape,
        grid=(LOCAL,),
        in_specs=[head] + [shard] * len(kvs) + ([] if state is None else [head, head]),
        out_specs=out_specs,
        compiler_params=pltpu.CompilerParams(vmem_limit_bytes=60 * MIB),
        cost_estimate=pl.CostEstimate(
            flops=8 * rows * keys * GW,
            bytes_accessed=4 * keys * GW + 16 * rows * GW,
            transcendentals=rows * keys * LOCAL,
        ),
        name="flash",
    )(query, *kvs, *(() if state is None else state[:2]))


AUDIO_ROWS = 32
BOTH = VBLK + AUDIO_ROWS


def audio_rows(place, margin, audio, own, sibling, third):
    ctx = place[0]
    core = lax.rem(ctx, 2)
    row_block = lax.broadcasted_iota(jnp.int32, (QROWS, 1), 0) // ABLK + ctx * 4
    query = audio[0, pl.ds(QAT, QROWS), :]
    pieces = [(own, r, ctx * 4 + r) for r in range(TOWERS)]
    after = lax.rem(ctx + 1, 16) * 4
    before = lax.rem(ctx + 15, 16) * 4 + 2
    for r in range(2):
        pieces.append((sibling, 2 * core + r, jnp.where(core == 0, after, before) + r))
        pieces.append((third, 2 - 2 * core + r, jnp.where(core == 0, before, after) + r))
    keys = jnp.concatenate([ref[r, 0] for ref, r, _ in pieces], axis=0)
    values = jnp.concatenate([ref[r, 1] for ref, r, _ in pieces], axis=0)
    raw = nt_dot(query, keys) * SCALE2
    scores = []
    for i, (_, _, block) in enumerate(pieces):
        hit = (
            (row_block == margin[block, 0])
            | (row_block == margin[block, 1])
            | (row_block == margin[block, 2])
        )
        scores.append(jnp.where(hit, raw[:, i * VBLK : (i + 1) * VBLK], NEG))
    scores = jnp.concatenate(scores, axis=1)
    weights = jnp.exp2(scores - jnp.max(scores, axis=1, keepdims=True))
    total = jnp.sum(weights, axis=1, keepdims=True)
    return nn_dot(weights.astype(jnp.bfloat16), values) / total


def cross_kernel(place, margin, q_ref, main, edge, own, sibling, third, out):
    ctx = place[0]
    phase = lax.rem(ctx, 4)
    base = (ctx - phase) * 4
    lane = lax.broadcasted_iota(jnp.int32, (1, 256), 1)
    halo_base = jnp.where(phase == 0, base - 2, jnp.where(phase == 3, base + 16, -100))
    main_base = base + lax.div(main_first(ctx), ABLK)
    ids = jnp.where(lane < WIN, lane // ABLK + main_base, lane // ABLK - WIN // ABLK + halo_base)
    ids = jnp.where(lane < WIN + HALO, ids, -100)
    spare = jnp.zeros((256 - WIN - HALO, HD), jnp.bfloat16)
    keys = jnp.concatenate([main[0, pl.ds(0, WIN), :], edge[0, pl.ds(HAT, HALO), :], spare], axis=0)
    values = jnp.concatenate(
        [main[0, pl.ds(WIN, WIN), :], edge[0, pl.ds(HAT + HALO, HALO), :], spare], axis=0
    )
    scores = nt_dot(q_ref[...], keys) * SCALE2
    parts = []
    for r in range(TOWERS):
        block = ctx * 4 + r
        hit = (ids == margin[block, 0]) | (ids == margin[block, 1]) | (ids == margin[block, 2])
        parts.append(jnp.where(hit, scores[r * VBLK : (r + 1) * VBLK], NEG))
    scores = jnp.concatenate(parts, axis=0)
    weights = jnp.exp2(scores - jnp.max(scores, axis=1, keepdims=True))
    total = jnp.sum(weights, axis=1, keepdims=True)
    result = (nn_dot(weights.astype(jnp.bfloat16), values) / total).astype(jnp.bfloat16)
    mixed = audio_rows(place, margin, main, own, sibling, third)
    for r in range(TOWERS):
        out[r, pl.ds(0, VBLK), :] = result[r * VBLK : (r + 1) * VBLK]
        padded = jnp.concatenate(
            [mixed[r * ABLK : (r + 1) * ABLK], jnp.zeros((AUDIO_ROWS - ABLK, HD), jnp.float32)], axis=0
        )
        out[r, pl.ds(VBLK, AUDIO_ROWS), :] = padded.astype(jnp.bfloat16)


def cross(place, margin, query, audio, own, sibling, third):
    rows = query.shape[0]
    shard = pl.BlockSpec((TOWERS, 2, VBLK, HD), lambda h, *_: (0, 0, 0, h))
    return pl.pallas_call(
        cross_kernel,
        out_shape=jax.ShapeDtypeStruct((TOWERS, BOTH, GW), jnp.bfloat16),
        grid_spec=pltpu.PrefetchScalarGridSpec(
            num_scalar_prefetch=2,
            grid=(LOCAL,),
            in_specs=[
                pl.BlockSpec((rows, HD), lambda h, *_: (0, h)),
                pl.BlockSpec((1, AROWS, HD), lambda h, place, margin: (place[2], 0, h)),
                pl.BlockSpec((1, AROWS, HD), lambda h, place, margin: (place[3], 0, h)),
                shard,
                shard,
                shard,
            ],
            out_specs=pl.BlockSpec((TOWERS, BOTH, HD), lambda h, *_: (0, 0, h)),
        ),
        compiler_params=pltpu.CompilerParams(vmem_limit_bytes=60 * MIB),
        cost_estimate=pl.CostEstimate(
            flops=8 * rows * 1024 * GW, bytes_accessed=4 * MIB, transcendentals=rows * 512 * 3
        ),
        name="cross",
    )(place, margin, query, audio, audio, own, sibling, third)


def weight_rows(pieces):
    return jnp.concatenate([piece(h) for h in range(LOCAL) for piece in pieces], axis=0)


def project_cross_kernel(place, own, sibling, w_ref, *outs):
    towers = [lax.rem(place[1] + step, TOWERS) for step in range(TOWERS)]
    pairs = [(step, ref) for step in range(TOWERS) for ref in (own, sibling)]
    for kind, (first, count) in enumerate(((0, VBLK), (VBLK, AUDIO_ROWS))):
        w = weight_rows([functools.partial(lambda b, h: w_ref[b, kind, h], b) for b in range(4)])
        a = jnp.concatenate([ref[towers[step], pl.ds(first, count), :] for step, ref in pairs], axis=0)
        y = nn_dot(a, w).astype(jnp.bfloat16)
        for i, (step, ref) in enumerate(pairs):
            at = first + (BOTH if ref is sibling else 0)
            outs[step][pl.ds(at, count), :] = y[i * count : (i + 1) * count]


def project_cross(place, own, sibling, w):
    width = w.shape[-1]
    tile = width // 3
    return pl.pallas_call(
        project_cross_kernel,
        out_shape=[jax.ShapeDtypeStruct((2 * BOTH, width), jnp.bfloat16)] * TOWERS,
        grid_spec=pltpu.PrefetchScalarGridSpec(
            num_scalar_prefetch=1,
            grid=(3,),
            in_specs=[
                full(own.shape),
                full(own.shape),
                pl.BlockSpec(w.shape[:-1] + (tile,), lambda i, place: (0, 0, 0, 0, i)),
            ],
            out_specs=[pl.BlockSpec((2 * BOTH, tile), lambda i, place: (0, i))] * TOWERS,
        ),
        compiler_params=pltpu.CompilerParams(vmem_limit_bytes=60 * MIB),
        cost_estimate=pl.CostEstimate(
            flops=2 * 1280 * GW * width, bytes_accessed=8 * MIB, transcendentals=0
        ),
        name="project_cross",
    )(place, own, sibling, w)


def project_self_kernel(place, own, sibling, w_ref, *refs):
    base_refs, (gain, own_out, sibling_out) = refs[:TOWERS], refs[TOWERS:]
    a = jnp.concatenate(
        [jnp.concatenate([ref[t] for t in range(TOWERS)], axis=1) for ref in (own, sibling)], axis=0
    )
    w = jnp.concatenate(
        [
            weight_rows([functools.partial(lambda b, h: w_ref[b * TOWERS + t, h], b) for b in range(4)])
            for t in range(TOWERS)
        ],
        axis=0,
    )
    acc = nn_dot(a, w)
    base = functools.reduce(jnp.add, [ref[...].astype(jnp.float32) for ref in base_refs])
    for i, out in enumerate((own_out, sibling_out)):
        video = acc[i * VBLK : (i + 1) * VBLK] + base[i * BOTH : i * BOTH + VBLK]
        audio = base[i * BOTH + VBLK : (i + 1) * BOTH]
        out[pl.ds(0, VBLK), :] = (gain[0:1] * video).astype(jnp.bfloat16)
        out[pl.ds(VBLK, AUDIO_ROWS), :] = (gain[1:2] * audio).astype(jnp.bfloat16)


def project_self(place, own, sibling, w, base, gains):
    width = w.shape[-1]
    tile = width // 3
    rows = pl.BlockSpec((BOTH, tile), lambda i, place: (0, i))
    return pl.pallas_call(
        project_self_kernel,
        out_shape=[jax.ShapeDtypeStruct((BOTH, width), jnp.bfloat16)] * 2,
        grid_spec=pltpu.PrefetchScalarGridSpec(
            num_scalar_prefetch=1,
            grid=(3,),
            in_specs=[
                full(own.shape),
                full(own.shape),
                pl.BlockSpec(w.shape[:-1] + (tile,), lambda i, place: (0, 0, 0, i)),
            ]
            + [pl.BlockSpec((2 * BOTH, tile), lambda i, place: (0, i))] * TOWERS
            + [pl.BlockSpec((2, tile), lambda i, place: (0, place[4] * 3 + i))],
            out_specs=[rows] * 2,
        ),
        compiler_params=pltpu.CompilerParams(vmem_limit_bytes=60 * MIB),
        cost_estimate=pl.CostEstimate(
            flops=4 * VBLK * 1536 * width, bytes_accessed=10 * MIB, transcendentals=0
        ),
        name="project_self",
    )(place, own, sibling, w, *base, gains)


def gate_kernel(*refs):
    pass


def gate(value, *after):
    return pl.pallas_call(
        gate_kernel,
        out_shape=jax.ShapeDtypeStruct(value.shape, value.dtype),
        in_specs=[ANY] * (1 + len(after)),
        out_specs=ANY,
        input_output_aliases={0: 0},
        compiler_params=pltpu.CompilerParams(vmem_limit_bytes=60 * MIB),
        name="gate",
    )(value, *after)


def exchange_towers(value):
    return lax.all_to_all(value, "tower", split_axis=0, concat_axis=0, tiled=True)


def shift_tower(value, step):
    return lax.ppermute(value, "tower", [(i, (i + step) % TOWERS) for i in range(TOWERS)])


def hop(value):
    total = 2 * CHIPS
    return lax.ppermute(value, "ctx", [(i, (i + 2 - 4 * (i % 2)) % total) for i in range(total)])


def swap_core(value):
    return lax.ppermute(value, "ctx", [(i, i ^ 1) for i in range(2 * CHIPS)])


def shards(video_q, video_k, video_v, audio_q, audio_k, audio_v, margin, out_weight, gate_gains):
    ctx = lax.axis_index("ctx")
    tower = lax.axis_index("tower")
    core = lax.rem(ctx, 2)
    place = jnp.stack([ctx, tower, ctx // 4, edge_tower(ctx), core]).astype(jnp.int32)
    gains = gate_gains[0]
    margins = margin[0]

    kv_parts, q_parts, w_self, w_rest = pack_video(
        place, video_k[0], video_v[0], video_q[0], out_weight
    )
    w_rest = lax.all_gather(w_rest, "batch", axis=0, tiled=False)
    w_self = lax.all_gather(w_self, ("batch", "tower"), axis=0, tiled=False)
    own = exchange_towers(kv_parts)
    sibling = swap_core(own)
    near, far = hop(own), hop(sibling)
    third = far

    query = exchange_towers(q_parts).reshape(TOWERS * VBLK, GW)
    audio = exchange_towers(pack_audio(place, audio_q[0], audio_k[0], audio_v[0]))
    state = flash(query, [own, sibling], None, False)
    started = state[2]

    for step in range(1, 4):
        now = [near, far, swap_core(near), swap_core(far)]
        near, far = hop(near), (hop(far) if step < 3 else None)
        state = flash(query, now, state, False)
        if step == 1:
            near = gate(near, started)
            audio = gate(audio, state[2])
        if step == 2:
            crossed = cross(place, margins, query, audio, own, sibling, third)
            parts = project_cross(place, crossed, swap_core(crossed), w_rest)
            base = [parts[0]] + [shift_tower(parts[i], i) for i in (1, 2, 3)]
            near = gate(near, state[2], parts[0])
    video_self = flash(query, [near, swap_core(near)], state, True)
    self_all = exchange_towers(video_self.reshape(TOWERS, VBLK, GW))
    mine, theirs = project_self(place, self_all, swap_core(self_all), w_self, base, gains)
    theirs = swap_core(theirs)
    outs = []
    for first, count in ((0, VBLK), (VBLK, ABLK)):
        a, b = mine[first : first + count], theirs[first : first + count]
        outs.append(
            jnp.where(core == 0, jnp.concatenate([a, b], axis=1), jnp.concatenate([b, a], axis=1))[None]
        )
    return tuple(outs)


def solution(mesh):
    return jax.shard_map(
        shards,
        mesh=mesh,
        in_specs=(
            P("batch", ("ctx", "tower"), None),
            P("batch", ("ctx", "tower"), None),
            P("batch", ("ctx", "tower"), None),
            P("batch", "tower", None),
            P("batch", "tower", None),
            P("batch", "tower", None),
            P("batch", None, None),
            P(None, "tower", "batch", None),
            P("batch", None, None),
        ),
        out_specs=(P("batch", ("ctx", "tower"), None), P("batch", ("ctx", "tower"), None)),
        check_vma=False,
    )
```

```python
import functools

import jax
import jax.numpy as jnp
from jax import lax
from jax.experimental import pallas as pl
from jax.experimental.pallas import tpu as pltpu
from jax.sharding import PartitionSpec as P

H = 12
HD = 128
VBLK = 128
ABLK = 24
TOWERS = 4
CHIPS = 8
LOCAL = H // TOWERS
GW = LOCAL * HD
NEG = -1e30
SCALE2 = HD**-0.5 * 1.4426950408889634
MIB = 1024 * 1024


def nt_dot(a, b):
    return lax.dot_general(a, b, (((1,), (1,)), ((), ())), preferred_element_type=jnp.float32)


def nn_dot(a, b):
    return jnp.dot(a, b, preferred_element_type=jnp.float32)


def full(shape):
    return pl.BlockSpec(shape, lambda *_: (0,) * len(shape))


BRIEF = pl.CostEstimate(flops=1, bytes_accessed=1, transcendentals=0)
ANY = pl.BlockSpec(memory_space=pl.ANY)


def start_copies(pairs, sem, first):
    copies = [pltpu.make_async_copy(a, b, sem.at[first + i]) for i, (a, b) in enumerate(pairs)]
    for copy in copies:
        copy.start()
    return copies


def pack_video_kernel(place, k_ref, v_ref, q_ref, w_ref, out, self_out, rest_out, rows, turned, w_rows, sem):
    half = w_ref.shape[3] // 2
    columns = pl.ds(pl.multiple_of(place[4] * half, 128), half)
    coming = start_copies([(ref, rows.at[i]) for i, ref in enumerate((k_ref, v_ref, q_ref))], sem, 0)
    coming += start_copies([(w_ref.at[:, :, :, columns], w_rows)], sem, 3)
    heads = [(g, h) for g in range(TOWERS) for h in range(LOCAL)]
    going = []
    for i in (1, 2):
        coming[i].wait()
        pairs = [
            (rows.at[i, :, pl.ds((g * LOCAL + h) * HD, HD)], out.at[g, i, h]) for g, h in heads
        ]
        going += start_copies(pairs, sem, 4 + (i - 1) * H)
    coming[0].wait()
    for g, h in heads:
        block = rows[0, :, pl.ds((g * LOCAL + h) * HD, HD)]
        turned[g, h] = block.astype(jnp.float32).T.astype(jnp.bfloat16)
    going += start_copies([(turned.at[g], out.at[g, 0]) for g in range(TOWERS)], sem, 28)
    coming[3].wait()
    going += start_copies([(w_rows.at[0], self_out), (w_rows.at[pl.ds(1, 2)], rest_out)], sem, 32)
    for copy in going:
        copy.wait()


def pack_video(place, k, v, q, w):
    rows = k.shape[0]
    narrow = (LOCAL, w.shape[2], w.shape[3] // 2)
    shapes = [(TOWERS, 3, LOCAL, rows, HD), narrow, (2,) + narrow]
    return pl.pallas_call(
        pack_video_kernel,
        out_shape=[jax.ShapeDtypeStruct(shape, jnp.bfloat16) for shape in shapes],
        grid_spec=pltpu.PrefetchScalarGridSpec(
            num_scalar_prefetch=1,
            grid=(1,),
            in_specs=[ANY] * 4,
            out_specs=[ANY] * 3,
            scratch_shapes=[
                pltpu.VMEM((3,) + k.shape, jnp.bfloat16),
                pltpu.VMEM((TOWERS, LOCAL, HD, rows), jnp.bfloat16),
                pltpu.VMEM((3,) + narrow, jnp.bfloat16),
                pltpu.SemaphoreType.DMA((34,)),
            ],
        ),
        compiler_params=pltpu.CompilerParams(vmem_limit_bytes=60 * MIB),
        name="pack_video",
    )(place, k, v, q, w)


WIN = 192
HALO = 48
QROWS = 96
QAT = 2 * WIN
HAT = QAT + QROWS
AROWS = HAT + 2 * HALO


def main_first(ctx):
    return jnp.clip(lax.rem(ctx, 4) * QROWS - HALO, 0, 384 - WIN)


def edge_tower(ctx):
    return jnp.clip(jnp.where(lax.rem(ctx, 4) == 0, ctx // 4 - 1, ctx // 4 + 1), 0, TOWERS - 1)


def pack_audio_kernel(place, q_ref, k_ref, v_ref, out, rows, sem):
    ctx = place[0]
    phase = lax.rem(ctx, 4)
    main = pl.ds(pl.multiple_of(main_first(ctx), 16), WIN)
    mine = pl.ds(pl.multiple_of(phase * QROWS, 16), QROWS)
    halo = pl.ds(pl.multiple_of(jnp.where(phase == 0, 384 - HALO, 0), 16), HALO)
    coming = start_copies(
        [
            (k_ref.at[main], rows.at[pl.ds(0, WIN)]),
            (v_ref.at[main], rows.at[pl.ds(WIN, WIN)]),
            (q_ref.at[mine], rows.at[pl.ds(QAT, QROWS)]),
            (k_ref.at[halo], rows.at[pl.ds(HAT, HALO)]),
            (v_ref.at[halo], rows.at[pl.ds(HAT + HALO, HALO)]),
        ],
        sem,
        0,
    )
    for copy in coming:
        copy.wait()
    going = start_copies(
        [(rows.at[:, pl.ds(g * GW, GW)], out.at[g]) for g in range(TOWERS)], sem, 5
    )
    for copy in going:
        copy.wait()


def pack_audio(place, q, k, v):
    return pl.pallas_call(
        pack_audio_kernel,
        out_shape=jax.ShapeDtypeStruct((TOWERS, AROWS, GW), jnp.bfloat16),
        grid_spec=pltpu.PrefetchScalarGridSpec(
            num_scalar_prefetch=1,
            grid=(1,),
            in_specs=[ANY] * 3,
            out_specs=ANY,
            scratch_shapes=[
                pltpu.VMEM((AROWS, q.shape[1]), jnp.bfloat16),
                pltpu.SemaphoreType.DMA((9,)),
            ],
        ),
        compiler_params=pltpu.CompilerParams(vmem_limit_bytes=60 * MIB),
        name="pack_audio",
    )(place, q, k, v)


def keys_of(kv_ref):
    return jnp.concatenate([kv_ref[r, 0, 0] for r in range(TOWERS)], axis=1)


def rows_of(kv_ref, which):
    return jnp.concatenate([kv_ref[r, which, 0] for r in range(TOWERS)], axis=0)


def flash_kernel(kv_count, first, last, *refs):
    q_ref = refs[0]
    kv_refs = refs[1 : 1 + kv_count]
    rest = refs[1 + kv_count :]
    if first:
        outs = rest
    else:
        acc_in, stat_in = rest[:2]
        outs = rest[2:]
    size = TOWERS * VBLK
    query = rows_of(q_ref, 0)
    scores = [nn_dot(query, keys_of(kv)) for kv in kv_refs]
    top = functools.reduce(
        jnp.maximum, [jnp.max(s, axis=1, keepdims=True) for s in scores]
    ) * SCALE2
    if not first:
        stat = stat_in[...]
        old_top, old_total = stat[:, 0:1], stat[:, 64:65]
        top = jnp.maximum(top, old_top)
        factor = jnp.exp2(old_top - top)
    total = None
    acc = None
    for s, kv in zip(scores, kv_refs):
        weights = jnp.exp2(s * SCALE2 - top)
        part = jnp.sum(weights, axis=1, keepdims=True)
        total = part if total is None else total + part
        part = nn_dot(weights.astype(jnp.bfloat16), rows_of(kv, 1))
        acc = part if acc is None else acc + part
    if not first:
        total = total + old_total * factor
        acc = acc + acc_in[...] * factor
    if last:
        outs[0][...] = (acc / total).astype(jnp.bfloat16)
    else:
        outs[0][...] = acc
        lane = lax.broadcasted_iota(jnp.int32, (size, HD), 1)
        outs[1][...] = jnp.where(lane < 64, top, total)
        outs[2][...] = total[:8] + jnp.zeros((8, HD), jnp.float32)


QUERY = pl.BlockSpec((TOWERS, 1, 1, VBLK, HD), lambda h, *_: (0, 2, h, 0, 0))
SHARD = pl.BlockSpec((TOWERS, 2, 1, VBLK, HD), lambda h, *_: (0, 0, h, 0, 0))


def flash(query, kvs, state, last):
    rows = TOWERS * VBLK
    keys = rows * len(kvs)
    wide = jax.ShapeDtypeStruct((rows, GW), jnp.float32)
    head = pl.BlockSpec((rows, HD), lambda h: (0, h))
    if last:
        out_shape = jax.ShapeDtypeStruct((rows, GW), jnp.bfloat16)
        out_specs = head
    else:
        out_shape = [wide, wide, jax.ShapeDtypeStruct((8, HD), jnp.float32)]
        out_specs = [head, head, pl.BlockSpec((8, HD), lambda h: (0, 0))]
    return pl.pallas_call(
        functools.partial(flash_kernel, len(kvs), state is None, last),
        out_shape=out_shape,
        grid=(LOCAL,),
        in_specs=[QUERY] + [SHARD] * len(kvs) + ([] if state is None else [head, head]),
        out_specs=out_specs,
        compiler_params=pltpu.CompilerParams(vmem_limit_bytes=60 * MIB),
        cost_estimate=BRIEF,
        name="flash",
    )(query, *kvs, *(() if state is None else state[:2]))


AUDIO_ROWS = 32
BOTH = VBLK + AUDIO_ROWS


def audio_rows(place, margin, audio, own, sibling, third):
    ctx = place[0]
    core = lax.rem(ctx, 2)
    row_block = lax.broadcasted_iota(jnp.int32, (QROWS, 1), 0) // ABLK + ctx * 4
    query = audio[0, pl.ds(QAT, QROWS), :]
    pieces = [(own, r, ctx * 4 + r) for r in range(TOWERS)]
    after = lax.rem(ctx + 1, 16) * 4
    before = lax.rem(ctx + 15, 16) * 4 + 2
    for r in range(2):
        pieces.append((sibling, 2 * core + r, jnp.where(core == 0, after, before) + r))
        pieces.append((third, 2 - 2 * core + r, jnp.where(core == 0, before, after) + r))
    keys = jnp.concatenate([ref[r, 0, 0] for ref, r, _ in pieces], axis=1)
    values = jnp.concatenate([ref[r, 1, 0] for ref, r, _ in pieces], axis=0)
    raw = nn_dot(query, keys) * SCALE2
    scores = []
    for i, (_, _, block) in enumerate(pieces):
        hit = (
            (row_block == margin[block, 0])
            | (row_block == margin[block, 1])
            | (row_block == margin[block, 2])
        )
        scores.append(jnp.where(hit, raw[:, i * VBLK : (i + 1) * VBLK], NEG))
    scores = jnp.concatenate(scores, axis=1)
    weights = jnp.exp2(scores - jnp.max(scores, axis=1, keepdims=True))
    total = jnp.sum(weights, axis=1, keepdims=True)
    return nn_dot(weights.astype(jnp.bfloat16), values) / total


def cross_kernel(place, margin, q_ref, main, edge, own, sibling, third, out):
    ctx = place[0]
    phase = lax.rem(ctx, 4)
    base = (ctx - phase) * 4
    lane = lax.broadcasted_iota(jnp.int32, (1, 256), 1)
    halo_base = jnp.where(phase == 0, base - 2, jnp.where(phase == 3, base + 16, -100))
    main_base = base + lax.div(main_first(ctx), ABLK)
    ids = jnp.where(lane < WIN, lane // ABLK + main_base, lane // ABLK - WIN // ABLK + halo_base)
    ids = jnp.where(lane < WIN + HALO, ids, -100)
    spare = jnp.zeros((256 - WIN - HALO, HD), jnp.bfloat16)
    keys = jnp.concatenate([main[0, pl.ds(0, WIN), :], edge[0, pl.ds(HAT, HALO), :], spare], axis=0)
    values = jnp.concatenate(
        [main[0, pl.ds(WIN, WIN), :], edge[0, pl.ds(HAT + HALO, HALO), :], spare], axis=0
    )
    scores = nt_dot(rows_of(q_ref, 0), keys) * SCALE2
    parts = []
    for r in range(TOWERS):
        block = ctx * 4 + r
        hit = (ids == margin[block, 0]) | (ids == margin[block, 1]) | (ids == margin[block, 2])
        parts.append(jnp.where(hit, scores[r * VBLK : (r + 1) * VBLK], NEG))
    scores = jnp.concatenate(parts, axis=0)
    weights = jnp.exp2(scores - jnp.max(scores, axis=1, keepdims=True))
    total = jnp.sum(weights, axis=1, keepdims=True)
    result = (nn_dot(weights.astype(jnp.bfloat16), values) / total).astype(jnp.bfloat16)
    mixed = audio_rows(place, margin, main, own, sibling, third)
    for r in range(TOWERS):
        out[r, pl.ds(0, VBLK), :] = result[r * VBLK : (r + 1) * VBLK]
        padded = jnp.concatenate(
            [mixed[r * ABLK : (r + 1) * ABLK], jnp.zeros((AUDIO_ROWS - ABLK, HD), jnp.float32)], axis=0
        )
        out[r, pl.ds(VBLK, AUDIO_ROWS), :] = padded.astype(jnp.bfloat16)


def cross(place, margin, query, audio, own, sibling, third):
    rows = TOWERS * VBLK
    return pl.pallas_call(
        cross_kernel,
        out_shape=jax.ShapeDtypeStruct((TOWERS, BOTH, GW), jnp.bfloat16),
        grid_spec=pltpu.PrefetchScalarGridSpec(
            num_scalar_prefetch=2,
            grid=(LOCAL,),
            in_specs=[
                QUERY,
                pl.BlockSpec((1, AROWS, HD), lambda h, place, margin: (place[2], 0, h)),
                pl.BlockSpec((1, AROWS, HD), lambda h, place, margin: (place[3], 0, h)),
                SHARD,
                SHARD,
                SHARD,
            ],
            out_specs=pl.BlockSpec((TOWERS, BOTH, HD), lambda h, *_: (0, 0, h)),
        ),
        compiler_params=pltpu.CompilerParams(vmem_limit_bytes=60 * MIB),
        cost_estimate=BRIEF,
        name="cross",
    )(place, margin, query, audio, audio, own, sibling, third)


def weight_rows(pieces):
    return jnp.concatenate([piece(h) for h in range(LOCAL) for piece in pieces], axis=0)


def project_cross_kernel(place, own, sibling, w_ref, mine, up, down, up_later, down_later):
    towers = [lax.rem(place[1] + step, TOWERS) for step in range(TOWERS)]
    pairs = [(step, ref) for step in range(TOWERS) for ref in (own, sibling)]
    targets = (
        (mine, 0),
        (mine, BOTH),
        (up_later, 0),
        (up, BOTH),
        (up, 0),
        (down, BOTH),
        (down, 0),
        (down_later, 0),
    )
    for kind, (first, count) in enumerate(((0, VBLK), (VBLK, AUDIO_ROWS))):
        w = weight_rows([functools.partial(lambda b, h: w_ref[b, kind, h], b) for b in range(4)])
        a = jnp.concatenate([ref[towers[step], pl.ds(first, count), :] for step, ref in pairs], axis=0)
        y = nn_dot(a, w).astype(jnp.bfloat16)
        for i, (out, at) in enumerate(targets):
            out[pl.ds(at + first, count), :] = y[i * count : (i + 1) * count]


def project_cross(place, own, sibling, w):
    width = w.shape[-1]
    tile = width // 3
    return pl.pallas_call(
        project_cross_kernel,
        out_shape=[jax.ShapeDtypeStruct((n * BOTH, width), jnp.bfloat16) for n in (2, 2, 2, 1, 1)],
        grid_spec=pltpu.PrefetchScalarGridSpec(
            num_scalar_prefetch=1,
            grid=(3,),
            in_specs=[
                full(own.shape),
                full(own.shape),
                pl.BlockSpec(w.shape[:-1] + (tile,), lambda i, place: (0, 0, 0, 0, i)),
            ],
            out_specs=[
                pl.BlockSpec((n * BOTH, tile), lambda i, place: (0, i)) for n in (2, 2, 2, 1, 1)
            ],
        ),
        compiler_params=pltpu.CompilerParams(vmem_limit_bytes=60 * MIB),
        cost_estimate=BRIEF,
        name="project_cross",
    )(place, own, sibling, w)


def project_self_kernel(place, own, sibling, w_ref, *refs):
    mine, up, down, up_later, down_later, gain, own_out, sibling_out = refs
    a = jnp.concatenate(
        [jnp.concatenate([ref[t] for t in range(TOWERS)], axis=1) for ref in (own, sibling)], axis=0
    )
    w = jnp.concatenate(
        [
            weight_rows([functools.partial(lambda b, h: w_ref[b * TOWERS + t, h], b) for b in range(4)])
            for t in range(TOWERS)
        ],
        axis=0,
    )
    acc = nn_dot(a, w)
    top = [mine[pl.ds(0, BOTH), :], down[pl.ds(0, BOTH), :], up_later[...]]
    bottom = [mine[pl.ds(BOTH, BOTH), :], up[pl.ds(BOTH, BOTH), :], down_later[...]]
    base = jnp.concatenate(
        [functools.reduce(jnp.add, [x.astype(jnp.float32) for x in xs]) for xs in (top, bottom)], axis=0
    )
    for i, out in enumerate((own_out, sibling_out)):
        video = acc[i * VBLK : (i + 1) * VBLK] + base[i * BOTH : i * BOTH + VBLK]
        audio = base[i * BOTH + VBLK : (i + 1) * BOTH]
        out[pl.ds(0, VBLK), :] = (gain[0:1] * video).astype(jnp.bfloat16)
        out[pl.ds(VBLK, AUDIO_ROWS), :] = (gain[1:2] * audio).astype(jnp.bfloat16)


def project_self(place, own, sibling, w, base, gains):
    width = w.shape[-1]
    tile = width // 6
    rows = pl.BlockSpec((BOTH, tile), lambda i, place: (0, i))
    return pl.pallas_call(
        project_self_kernel,
        out_shape=[jax.ShapeDtypeStruct((BOTH, width), jnp.bfloat16)] * 2,
        grid_spec=pltpu.PrefetchScalarGridSpec(
            num_scalar_prefetch=1,
            grid=(6,),
            in_specs=[
                full(own.shape),
                full(own.shape),
                pl.BlockSpec(w.shape[:-1] + (tile,), lambda i, place: (0, 0, 0, i)),
            ]
            + [pl.BlockSpec((n * BOTH, tile), lambda i, place: (0, i)) for n in (2, 2, 2, 1, 1)]
            + [pl.BlockSpec((2, tile), lambda i, place: (0, place[4] * 6 + i))],
            out_specs=[rows] * 2,
        ),
        compiler_params=pltpu.CompilerParams(vmem_limit_bytes=60 * MIB),
        cost_estimate=BRIEF,
        name="project_self",
    )(place, own, sibling, w, *base, gains)


def assemble_kernel(place, mine, theirs, video, audio):
    def put(ref):
        video[...] = ref[pl.ds(0, VBLK), :]
        audio[...] = ref[pl.ds(VBLK, AUDIO_ROWS), :].astype(jnp.float32)[:ABLK].astype(jnp.bfloat16)

    @pl.when(pl.program_id(0) == 0)
    def _():
        put(mine)

    @pl.when(pl.program_id(0) == 1)
    def _():
        put(theirs)


def assemble(place, mine, theirs):
    width = mine.shape[1]

    def column(i, place):
        return (0, jnp.where(i == 0, place[4], 1 - place[4]))

    return pl.pallas_call(
        assemble_kernel,
        out_shape=[
            jax.ShapeDtypeStruct((VBLK, 2 * width), jnp.bfloat16),
            jax.ShapeDtypeStruct((ABLK, 2 * width), jnp.bfloat16),
        ],
        grid_spec=pltpu.PrefetchScalarGridSpec(
            num_scalar_prefetch=1,
            grid=(2,),
            in_specs=[full(mine.shape)] * 2,
            out_specs=[pl.BlockSpec((VBLK, width), column), pl.BlockSpec((ABLK, width), column)],
        ),
        compiler_params=pltpu.CompilerParams(vmem_limit_bytes=60 * MIB),
        name="assemble",
    )(place, mine, theirs)


def gate_kernel(*refs):
    pass


def gate(value, *after):
    return pl.pallas_call(
        gate_kernel,
        out_shape=jax.ShapeDtypeStruct(value.shape, value.dtype),
        in_specs=[ANY] * (1 + len(after)),
        out_specs=ANY,
        input_output_aliases={0: 0},
        compiler_params=pltpu.CompilerParams(vmem_limit_bytes=60 * MIB),
        name="gate",
    )(value, *after)


def exchange_towers(value):
    return lax.all_to_all(value, "tower", split_axis=0, concat_axis=0, tiled=True)


def add(a, b):
    return (a.astype(jnp.float32) + b.astype(jnp.float32)).astype(jnp.bfloat16)


def shift_tower(value, step):
    return lax.ppermute(value, "tower", [(i, (i + step) % TOWERS) for i in range(TOWERS)])


def hop(value):
    total = 2 * CHIPS
    return lax.ppermute(value, "ctx", [(i, (i + 2 - 4 * (i % 2)) % total) for i in range(total)])


def swap_core(value):
    return lax.ppermute(value, "ctx", [(i, i ^ 1) for i in range(2 * CHIPS)])


def shards(video_q, video_k, video_v, audio_q, audio_k, audio_v, margin, out_weight, gate_gains):
    ctx = lax.axis_index("ctx")
    tower = lax.axis_index("tower")
    core = lax.rem(ctx, 2)
    place = jnp.stack([ctx, tower, ctx // 4, edge_tower(ctx), core]).astype(jnp.int32)
    gains = gate_gains[0]
    margins = margin[0]

    parts, w_self, w_rest = pack_video(place, video_k[0], video_v[0], video_q[0], out_weight)
    w_rest = lax.all_gather(w_rest, "batch", axis=0, tiled=False)
    w_self = lax.all_gather(w_self, ("batch", "tower"), axis=0, tiled=False)
    query = exchange_towers(parts)
    own = query[:, :2]
    sibling = swap_core(own)
    near, far = hop(own), hop(sibling)
    third = far

    audio = exchange_towers(pack_audio(place, audio_q[0], audio_k[0], audio_v[0]))
    acc, stat, token = flash(query, [own, sibling], None, False)
    audio = gate(audio, token)
    crossed = cross(place, margins, query, audio, own, sibling, third)
    rest, up, down, up_later, down_later = project_cross(place, crossed, swap_core(crossed), w_rest)
    acc = gate(acc, rest)
    up, down = shift_tower(up, 1), shift_tower(down, -1)
    up_later = add(up_later, up[:BOTH])
    down_later = add(down_later, down[BOTH:])

    tokens = [token]
    for step in range(1, 4):
        if step == 3:
            acc = gate(acc, up_later, down_later)
            up_later, down_later = shift_tower(up_later, 1), shift_tower(down_later, -1)
        now = [near, far, swap_core(near), swap_core(far)]
        near, far = hop(near), (hop(far) if step < 3 else None)
        acc, stat, token = flash(query, now, (acc, stat), False)
        tokens.append(token)
        if step < 3:
            near, far = gate(near, tokens[step - 1]), gate(far, tokens[step - 1])
        else:
            near = gate(near, tokens[step - 1], up_later, down_later)
    video_self = flash(query, [near, swap_core(near)], (acc, stat), True)
    base = (rest, up, down, up_later, down_later)

    self_all = exchange_towers(video_self.reshape(TOWERS, VBLK, GW))
    mine, theirs = project_self(place, self_all, swap_core(self_all), w_self, base, gains)
    video_out, audio_out = assemble(place, mine, swap_core(theirs))
    return (video_out[None], audio_out[None])


def solution(mesh):
    return jax.shard_map(
        shards,
        mesh=mesh,
        in_specs=(
            P("batch", ("ctx", "tower"), None),
            P("batch", ("ctx", "tower"), None),
            P("batch", ("ctx", "tower"), None),
            P("batch", "tower", None),
            P("batch", "tower", None),
            P("batch", "tower", None),
            P("batch", None, None),
            P(None, "tower", "batch", None),
            P("batch", None, None),
        ),
        out_specs=(P("batch", ("ctx", "tower"), None), P("batch", ("ctx", "tower"), None)),
        check_vma=False,
    )
```

```python
import functools

import jax
import jax.numpy as jnp
from jax import lax
from jax.experimental import pallas as pl
from jax.experimental.pallas import tpu as pltpu
from jax.sharding import PartitionSpec as P

H = 12
HD = 128
VBLK = 128
ABLK = 24
TOWERS = 4
CHIPS = 8
LOCAL = H // TOWERS
GW = LOCAL * HD
NEG = -1e30
SCALE2 = HD**-0.5 * 1.4426950408889634
MIB = 1024 * 1024


def nt_dot(a, b):
    return lax.dot_general(a, b, (((1,), (1,)), ((), ())), preferred_element_type=jnp.float32)


def nn_dot(a, b):
    return jnp.dot(a, b, preferred_element_type=jnp.float32)


def full(shape):
    return pl.BlockSpec(shape, lambda *_: (0,) * len(shape))


BRIEF = pl.CostEstimate(flops=1, bytes_accessed=1, transcendentals=0)
ANY = pl.BlockSpec(memory_space=pl.ANY)


def start_copies(pairs, sem, first):
    copies = [pltpu.make_async_copy(a, b, sem.at[first + i]) for i, (a, b) in enumerate(pairs)]
    for copy in copies:
        copy.start()
    return copies


def pack_video_kernel(place, k_ref, v_ref, q_ref, w_ref, out, self_out, rest_out, rows, turned, w_rows, sem):
    half = w_ref.shape[3] // 2
    columns = pl.ds(pl.multiple_of(place[4] * half, 128), half)
    coming = start_copies([(ref, rows.at[i]) for i, ref in enumerate((k_ref, v_ref, q_ref))], sem, 0)
    coming += start_copies([(w_ref.at[:, :, :, columns], w_rows)], sem, 3)
    heads = [(g, h) for g in range(TOWERS) for h in range(LOCAL)]
    going = []
    for i in (1, 2):
        coming[i].wait()
        pairs = [
            (rows.at[i, :, pl.ds((g * LOCAL + h) * HD, HD)], out.at[g, i, h]) for g, h in heads
        ]
        going += start_copies(pairs, sem, 4 + (i - 1) * H)
    coming[0].wait()
    for g, h in heads:
        block = rows[0, :, pl.ds((g * LOCAL + h) * HD, HD)]
        turned[g, h] = block.astype(jnp.float32).T.astype(jnp.bfloat16)
    going += start_copies([(turned.at[g], out.at[g, 0]) for g in range(TOWERS)], sem, 28)
    coming[3].wait()
    going += start_copies([(w_rows.at[0], self_out), (w_rows.at[pl.ds(1, 2)], rest_out)], sem, 32)
    for copy in going:
        copy.wait()


def pack_video(place, k, v, q, w):
    rows = k.shape[0]
    narrow = (LOCAL, w.shape[2], w.shape[3] // 2)
    shapes = [(TOWERS, 3, LOCAL, rows, HD), narrow, (2,) + narrow]
    return pl.pallas_call(
        pack_video_kernel,
        out_shape=[jax.ShapeDtypeStruct(shape, jnp.bfloat16) for shape in shapes],
        grid_spec=pltpu.PrefetchScalarGridSpec(
            num_scalar_prefetch=1,
            grid=(1,),
            in_specs=[ANY] * 4,
            out_specs=[ANY] * 3,
            scratch_shapes=[
                pltpu.VMEM((3,) + k.shape, jnp.bfloat16),
                pltpu.VMEM((TOWERS, LOCAL, HD, rows), jnp.bfloat16),
                pltpu.VMEM((3,) + narrow, jnp.bfloat16),
                pltpu.SemaphoreType.DMA((34,)),
            ],
        ),
        compiler_params=pltpu.CompilerParams(vmem_limit_bytes=60 * MIB),
        name="pack_video",
    )(place, k, v, q, w)


WIN = 192
HALO = 48
QROWS = 96
QAT = 2 * WIN
HAT = QAT + QROWS
AROWS = HAT + 2 * HALO


def main_first(ctx):
    return jnp.clip(lax.rem(ctx, 4) * QROWS - HALO, 0, 384 - WIN)


def edge_tower(ctx):
    return jnp.clip(jnp.where(lax.rem(ctx, 4) == 0, ctx // 4 - 1, ctx // 4 + 1), 0, TOWERS - 1)


def pack_audio_kernel(place, q_ref, k_ref, v_ref, out, rows, sem):
    ctx = place[0]
    phase = lax.rem(ctx, 4)
    main = pl.ds(pl.multiple_of(main_first(ctx), 16), WIN)
    mine = pl.ds(pl.multiple_of(phase * QROWS, 16), QROWS)
    halo = pl.ds(pl.multiple_of(jnp.where(phase == 0, 384 - HALO, 0), 16), HALO)
    coming = start_copies(
        [
            (k_ref.at[main], rows.at[pl.ds(0, WIN)]),
            (v_ref.at[main], rows.at[pl.ds(WIN, WIN)]),
            (q_ref.at[mine], rows.at[pl.ds(QAT, QROWS)]),
            (k_ref.at[halo], rows.at[pl.ds(HAT, HALO)]),
            (v_ref.at[halo], rows.at[pl.ds(HAT + HALO, HALO)]),
        ],
        sem,
        0,
    )
    for copy in coming:
        copy.wait()
    going = start_copies(
        [(rows.at[:, pl.ds(g * GW, GW)], out.at[g]) for g in range(TOWERS)], sem, 5
    )
    for copy in going:
        copy.wait()


def pack_audio(place, q, k, v):
    return pl.pallas_call(
        pack_audio_kernel,
        out_shape=jax.ShapeDtypeStruct((TOWERS, AROWS, GW), jnp.bfloat16),
        grid_spec=pltpu.PrefetchScalarGridSpec(
            num_scalar_prefetch=1,
            grid=(1,),
            in_specs=[ANY] * 3,
            out_specs=ANY,
            scratch_shapes=[
                pltpu.VMEM((AROWS, q.shape[1]), jnp.bfloat16),
                pltpu.SemaphoreType.DMA((9,)),
            ],
        ),
        compiler_params=pltpu.CompilerParams(vmem_limit_bytes=60 * MIB),
        name="pack_audio",
    )(place, q, k, v)


def keys_of(kv_ref):
    return jnp.concatenate([kv_ref[r, 0, 0] for r in range(TOWERS)], axis=1)


def rows_of(kv_ref, which):
    return jnp.concatenate([kv_ref[r, which, 0] for r in range(TOWERS)], axis=0)


def lane_tiles(x):
    return [x[:, i : i + HD] for i in range(0, x.shape[1], HD)]


def flash_kernel(kv_count, first, last, *refs):
    q_ref = refs[0]
    kv_refs = refs[1 : 1 + kv_count]
    rest = refs[1 + kv_count :]
    if first:
        outs = rest
    else:
        acc_in, top_in, total_in = rest[:3]
        outs = rest[3:]
    query = rows_of(q_ref, 0)
    scores = [nn_dot(query, keys_of(kv)) for kv in kv_refs]
    top = functools.reduce(jnp.maximum, [t for s in scores for t in lane_tiles(s)])
    top = jnp.max(top, axis=1, keepdims=True) * SCALE2
    if first:
        top = jnp.broadcast_to(top, (TOWERS * VBLK, HD))
        acc = total = None
    else:
        top = jnp.maximum(top, top_in[...])
        factor = jnp.exp2(top_in[...] - top)
        acc = acc_in[...] * factor
        total = total_in[...] * factor
    wide = jnp.concatenate([top] * TOWERS, axis=1)
    for s, kv in zip(scores, kv_refs):
        weights = jnp.exp2(s * SCALE2 - wide)
        part = functools.reduce(jnp.add, lane_tiles(weights))
        total = part if total is None else total + part
        part = nn_dot(weights.astype(jnp.bfloat16), rows_of(kv, 1))
        acc = part if acc is None else acc + part
    if last:
        outs[0][...] = (acc / jnp.sum(total, axis=1, keepdims=True)).astype(jnp.bfloat16)
    else:
        outs[0][...] = acc
        outs[1][...] = top
        outs[2][...] = total
        outs[3][...] = total[:8]


QUERY = pl.BlockSpec((TOWERS, 1, 1, VBLK, HD), lambda h, *_: (0, 2, h, 0, 0))
SHARD = pl.BlockSpec((TOWERS, 2, 1, VBLK, HD), lambda h, *_: (0, 0, h, 0, 0))


def flash(query, kvs, state, last):
    rows = TOWERS * VBLK
    keys = rows * len(kvs)
    wide = jax.ShapeDtypeStruct((rows, GW), jnp.float32)
    head = pl.BlockSpec((rows, HD), lambda h: (0, h))
    if last:
        out_shape = jax.ShapeDtypeStruct((rows, GW), jnp.bfloat16)
        out_specs = head
    else:
        out_shape = [wide, wide, wide, jax.ShapeDtypeStruct((8, HD), jnp.float32)]
        out_specs = [head, head, head, pl.BlockSpec((8, HD), lambda h: (0, 0))]
    return pl.pallas_call(
        functools.partial(flash_kernel, len(kvs), state is None, last),
        out_shape=out_shape,
        grid=(LOCAL,),
        in_specs=[QUERY] + [SHARD] * len(kvs) + ([] if state is None else [head] * 3),
        out_specs=out_specs,
        compiler_params=pltpu.CompilerParams(vmem_limit_bytes=60 * MIB),
        cost_estimate=BRIEF,
        name="flash",
    )(query, *kvs, *(() if state is None else state))


AUDIO_ROWS = 32
BOTH = VBLK + AUDIO_ROWS


def weighted(scores, values):
    weights = jnp.exp2(scores - jnp.max(scores, axis=1, keepdims=True)).astype(jnp.bfloat16)
    result = nn_dot(weights, jnp.concatenate([values, jnp.ones_like(values)], axis=1))
    return result[:, :HD] / result[:, HD:]


def audio_rows(place, margin, audio, own, sibling, third):
    ctx = place[0]
    core = lax.rem(ctx, 2)
    row_block = lax.broadcasted_iota(jnp.int32, (QROWS, 1), 0) // ABLK + ctx * 4
    query = audio[0, pl.ds(QAT, QROWS), :]
    pieces = [(own, r, ctx * 4 + r) for r in range(TOWERS)]
    after = lax.rem(ctx + 1, 16) * 4
    before = lax.rem(ctx + 15, 16) * 4 + 2
    for r in range(2):
        pieces.append((sibling, 2 * core + r, jnp.where(core == 0, after, before) + r))
        pieces.append((third, 2 - 2 * core + r, jnp.where(core == 0, before, after) + r))
    keys = jnp.concatenate([ref[r, 0, 0] for ref, r, _ in pieces], axis=1)
    values = jnp.concatenate([ref[r, 1, 0] for ref, r, _ in pieces], axis=0)
    raw = nn_dot(query, keys) * SCALE2
    scores = []
    for i, (_, _, block) in enumerate(pieces):
        hit = (
            (row_block == margin[block, 0])
            | (row_block == margin[block, 1])
            | (row_block == margin[block, 2])
        )
        scores.append(jnp.where(hit, raw[:, i * VBLK : (i + 1) * VBLK], NEG))
    scores = jnp.concatenate(scores, axis=1)
    return weighted(scores, values)


def cross_kernel(place, margin, q_ref, main, edge, own, sibling, third, out):
    ctx = place[0]
    phase = lax.rem(ctx, 4)
    base = (ctx - phase) * 4
    lane = lax.broadcasted_iota(jnp.int32, (1, 256), 1)
    halo_base = jnp.where(phase == 0, base - 2, jnp.where(phase == 3, base + 16, -100))
    main_base = base + lax.div(main_first(ctx), ABLK)
    ids = jnp.where(lane < WIN, lane // ABLK + main_base, lane // ABLK - WIN // ABLK + halo_base)
    ids = jnp.where(lane < WIN + HALO, ids, -100)
    spare = jnp.zeros((256 - WIN - HALO, HD), jnp.bfloat16)
    keys = jnp.concatenate([main[0, pl.ds(0, WIN), :], edge[0, pl.ds(HAT, HALO), :], spare], axis=0)
    values = jnp.concatenate(
        [main[0, pl.ds(WIN, WIN), :], edge[0, pl.ds(HAT + HALO, HALO), :], spare], axis=0
    )
    scores = nt_dot(rows_of(q_ref, 0), keys) * SCALE2
    parts = []
    for r in range(TOWERS):
        block = ctx * 4 + r
        hit = (ids == margin[block, 0]) | (ids == margin[block, 1]) | (ids == margin[block, 2])
        parts.append(jnp.where(hit, scores[r * VBLK : (r + 1) * VBLK], NEG))
    scores = jnp.concatenate(parts, axis=0)
    result = weighted(scores, values).astype(jnp.bfloat16)
    mixed = audio_rows(place, margin, main, own, sibling, third)
    for r in range(TOWERS):
        out[r, pl.ds(0, VBLK), :] = result[r * VBLK : (r + 1) * VBLK]
        padded = jnp.concatenate(
            [mixed[r * ABLK : (r + 1) * ABLK], jnp.zeros((AUDIO_ROWS - ABLK, HD), jnp.float32)], axis=0
        )
        out[r, pl.ds(VBLK, AUDIO_ROWS), :] = padded.astype(jnp.bfloat16)


def cross(place, margin, query, audio, own, sibling, third):
    rows = TOWERS * VBLK
    return pl.pallas_call(
        cross_kernel,
        out_shape=jax.ShapeDtypeStruct((TOWERS, BOTH, GW), jnp.bfloat16),
        grid_spec=pltpu.PrefetchScalarGridSpec(
            num_scalar_prefetch=2,
            grid=(LOCAL,),
            in_specs=[
                QUERY,
                pl.BlockSpec((1, AROWS, HD), lambda h, place, margin: (place[2], 0, h)),
                pl.BlockSpec((1, AROWS, HD), lambda h, place, margin: (place[3], 0, h)),
                SHARD,
                SHARD,
                SHARD,
            ],
            out_specs=pl.BlockSpec((TOWERS, BOTH, HD), lambda h, *_: (0, 0, h)),
        ),
        compiler_params=pltpu.CompilerParams(vmem_limit_bytes=60 * MIB),
        cost_estimate=BRIEF,
        name="cross",
    )(place, margin, query, audio, audio, own, sibling, third)


def weight_rows(pieces):
    return jnp.concatenate([piece(h) for h in range(LOCAL) for piece in pieces], axis=0)


def project_cross_kernel(place, own, sibling, w_ref, mine, up, down, up_later, down_later):
    towers = [lax.rem(place[1] + step, TOWERS) for step in range(TOWERS)]
    pairs = [(step, ref) for step in range(TOWERS) for ref in (own, sibling)]
    targets = (
        (mine, 0),
        (mine, BOTH),
        (up_later, 0),
        (up, BOTH),
        (up, 0),
        (down, BOTH),
        (down, 0),
        (down_later, 0),
    )
    for kind, (first, count) in enumerate(((0, VBLK), (VBLK, AUDIO_ROWS))):
        w = weight_rows([functools.partial(lambda b, h: w_ref[b, kind, h], b) for b in range(4)])
        a = jnp.concatenate([ref[towers[step], pl.ds(first, count), :] for step, ref in pairs], axis=0)
        y = nn_dot(a, w).astype(jnp.bfloat16)
        for i, (out, at) in enumerate(targets):
            out[pl.ds(at + first, count), :] = y[i * count : (i + 1) * count]


def project_cross(place, own, sibling, w):
    width = w.shape[-1]
    tile = width // 3
    return pl.pallas_call(
        project_cross_kernel,
        out_shape=[jax.ShapeDtypeStruct((n * BOTH, width), jnp.bfloat16) for n in (2, 2, 2, 1, 1)],
        grid_spec=pltpu.PrefetchScalarGridSpec(
            num_scalar_prefetch=1,
            grid=(3,),
            in_specs=[
                full(own.shape),
                full(own.shape),
                pl.BlockSpec(w.shape[:-1] + (tile,), lambda i, place: (0, 0, 0, 0, i)),
            ],
            out_specs=[
                pl.BlockSpec((n * BOTH, tile), lambda i, place: (0, i)) for n in (2, 2, 2, 1, 1)
            ],
        ),
        compiler_params=pltpu.CompilerParams(vmem_limit_bytes=60 * MIB),
        cost_estimate=BRIEF,
        name="project_cross",
    )(place, own, sibling, w)


def project_self_kernel(place, own, sibling, w_ref, *refs):
    mine, up, down, up_later, down_later, gain, video_out, audio_out, sibling_out = refs
    a = jnp.concatenate(
        [jnp.concatenate([ref[t] for t in range(TOWERS)], axis=1) for ref in (own, sibling)], axis=0
    )
    w = jnp.concatenate(
        [
            weight_rows([functools.partial(lambda b, h: w_ref[t * 4 + b, h], b) for b in range(4)])
            for t in range(TOWERS)
        ],
        axis=0,
    )
    acc = nn_dot(a, w)
    top = [mine[pl.ds(0, BOTH), :], down[pl.ds(0, BOTH), :], up_later[...]]
    bottom = [mine[pl.ds(BOTH, BOTH), :], up[pl.ds(BOTH, BOTH), :], down_later[...]]
    base = jnp.concatenate(
        [functools.reduce(jnp.add, [x.astype(jnp.float32) for x in xs]) for xs in (top, bottom)], axis=0
    )
    video, audio = [], []
    for i in range(2):
        video.append(gain[0:1] * (acc[i * VBLK : (i + 1) * VBLK] + base[i * BOTH : i * BOTH + VBLK]))
        audio.append(gain[1:2] * base[i * BOTH + VBLK : (i + 1) * BOTH])
    video_out[...] = video[0].astype(jnp.bfloat16)
    audio_out[...] = audio[0][:ABLK].astype(jnp.bfloat16)
    sibling_out[pl.ds(0, VBLK), :] = video[1].astype(jnp.bfloat16)
    sibling_out[pl.ds(VBLK, AUDIO_ROWS), :] = audio[1].astype(jnp.bfloat16)


def project_self(place, own, sibling, w, base, gains):
    width = w.shape[-1]
    tile = width // 3
    out = lambda rows: pl.BlockSpec((rows, tile), lambda i, place: (0, place[4] * 3 + i))
    return pl.pallas_call(
        project_self_kernel,
        out_shape=[
            jax.ShapeDtypeStruct((VBLK, 2 * width), jnp.bfloat16),
            jax.ShapeDtypeStruct((ABLK, 2 * width), jnp.bfloat16),
            jax.ShapeDtypeStruct((BOTH, width), jnp.bfloat16),
        ],
        grid_spec=pltpu.PrefetchScalarGridSpec(
            num_scalar_prefetch=1,
            grid=(3,),
            in_specs=[
                full(own.shape),
                full(own.shape),
                pl.BlockSpec(w.shape[:-1] + (tile,), lambda i, place: (0, 0, 0, i)),
            ]
            + [pl.BlockSpec((n * BOTH, tile), lambda i, place: (0, i)) for n in (2, 2, 2, 1, 1)]
            + [pl.BlockSpec((2, tile), lambda i, place: (0, place[4] * 3 + i))],
            out_specs=[out(VBLK), out(ABLK), pl.BlockSpec((BOTH, tile), lambda i, place: (0, i))],
        ),
        compiler_params=pltpu.CompilerParams(vmem_limit_bytes=24 * MIB),
        cost_estimate=BRIEF,
        name="project_self",
    )(place, own, sibling, w, *base, gains)


def assemble_kernel(place, video_in, audio_in, theirs, video, audio):
    video[...] = theirs[pl.ds(0, VBLK), :]
    audio[...] = theirs[pl.ds(VBLK, AUDIO_ROWS), :].astype(jnp.float32)[:ABLK].astype(jnp.bfloat16)


def assemble(place, video, audio, theirs):
    width = theirs.shape[1]

    def column(i, place):
        return (0, 1 - place[4])

    return pl.pallas_call(
        assemble_kernel,
        out_shape=[jax.ShapeDtypeStruct(x.shape, x.dtype) for x in (video, audio)],
        grid_spec=pltpu.PrefetchScalarGridSpec(
            num_scalar_prefetch=1,
            grid=(1,),
            in_specs=[ANY, ANY, full(theirs.shape)],
            out_specs=[pl.BlockSpec((VBLK, width), column), pl.BlockSpec((ABLK, width), column)],
        ),
        input_output_aliases={1: 0, 2: 1},
        compiler_params=pltpu.CompilerParams(vmem_limit_bytes=16 * MIB),
        name="assemble",
    )(place, video, audio, theirs)


def gate_kernel(*refs):
    pass


def gate(value, *after):
    return pl.pallas_call(
        gate_kernel,
        out_shape=jax.ShapeDtypeStruct(value.shape, value.dtype),
        in_specs=[ANY] * (1 + len(after)),
        out_specs=ANY,
        input_output_aliases={0: 0},
        compiler_params=pltpu.CompilerParams(vmem_limit_bytes=60 * MIB),
        name="gate",
    )(value, *after)


def exchange_towers(value):
    return lax.all_to_all(value, "tower", split_axis=0, concat_axis=0, tiled=True)


def add(a, b):
    return (a.astype(jnp.float32) + b.astype(jnp.float32)).astype(jnp.bfloat16)


def shift_tower(value, step):
    return lax.ppermute(value, "tower", [(i, (i + step) % TOWERS) for i in range(TOWERS)])


def hop(value):
    total = 2 * CHIPS
    return lax.ppermute(value, "ctx", [(i, (i + 2 - 4 * (i % 2)) % total) for i in range(total)])


def swap_core(value):
    return lax.ppermute(value, "ctx", [(i, i ^ 1) for i in range(2 * CHIPS)])


def shards(video_q, video_k, video_v, audio_q, audio_k, audio_v, margin, out_weight, gate_gains):
    ctx = lax.axis_index("ctx")
    tower = lax.axis_index("tower")
    core = lax.rem(ctx, 2)
    place = jnp.stack([ctx, tower, ctx // 4, edge_tower(ctx), core]).astype(jnp.int32)
    gains = gate_gains[0]
    margins = margin[0]

    parts, w_self, w_rest = pack_video(place, video_k[0], video_v[0], video_q[0], out_weight)
    w_rest = lax.all_gather(w_rest, "batch", axis=0, tiled=False)
    w_self = lax.all_gather(w_self, ("tower", "batch"), axis=0, tiled=False)
    query = exchange_towers(parts)
    own = query[:, :2]
    sibling = swap_core(own)
    near, far = hop(own), hop(sibling)

    audio = exchange_towers(pack_audio(place, audio_q[0], audio_k[0], audio_v[0]))
    acc, top, total, token = flash(query, [own, sibling], None, False)
    near, far = gate(near, token), gate(far, token)
    third = far
    audio = gate(audio, token)
    crossed = cross(place, margins, query, audio, own, sibling, third)
    rest, up, down, up_later, down_later = project_cross(place, crossed, swap_core(crossed), w_rest)
    acc = gate(acc, rest)
    up, down = shift_tower(up, 1), shift_tower(down, -1)
    up_later = add(up_later, up[:BOTH])
    down_later = add(down_later, down[BOTH:])

    tokens = [token]
    for step in range(1, 4):
        now = [near, far, swap_core(near), swap_core(far)]
        near, far = hop(near), (hop(far) if step < 3 else None)
        acc, top, total, token = flash(query, now, (acc, top, total), False)
        tokens.append(token)
        near = gate(near, tokens[step - 1])
        if step < 3:
            far = gate(far, tokens[step - 1])
    acc = gate(acc, up_later, down_later)
    up_later, down_later = shift_tower(up_later, 1), shift_tower(down_later, -1)
    video_self = flash(query, [near, swap_core(near)], (acc, top, total), True)
    base = (rest, up, down, up_later, down_later)

    self_all = exchange_towers(video_self.reshape(TOWERS, VBLK, GW))
    video_out, audio_out, theirs = project_self(place, self_all, swap_core(self_all), w_self, base, gains)
    video_out, audio_out = assemble(place, video_out, audio_out, swap_core(theirs))
    return (video_out[None], audio_out[None])


def solution(mesh):
    return jax.shard_map(
        shards,
        mesh=mesh,
        in_specs=(
            P("batch", ("ctx", "tower"), None),
            P("batch", ("ctx", "tower"), None),
            P("batch", ("ctx", "tower"), None),
            P("batch", "tower", None),
            P("batch", "tower", None),
            P("batch", "tower", None),
            P("batch", None, None),
            P(None, "tower", "batch", None),
            P("batch", None, None),
        ),
        out_specs=(P("batch", ("ctx", "tower"), None), P("batch", ("ctx", "tower"), None)),
        check_vma=False,
    )
```

```python
import functools

import jax
import jax.numpy as jnp
from jax import lax
from jax.experimental import pallas as pl
from jax.experimental.pallas import tpu as pltpu
from jax.sharding import PartitionSpec as P

H = 12
HD = 128
VBLK = 128
ABLK = 24
TOWERS = 4
CHIPS = 8
LOCAL = H // TOWERS
GW = LOCAL * HD
NEG = -1e30
SCALE2 = HD**-0.5 * 1.4426950408889634
MIB = 1024 * 1024


def nt_dot(a, b):
    return lax.dot_general(a, b, (((1,), (1,)), ((), ())), preferred_element_type=jnp.float32)


def nn_dot(a, b):
    return jnp.dot(a, b, preferred_element_type=jnp.float32)


def full(shape):
    return pl.BlockSpec(shape, lambda *_: (0,) * len(shape))


BRIEF = pl.CostEstimate(flops=1, bytes_accessed=1, transcendentals=0)
ANY = pl.BlockSpec(memory_space=pl.ANY)


def start_copies(pairs, sem, first):
    copies = [pltpu.make_async_copy(a, b, sem.at[first + i]) for i, (a, b) in enumerate(pairs)]
    for copy in copies:
        copy.start()
    return copies


def pack_video_kernel(place, k_ref, v_ref, q_ref, w_ref, out, self_out, rest_out, rows, turned, w_rows, sem):
    half = w_ref.shape[3] // 2
    columns = pl.ds(pl.multiple_of(place[4] * half, 128), half)
    coming = start_copies([(ref, rows.at[i]) for i, ref in enumerate((k_ref, v_ref, q_ref))], sem, 0)
    coming += start_copies([(w_ref.at[:, :, :, columns], w_rows)], sem, 3)
    heads = [(g, h) for g in range(TOWERS) for h in range(LOCAL)]
    going = []
    for i in (1, 2):
        coming[i].wait()
        pairs = [
            (rows.at[i, :, pl.ds((g * LOCAL + h) * HD, HD)], out.at[g, i, h]) for g, h in heads
        ]
        going += start_copies(pairs, sem, 4 + (i - 1) * H)
    coming[0].wait()
    for g, h in heads:
        block = rows[0, :, pl.ds((g * LOCAL + h) * HD, HD)]
        turned[g, h] = block.astype(jnp.float32).T.astype(jnp.bfloat16)
    going += start_copies([(turned.at[g], out.at[g, 0]) for g in range(TOWERS)], sem, 28)
    coming[3].wait()
    going += start_copies([(w_rows.at[0], self_out), (w_rows.at[pl.ds(1, 2)], rest_out)], sem, 32)
    for copy in going:
        copy.wait()


def pack_video(place, k, v, q, w):
    rows = k.shape[0]
    narrow = (LOCAL, w.shape[2], w.shape[3] // 2)
    shapes = [(TOWERS, 3, LOCAL, rows, HD), narrow, (2,) + narrow]
    return pl.pallas_call(
        pack_video_kernel,
        out_shape=[jax.ShapeDtypeStruct(shape, jnp.bfloat16) for shape in shapes],
        grid_spec=pltpu.PrefetchScalarGridSpec(
            num_scalar_prefetch=1,
            grid=(1,),
            in_specs=[ANY] * 4,
            out_specs=[ANY] * 3,
            scratch_shapes=[
                pltpu.VMEM((3,) + k.shape, jnp.bfloat16),
                pltpu.VMEM((TOWERS, LOCAL, HD, rows), jnp.bfloat16),
                pltpu.VMEM((3,) + narrow, jnp.bfloat16),
                pltpu.SemaphoreType.DMA((34,)),
            ],
        ),
        compiler_params=pltpu.CompilerParams(vmem_limit_bytes=60 * MIB),
        name="pack_video",
    )(place, k, v, q, w)


WIN = 192
HALO = 48
QROWS = 96
QAT = 2 * WIN
HAT = QAT + QROWS
AROWS = HAT + 2 * HALO


def main_first(ctx):
    return jnp.clip(lax.rem(ctx, 4) * QROWS - HALO, 0, 384 - WIN)


def edge_tower(ctx):
    return jnp.clip(jnp.where(lax.rem(ctx, 4) == 0, ctx // 4 - 1, ctx // 4 + 1), 0, TOWERS - 1)


def pack_audio_kernel(place, q_ref, k_ref, v_ref, out, rows, sem):
    ctx = place[0]
    phase = lax.rem(ctx, 4)
    main = pl.ds(pl.multiple_of(main_first(ctx), 16), WIN)
    mine = pl.ds(pl.multiple_of(phase * QROWS, 16), QROWS)
    halo = pl.ds(pl.multiple_of(jnp.where(phase == 0, 384 - HALO, 0), 16), HALO)
    coming = start_copies(
        [
            (k_ref.at[main], rows.at[pl.ds(0, WIN)]),
            (v_ref.at[main], rows.at[pl.ds(WIN, WIN)]),
            (q_ref.at[mine], rows.at[pl.ds(QAT, QROWS)]),
            (k_ref.at[halo], rows.at[pl.ds(HAT, HALO)]),
            (v_ref.at[halo], rows.at[pl.ds(HAT + HALO, HALO)]),
        ],
        sem,
        0,
    )
    for copy in coming:
        copy.wait()
    going = start_copies(
        [(rows.at[:, pl.ds(g * GW, GW)], out.at[g]) for g in range(TOWERS)], sem, 5
    )
    for copy in going:
        copy.wait()


def pack_audio(place, q, k, v):
    return pl.pallas_call(
        pack_audio_kernel,
        out_shape=jax.ShapeDtypeStruct((TOWERS, AROWS, GW), jnp.bfloat16),
        grid_spec=pltpu.PrefetchScalarGridSpec(
            num_scalar_prefetch=1,
            grid=(1,),
            in_specs=[ANY] * 3,
            out_specs=ANY,
            scratch_shapes=[
                pltpu.VMEM((AROWS, q.shape[1]), jnp.bfloat16),
                pltpu.SemaphoreType.DMA((9,)),
            ],
        ),
        compiler_params=pltpu.CompilerParams(vmem_limit_bytes=60 * MIB),
        name="pack_audio",
    )(place, q, k, v)


def keys_of(kv_ref):
    return jnp.concatenate([kv_ref[r, 0, 0] for r in range(TOWERS)], axis=1)


def rows_of(kv_ref, which):
    return jnp.concatenate([kv_ref[r, which, 0] for r in range(TOWERS)], axis=0)


def lane_tiles(x):
    return [x[:, i : i + HD] for i in range(0, x.shape[1], HD)]


def flash_kernel(kv_count, first, last, *refs):
    q_ref = refs[0]
    kv_refs = refs[1 : 1 + kv_count]
    rest = refs[1 + kv_count :]
    if first:
        outs = rest
    else:
        acc_in, top_in, total_in = rest[:3]
        outs = rest[3:]
    size = 2 * VBLK
    tiles = [slice(i * size, (i + 1) * size) for i in range(2)]
    query = rows_of(q_ref, 0)
    keys = [keys_of(kv) for kv in kv_refs]
    all_scores = [[nn_dot(query[rows], k) for k in keys] for rows in tiles]
    for rows, scores in zip(tiles, all_scores):
        top = functools.reduce(jnp.maximum, [t for s in scores for t in lane_tiles(s)])
        top = jnp.max(top, axis=1, keepdims=True) * SCALE2
        if first:
            top = jnp.broadcast_to(top, (size, HD))
            acc = total = None
        else:
            top = jnp.maximum(top, top_in[rows])
            factor = jnp.exp2(top_in[rows] - top)
            acc = acc_in[rows] * factor
            total = total_in[rows] * factor
        wide = jnp.concatenate([top] * TOWERS, axis=1)
        for s, kv in zip(scores, kv_refs):
            weights = jnp.exp2(s * SCALE2 - wide)
            part = functools.reduce(jnp.add, lane_tiles(weights))
            total = part if total is None else total + part
            part = nn_dot(weights.astype(jnp.bfloat16), rows_of(kv, 1))
            acc = part if acc is None else acc + part
        if last:
            outs[0][rows] = (acc / jnp.sum(total, axis=1, keepdims=True)).astype(jnp.bfloat16)
        else:
            outs[0][rows] = acc
            outs[1][rows] = top
            outs[2][rows] = total
            outs[3][...] = total[:8]


QUERY = pl.BlockSpec((TOWERS, 1, 1, VBLK, HD), lambda h, *_: (0, 2, h, 0, 0))
SHARD = pl.BlockSpec((TOWERS, 2, 1, VBLK, HD), lambda h, *_: (0, 0, h, 0, 0))


def flash(query, kvs, state, last):
    rows = TOWERS * VBLK
    keys = rows * len(kvs)
    wide = jax.ShapeDtypeStruct((rows, GW), jnp.float32)
    head = pl.BlockSpec((rows, HD), lambda h: (0, h))
    if last:
        out_shape = jax.ShapeDtypeStruct((rows, GW), jnp.bfloat16)
        out_specs = head
    else:
        out_shape = [wide, wide, wide, jax.ShapeDtypeStruct((8, HD), jnp.float32)]
        out_specs = [head, head, head, pl.BlockSpec((8, HD), lambda h: (0, 0))]
    return pl.pallas_call(
        functools.partial(flash_kernel, len(kvs), state is None, last),
        out_shape=out_shape,
        grid=(LOCAL,),
        in_specs=[QUERY] + [SHARD] * len(kvs) + ([] if state is None else [head] * 3),
        out_specs=out_specs,
        compiler_params=pltpu.CompilerParams(vmem_limit_bytes=60 * MIB),
        cost_estimate=BRIEF,
        name="flash",
    )(query, *kvs, *(() if state is None else state))


AUDIO_ROWS = 32
BOTH = VBLK + AUDIO_ROWS


def weighted(scores, values):
    weights = jnp.exp2(scores - jnp.max(scores, axis=1, keepdims=True)).astype(jnp.bfloat16)
    result = nn_dot(weights, jnp.concatenate([values, jnp.ones_like(values)], axis=1))
    return result[:, :HD] / result[:, HD:]


def audio_rows(place, margin, audio, own, sibling, third):
    ctx = place[0]
    core = lax.rem(ctx, 2)
    row_block = lax.broadcasted_iota(jnp.int32, (QROWS, 1), 0) // ABLK + ctx * 4
    query = audio[0, pl.ds(QAT, QROWS), :]
    pieces = [(own, r, ctx * 4 + r) for r in range(TOWERS)]
    after = lax.rem(ctx + 1, 16) * 4
    before = lax.rem(ctx + 15, 16) * 4 + 2
    for r in range(2):
        pieces.append((sibling, 2 * core + r, jnp.where(core == 0, after, before) + r))
        pieces.append((third, 2 - 2 * core + r, jnp.where(core == 0, before, after) + r))
    keys = jnp.concatenate([ref[r, 0, 0] for ref, r, _ in pieces], axis=1)
    values = jnp.concatenate([ref[r, 1, 0] for ref, r, _ in pieces], axis=0)
    raw = nn_dot(query, keys) * SCALE2
    scores = []
    for i, (_, _, block) in enumerate(pieces):
        hit = (
            (row_block == margin[block, 0])
            | (row_block == margin[block, 1])
            | (row_block == margin[block, 2])
        )
        scores.append(jnp.where(hit, raw[:, i * VBLK : (i + 1) * VBLK], NEG))
    scores = jnp.concatenate(scores, axis=1)
    return weighted(scores, values)


def cross_kernel(place, margin, q_ref, main, edge, own, sibling, third, out):
    ctx = place[0]
    phase = lax.rem(ctx, 4)
    base = (ctx - phase) * 4
    lane = lax.broadcasted_iota(jnp.int32, (1, 256), 1)
    halo_base = jnp.where(phase == 0, base - 2, jnp.where(phase == 3, base + 16, -100))
    main_base = base + lax.div(main_first(ctx), ABLK)
    ids = jnp.where(lane < WIN, lane // ABLK + main_base, lane // ABLK - WIN // ABLK + halo_base)
    ids = jnp.where(lane < WIN + HALO, ids, -100)
    spare = jnp.zeros((256 - WIN - HALO, HD), jnp.bfloat16)
    keys = jnp.concatenate([main[0, pl.ds(0, WIN), :], edge[0, pl.ds(HAT, HALO), :], spare], axis=0)
    values = jnp.concatenate(
        [main[0, pl.ds(WIN, WIN), :], edge[0, pl.ds(HAT + HALO, HALO), :], spare], axis=0
    )
    scores = nt_dot(rows_of(q_ref, 0), keys) * SCALE2
    parts = []
    for r in range(TOWERS):
        block = ctx * 4 + r
        hit = (ids == margin[block, 0]) | (ids == margin[block, 1]) | (ids == margin[block, 2])
        parts.append(jnp.where(hit, scores[r * VBLK : (r + 1) * VBLK], NEG))
    scores = jnp.concatenate(parts, axis=0)
    result = weighted(scores, values).astype(jnp.bfloat16)
    mixed = audio_rows(place, margin, main, own, sibling, third)
    for r in range(TOWERS):
        out[r, pl.ds(0, VBLK), :] = result[r * VBLK : (r + 1) * VBLK]
        padded = jnp.concatenate(
            [mixed[r * ABLK : (r + 1) * ABLK], jnp.zeros((AUDIO_ROWS - ABLK, HD), jnp.float32)], axis=0
        )
        out[r, pl.ds(VBLK, AUDIO_ROWS), :] = padded.astype(jnp.bfloat16)


def cross(place, margin, query, audio, own, sibling, third):
    rows = TOWERS * VBLK
    return pl.pallas_call(
        cross_kernel,
        out_shape=jax.ShapeDtypeStruct((TOWERS, BOTH, GW), jnp.bfloat16),
        grid_spec=pltpu.PrefetchScalarGridSpec(
            num_scalar_prefetch=2,
            grid=(LOCAL,),
            in_specs=[
                QUERY,
                pl.BlockSpec((1, AROWS, HD), lambda h, place, margin: (place[2], 0, h)),
                pl.BlockSpec((1, AROWS, HD), lambda h, place, margin: (place[3], 0, h)),
                SHARD,
                SHARD,
                SHARD,
            ],
            out_specs=pl.BlockSpec((TOWERS, BOTH, HD), lambda h, *_: (0, 0, h)),
        ),
        compiler_params=pltpu.CompilerParams(vmem_limit_bytes=60 * MIB),
        cost_estimate=BRIEF,
        name="cross",
    )(place, margin, query, audio, audio, own, sibling, third)


def weight_rows(pieces):
    return jnp.concatenate([piece(h) for h in range(LOCAL) for piece in pieces], axis=0)


def project_cross_kernel(place, own, sibling, w_ref, mine, up, down, up_later, down_later):
    towers = [lax.rem(place[1] + step, TOWERS) for step in range(TOWERS)]
    pairs = [(step, ref) for step in range(TOWERS) for ref in (own, sibling)]
    targets = (
        (mine, 0),
        (mine, BOTH),
        (up_later, 0),
        (up, BOTH),
        (up, 0),
        (down, BOTH),
        (down, 0),
        (down_later, 0),
    )
    for kind, (first, count) in enumerate(((0, VBLK), (VBLK, AUDIO_ROWS))):
        w = weight_rows([functools.partial(lambda b, h: w_ref[b, kind, h], b) for b in range(4)])
        a = jnp.concatenate([ref[towers[step], pl.ds(first, count), :] for step, ref in pairs], axis=0)
        y = nn_dot(a, w).astype(jnp.bfloat16)
        for i, (out, at) in enumerate(targets):
            out[pl.ds(at + first, count), :] = y[i * count : (i + 1) * count]


def project_cross(place, own, sibling, w):
    width = w.shape[-1]
    tile = width // 3
    return pl.pallas_call(
        project_cross_kernel,
        out_shape=[jax.ShapeDtypeStruct((n * BOTH, width), jnp.bfloat16) for n in (2, 2, 2, 1, 1)],
        grid_spec=pltpu.PrefetchScalarGridSpec(
            num_scalar_prefetch=1,
            grid=(3,),
            in_specs=[
                full(own.shape),
                full(own.shape),
                pl.BlockSpec(w.shape[:-1] + (tile,), lambda i, place: (0, 0, 0, 0, i)),
            ],
            out_specs=[
                pl.BlockSpec((n * BOTH, tile), lambda i, place: (0, i)) for n in (2, 2, 2, 1, 1)
            ],
        ),
        compiler_params=pltpu.CompilerParams(vmem_limit_bytes=60 * MIB),
        cost_estimate=BRIEF,
        name="project_cross",
    )(place, own, sibling, w)


def project_self_kernel(place, own, sibling, w_ref, *refs):
    mine, up, down, up_later, down_later, gain, video_out, audio_out, sibling_out = refs
    a = jnp.concatenate(
        [jnp.concatenate([ref[t] for t in range(TOWERS)], axis=1) for ref in (own, sibling)], axis=0
    )
    w = jnp.concatenate(
        [
            weight_rows([functools.partial(lambda b, h: w_ref[b * TOWERS + t, h], b) for b in range(4)])
            for t in range(TOWERS)
        ],
        axis=0,
    )
    acc = nn_dot(a, w)
    top = [mine[pl.ds(0, BOTH), :], down[pl.ds(0, BOTH), :], up_later[...]]
    bottom = [mine[pl.ds(BOTH, BOTH), :], up[pl.ds(BOTH, BOTH), :], down_later[...]]
    base = jnp.concatenate(
        [functools.reduce(jnp.add, [x.astype(jnp.float32) for x in xs]) for xs in (top, bottom)], axis=0
    )
    video, audio = [], []
    for i in range(2):
        video.append(gain[0:1] * (acc[i * VBLK : (i + 1) * VBLK] + base[i * BOTH : i * BOTH + VBLK]))
        audio.append(gain[1:2] * base[i * BOTH + VBLK : (i + 1) * BOTH])
    video_out[...] = video[0].astype(jnp.bfloat16)
    audio_out[...] = audio[0][:ABLK].astype(jnp.bfloat16)
    sibling_out[pl.ds(0, VBLK), :] = video[1].astype(jnp.bfloat16)
    sibling_out[pl.ds(VBLK, AUDIO_ROWS), :] = audio[1].astype(jnp.bfloat16)


def project_self(place, own, sibling, w, base, gains):
    width = w.shape[-1]
    tile = width // 3
    out = lambda rows: pl.BlockSpec((rows, tile), lambda i, place: (0, place[4] * 3 + i))
    return pl.pallas_call(
        project_self_kernel,
        out_shape=[
            jax.ShapeDtypeStruct((VBLK, 2 * width), jnp.bfloat16),
            jax.ShapeDtypeStruct((ABLK, 2 * width), jnp.bfloat16),
            jax.ShapeDtypeStruct((BOTH, width), jnp.bfloat16),
        ],
        grid_spec=pltpu.PrefetchScalarGridSpec(
            num_scalar_prefetch=1,
            grid=(3,),
            in_specs=[
                full(own.shape),
                full(own.shape),
                pl.BlockSpec(w.shape[:-1] + (tile,), lambda i, place: (0, 0, 0, i)),
            ]
            + [pl.BlockSpec((n * BOTH, tile), lambda i, place: (0, i)) for n in (2, 2, 2, 1, 1)]
            + [pl.BlockSpec((2, tile), lambda i, place: (0, place[4] * 3 + i))],
            out_specs=[out(VBLK), out(ABLK), pl.BlockSpec((BOTH, tile), lambda i, place: (0, i))],
        ),
        compiler_params=pltpu.CompilerParams(vmem_limit_bytes=24 * MIB),
        cost_estimate=BRIEF,
        name="project_self",
    )(place, own, sibling, w, *base, gains)


def assemble_kernel(place, video_in, audio_in, theirs, video, audio):
    video[...] = theirs[pl.ds(0, VBLK), :]
    audio[...] = theirs[pl.ds(VBLK, AUDIO_ROWS), :].astype(jnp.float32)[:ABLK].astype(jnp.bfloat16)


def assemble(place, video, audio, theirs):
    width = theirs.shape[1]

    def column(i, place):
        return (0, 1 - place[4])

    return pl.pallas_call(
        assemble_kernel,
        out_shape=[jax.ShapeDtypeStruct(x.shape, x.dtype) for x in (video, audio)],
        grid_spec=pltpu.PrefetchScalarGridSpec(
            num_scalar_prefetch=1,
            grid=(1,),
            in_specs=[ANY, ANY, full(theirs.shape)],
            out_specs=[pl.BlockSpec((VBLK, width), column), pl.BlockSpec((ABLK, width), column)],
        ),
        input_output_aliases={1: 0, 2: 1},
        compiler_params=pltpu.CompilerParams(vmem_limit_bytes=16 * MIB),
        name="assemble",
    )(place, video, audio, theirs)


def gate_kernel(*refs):
    pass


def gate(value, *after):
    return pl.pallas_call(
        gate_kernel,
        out_shape=jax.ShapeDtypeStruct(value.shape, value.dtype),
        in_specs=[ANY] * (1 + len(after)),
        out_specs=ANY,
        input_output_aliases={0: 0},
        compiler_params=pltpu.CompilerParams(vmem_limit_bytes=60 * MIB),
        name="gate",
    )(value, *after)


def exchange_towers(value):
    return lax.all_to_all(value, "tower", split_axis=0, concat_axis=0, tiled=True)


def add(a, b):
    return (a.astype(jnp.float32) + b.astype(jnp.float32)).astype(jnp.bfloat16)


def shift_tower(value, step):
    return lax.ppermute(value, "tower", [(i, (i + step) % TOWERS) for i in range(TOWERS)])


def hop(value):
    total = 2 * CHIPS
    return lax.ppermute(value, "ctx", [(i, (i + 2 - 4 * (i % 2)) % total) for i in range(total)])


def swap_core(value):
    return lax.ppermute(value, "ctx", [(i, i ^ 1) for i in range(2 * CHIPS)])


def shards(video_q, video_k, video_v, audio_q, audio_k, audio_v, margin, out_weight, gate_gains):
    ctx = lax.axis_index("ctx")
    tower = lax.axis_index("tower")
    core = lax.rem(ctx, 2)
    place = jnp.stack([ctx, tower, ctx // 4, edge_tower(ctx), core]).astype(jnp.int32)
    gains = gate_gains[0]
    margins = margin[0]

    parts, w_self, w_rest = pack_video(place, video_k[0], video_v[0], video_q[0], out_weight)
    w_rest = lax.all_gather(w_rest, "batch", axis=0, tiled=False)
    w_self = lax.all_gather(w_self, "tower", axis=0, tiled=False)
    query = exchange_towers(parts)
    own = query[:, :2]
    sibling = swap_core(own)
    near, far = hop(own), hop(sibling)

    audio = exchange_towers(pack_audio(place, audio_q[0], audio_k[0], audio_v[0]))
    acc, top, total, token = flash(query, [own, sibling], None, False)
    near, far = gate(near, token), gate(far, token)
    third = far
    tokens = [token]
    for step in range(1, 4):
        now = [near, far, swap_core(near), swap_core(far)]
        near, far = hop(near), (hop(far) if step < 3 else None)
        acc, top, total, token = flash(query, now, (acc, top, total), False)
        tokens.append(token)
        if step == 1:
            crossed = cross(place, margins, query, gate(audio, token), own, sibling, third)
            rest, up, down, up_later, down_later = project_cross(
                place, crossed, swap_core(crossed), w_rest
            )
            acc = gate(acc, rest)
            w_self = lax.all_gather(gate(w_self, token), "batch", axis=0, tiled=False)
            w_self = w_self.reshape((16,) + w_self.shape[2:])
            up, down = shift_tower(up, 1), shift_tower(down, -1)
            up_later = add(up_later, up[:BOTH])
            down_later = add(down_later, down[BOTH:])
        near = gate(near, tokens[step - 1])
        if step < 3:
            far = gate(far, tokens[step - 1])
    acc = gate(acc, up_later, down_later)
    up_later, down_later = shift_tower(up_later, 1), shift_tower(down_later, -1)
    video_self = flash(query, [near, swap_core(near)], (acc, top, total), True)
    base = (rest, up, down, up_later, down_later)

    self_all = exchange_towers(video_self.reshape(TOWERS, VBLK, GW))
    video_out, audio_out, theirs = project_self(place, self_all, swap_core(self_all), w_self, base, gains)
    video_out, audio_out = assemble(place, video_out, audio_out, swap_core(theirs))
    return (video_out[None], audio_out[None])


def solution(mesh):
    return jax.shard_map(
        shards,
        mesh=mesh,
        in_specs=(
            P("batch", ("ctx", "tower"), None),
            P("batch", ("ctx", "tower"), None),
            P("batch", ("ctx", "tower"), None),
            P("batch", "tower", None),
            P("batch", "tower", None),
            P("batch", "tower", None),
            P("batch", None, None),
            P(None, "tower", "batch", None),
            P("batch", None, None),
        ),
        out_specs=(P("batch", ("ctx", "tower"), None), P("batch", ("ctx", "tower"), None)),
        check_vma=False,
    )
```

```python
import functools

import jax
import jax.numpy as jnp
from jax import lax
from jax.experimental import pallas as pl
from jax.experimental.pallas import tpu as pltpu
from jax.sharding import PartitionSpec as P

H = 12
HD = 128
VBLK = 128
ABLK = 24
TOWERS = 4
CHIPS = 8
LOCAL = H // TOWERS
GW = LOCAL * HD
NEG = -1e30
SCALE2 = HD**-0.5 * 1.4426950408889634
MIB = 1024 * 1024


def nt_dot(a, b):
    return lax.dot_general(a, b, (((1,), (1,)), ((), ())), preferred_element_type=jnp.float32)


def nn_dot(a, b):
    return jnp.dot(a, b, preferred_element_type=jnp.float32)


def full(shape):
    return pl.BlockSpec(shape, lambda *_: (0,) * len(shape))


BRIEF = pl.CostEstimate(flops=1, bytes_accessed=1, transcendentals=0)
ANY = pl.BlockSpec(memory_space=pl.ANY)


def start_copies(pairs, sem, first):
    copies = [pltpu.make_async_copy(a, b, sem.at[first + i]) for i, (a, b) in enumerate(pairs)]
    for copy in copies:
        copy.start()
    return copies


WIN = 192
HALO = 48
QROWS = 96
QAT = 2 * WIN
HAT = QAT + QROWS
AROWS = HAT + 2 * HALO


def main_first(ctx):
    return jnp.clip(lax.rem(ctx, 4) * QROWS - HALO, 0, 384 - WIN)


def edge_tower(ctx):
    phase = lax.rem(ctx, 4)
    edge = jnp.where(phase == 0, ctx // 4 - 1, ctx // 4 + 1)
    return jnp.where(((phase == 0) | (phase == 3)) & (edge >= 0) & (edge < TOWERS), edge, -1)


def pack_kernel(
    place, k_ref, v_ref, q_ref, ak_ref, av_ref, aq_ref, w_ref,
    out, self_out, rest_out, main0, main1, main2, main3, halo0, halo1, halo2, halo3,
    rows, turned, audio, w_rows, sem,
):
    ctx, tower = place[0], place[1]
    phase = lax.rem(ctx, 4)
    main = pl.ds(pl.multiple_of(main_first(ctx), 16), WIN)
    mine = pl.ds(pl.multiple_of(phase * QROWS, 16), QROWS)
    halo = pl.ds(pl.multiple_of(jnp.where(phase == 0, 384 - HALO, 0), 16), HALO)
    half = w_ref.shape[3] // 2
    columns = pl.ds(pl.multiple_of(place[4] * half, 128), half)
    coming = start_copies([(ref, rows.at[i]) for i, ref in enumerate((k_ref, v_ref, q_ref))], sem, 0)
    coming_w = start_copies([(w_ref.at[:, :, :, columns], w_rows)], sem, 3)
    coming_audio = start_copies(
        [
            (ak_ref.at[main], audio.at[pl.ds(0, WIN)]),
            (av_ref.at[main], audio.at[pl.ds(WIN, WIN)]),
            (aq_ref.at[mine], audio.at[pl.ds(QAT, QROWS)]),
            (ak_ref.at[halo], audio.at[pl.ds(HAT, HALO)]),
            (av_ref.at[halo], audio.at[pl.ds(HAT + HALO, HALO)]),
        ],
        sem,
        4,
    )
    heads = [(g, h) for g in range(TOWERS) for h in range(LOCAL)]
    going = []
    for i in (1, 2):
        coming[i].wait()
        pairs = [
            (rows.at[i, :, pl.ds((g * LOCAL + h) * HD, HD)], out.at[g, i, h]) for g, h in heads
        ]
        going += start_copies(pairs, sem, 9 + (i - 1) * H)
    coming[0].wait()
    for g, h in heads:
        block = rows[0, :, pl.ds((g * LOCAL + h) * HD, HD)]
        turned[g, h] = block.astype(jnp.float32).T.astype(jnp.bfloat16)
    going += start_copies([(turned.at[g], out.at[g, 0]) for g in range(TOWERS)], sem, 33)
    coming_w[0].wait()
    going += start_copies([(w_rows.at[0], self_out), (w_rows.at[pl.ds(1, 2)], rest_out)], sem, 37)
    for copy in coming_audio:
        copy.wait()
    pairs = []
    for step, (main_out, halo_out) in enumerate(
        ((main0, halo0), (main1, halo1), (main2, halo2), (main3, halo3))
    ):
        group = pl.ds(pl.multiple_of(lax.rem(tower + step, TOWERS) * GW, 128), GW)
        pairs.append((audio.at[pl.ds(0, HAT), group], main_out))
        pairs.append((audio.at[pl.ds(HAT, 2 * HALO), group], halo_out))
    going += start_copies(pairs, sem, 39)
    for copy in going:
        copy.wait()


def pack(place, k, v, q, ak, av, aq, w):
    rows = k.shape[0]
    narrow = (LOCAL, w.shape[2], w.shape[3] // 2)
    shapes = [(TOWERS, 3, LOCAL, rows, HD), narrow, (2,) + narrow]
    shapes += [(HAT, GW)] * TOWERS + [(2 * HALO, GW)] * TOWERS
    return pl.pallas_call(
        pack_kernel,
        out_shape=[jax.ShapeDtypeStruct(shape, jnp.bfloat16) for shape in shapes],
        grid_spec=pltpu.PrefetchScalarGridSpec(
            num_scalar_prefetch=1,
            grid=(1,),
            in_specs=[ANY] * 7,
            out_specs=[ANY] * len(shapes),
            scratch_shapes=[
                pltpu.VMEM((3,) + k.shape, jnp.bfloat16),
                pltpu.VMEM((TOWERS, LOCAL, HD, rows), jnp.bfloat16),
                pltpu.VMEM((AROWS, aq.shape[1]), jnp.bfloat16),
                pltpu.VMEM((3,) + narrow, jnp.bfloat16),
                pltpu.SemaphoreType.DMA((47,)),
            ],
        ),
        compiler_params=pltpu.CompilerParams(vmem_limit_bytes=60 * MIB),
        name="pack",
    )(place, k, v, q, ak, av, aq, w)


def ctx_towers(pairs):
    return [(c * TOWERS + s, c * TOWERS + d) for c, s, d in pairs]


def send_main(value, step):
    pairs = [(c, c // 4, (c // 4 + step) % TOWERS) for c in range(16)]
    return lax.ppermute(value, ("ctx", "tower"), ctx_towers(pairs))


def send_halo(value, step):
    pairs = []
    for c in range(16):
        source = c // 4 - 1 if c % 4 == 0 else c // 4 + 1
        if c % 4 in (0, 3) and 0 <= source < TOWERS:
            pairs.append((c, source, (source + step) % TOWERS))
    return lax.ppermute(value, ("ctx", "tower"), ctx_towers(pairs))


def keys_of(kv_ref):
    return jnp.concatenate([kv_ref[r, 0, 0] for r in range(TOWERS)], axis=1)


def rows_of(kv_ref, which):
    return jnp.concatenate([kv_ref[r, which, 0] for r in range(TOWERS)], axis=0)


def lane_tiles(x):
    return [x[:, i : i + HD] for i in range(0, x.shape[1], HD)]


def flash_kernel(kv_count, first, last, after, *refs):
    q_ref = refs[0]
    kv_refs = refs[1 : 1 + kv_count]
    rest = refs[1 + kv_count :]
    rest = rest[: len(rest) - (1 if last else 4) - after] + rest[len(rest) - (1 if last else 4) :]
    if first:
        outs = rest
    else:
        acc_in, top_in, total_in = rest[:3]
        outs = rest[3:]
    size = 2 * VBLK
    tiles = [slice(i * size, (i + 1) * size) for i in range(2)]
    query = rows_of(q_ref, 0)
    keys = [keys_of(kv) for kv in kv_refs]
    all_scores = [[nn_dot(query[rows], k) for k in keys] for rows in tiles]
    for rows, scores in zip(tiles, all_scores):
        top = functools.reduce(jnp.maximum, [t for s in scores for t in lane_tiles(s)])
        top = jnp.max(top, axis=1, keepdims=True) * SCALE2
        if first:
            top = jnp.broadcast_to(top, (size, HD))
            acc = total = None
        else:
            top = jnp.maximum(top, top_in[rows])
            factor = jnp.exp2(top_in[rows] - top)
            acc = acc_in[rows] * factor
            total = total_in[rows] * factor
        wide = jnp.concatenate([top] * TOWERS, axis=1)
        for s, kv in zip(scores, kv_refs):
            weights = jnp.exp2(s * SCALE2 - wide)
            part = functools.reduce(jnp.add, lane_tiles(weights))
            total = part if total is None else total + part
            part = nn_dot(weights.astype(jnp.bfloat16), rows_of(kv, 1))
            acc = part if acc is None else acc + part
        if last:
            outs[0][rows] = (acc / jnp.sum(total, axis=1, keepdims=True)).astype(jnp.bfloat16)
        else:
            outs[0][rows] = acc
            outs[1][rows] = top
            outs[2][rows] = total
            outs[3][...] = total[:8]


QUERY = pl.BlockSpec((TOWERS, 1, 1, VBLK, HD), lambda h, *_: (0, 2, h, 0, 0))
SHARD = pl.BlockSpec((TOWERS, 2, 1, VBLK, HD), lambda h, *_: (0, 0, h, 0, 0))


def flash(query, kvs, state, last, after=()):
    rows = TOWERS * VBLK
    keys = rows * len(kvs)
    wide = jax.ShapeDtypeStruct((rows, GW), jnp.float32)
    head = pl.BlockSpec((rows, HD), lambda h: (0, h))
    if last:
        out_shape = jax.ShapeDtypeStruct((rows, GW), jnp.bfloat16)
        out_specs = head
    else:
        out_shape = [wide, wide, wide, jax.ShapeDtypeStruct((8, HD), jnp.float32)]
        out_specs = [head, head, head, pl.BlockSpec((8, HD), lambda h: (0, 0))]
    return pl.pallas_call(
        functools.partial(flash_kernel, len(kvs), state is None, last, len(after)),
        out_shape=out_shape,
        grid=(LOCAL,),
        in_specs=[QUERY] + [SHARD] * len(kvs) + ([] if state is None else [head] * 3) + [ANY] * len(after),
        out_specs=out_specs,
        compiler_params=pltpu.CompilerParams(vmem_limit_bytes=60 * MIB),
        cost_estimate=BRIEF,
        name="flash",
    )(query, *kvs, *(() if state is None else state), *after)


AUDIO_ROWS = 32
BOTH = VBLK + AUDIO_ROWS


def weighted(scores, values):
    weights = jnp.exp2(scores - jnp.max(scores, axis=1, keepdims=True)).astype(jnp.bfloat16)
    result = nn_dot(weights, jnp.concatenate([values, jnp.ones_like(values)], axis=1))
    return result[:, :HD] / result[:, HD:]


def audio_rows(place, margin, main, own, sibling, third):
    ctx = place[0]
    core = lax.rem(ctx, 2)
    row_block = lax.broadcasted_iota(jnp.int32, (QROWS, 1), 0) // ABLK + ctx * 4
    query = main[QAT:]
    pieces = [(own, r, ctx * 4 + r) for r in range(TOWERS)]
    after = lax.rem(ctx + 1, 16) * 4
    before = lax.rem(ctx + 15, 16) * 4 + 2
    for r in range(2):
        pieces.append((sibling, 2 * core + r, jnp.where(core == 0, after, before) + r))
        pieces.append((third, 2 - 2 * core + r, jnp.where(core == 0, before, after) + r))
    keys = jnp.concatenate([ref[r, 0, 0] for ref, r, _ in pieces], axis=1)
    values = jnp.concatenate([ref[r, 1, 0] for ref, r, _ in pieces], axis=0)
    raw = nn_dot(query, keys) * SCALE2
    scores = []
    for i, (_, _, block) in enumerate(pieces):
        hit = (
            (row_block == margin[block, 0])
            | (row_block == margin[block, 1])
            | (row_block == margin[block, 2])
        )
        scores.append(jnp.where(hit, raw[:, i * VBLK : (i + 1) * VBLK], NEG))
    scores = jnp.concatenate(scores, axis=1)
    return weighted(scores, values)


def cross_kernel(place, margin, q_ref, *refs):
    mains, halos, (own, sibling, third, out) = refs[:4], refs[4:8], refs[8:]
    main = functools.reduce(
        jnp.add, [ref[...] for ref in mains[1:]], jnp.where(place[1] == place[2], mains[0][...], 0)
    )
    halo = functools.reduce(
        jnp.add, [ref[...] for ref in halos[1:]], jnp.where(place[1] == place[3], halos[0][...], 0)
    )
    ctx = place[0]
    phase = lax.rem(ctx, 4)
    base = (ctx - phase) * 4
    lane = lax.broadcasted_iota(jnp.int32, (1, 256), 1)
    halo_base = jnp.where(phase == 0, base - 2, jnp.where(phase == 3, base + 16, -100))
    main_base = base + lax.div(main_first(ctx), ABLK)
    ids = jnp.where(lane < WIN, lane // ABLK + main_base, lane // ABLK - WIN // ABLK + halo_base)
    ids = jnp.where(lane < WIN + HALO, ids, -100)
    spare = jnp.zeros((256 - WIN - HALO, HD), jnp.bfloat16)
    keys = jnp.concatenate([main[:WIN], halo[:HALO], spare], axis=0)
    values = jnp.concatenate(
        [main[WIN:QAT], halo[HALO:], spare], axis=0
    )
    scores = nt_dot(rows_of(q_ref, 0), keys) * SCALE2
    parts = []
    for r in range(TOWERS):
        block = ctx * 4 + r
        hit = (ids == margin[block, 0]) | (ids == margin[block, 1]) | (ids == margin[block, 2])
        parts.append(jnp.where(hit, scores[r * VBLK : (r + 1) * VBLK], NEG))
    scores = jnp.concatenate(parts, axis=0)
    result = weighted(scores, values).astype(jnp.bfloat16)
    mixed = audio_rows(place, margin, main, own, sibling, third)
    for r in range(TOWERS):
        out[r, pl.ds(0, VBLK), :] = result[r * VBLK : (r + 1) * VBLK]
        padded = jnp.concatenate(
            [mixed[r * ABLK : (r + 1) * ABLK], jnp.zeros((AUDIO_ROWS - ABLK, HD), jnp.float32)], axis=0
        )
        out[r, pl.ds(VBLK, AUDIO_ROWS), :] = padded.astype(jnp.bfloat16)


def cross(place, margin, query, mains, halos, own, sibling, third):
    rows = TOWERS * VBLK
    return pl.pallas_call(
        cross_kernel,
        out_shape=jax.ShapeDtypeStruct((TOWERS, BOTH, GW), jnp.bfloat16),
        grid_spec=pltpu.PrefetchScalarGridSpec(
            num_scalar_prefetch=2,
            grid=(LOCAL,),
            in_specs=[
                QUERY,
            ]
            + [pl.BlockSpec((HAT, HD), lambda h, *_: (0, h))] * TOWERS
            + [pl.BlockSpec((2 * HALO, HD), lambda h, *_: (0, h))] * TOWERS
            + [SHARD] * 3,
            out_specs=pl.BlockSpec((TOWERS, BOTH, HD), lambda h, *_: (0, 0, h)),
        ),
        compiler_params=pltpu.CompilerParams(vmem_limit_bytes=60 * MIB),
        cost_estimate=BRIEF,
        name="cross",
    )(place, margin, query, *mains, *halos, own, sibling, third)


def weight_rows(pieces):
    return jnp.concatenate([piece(h) for h in range(LOCAL) for piece in pieces], axis=0)


def project_cross_kernel(place, own, sibling, w_ref, _, __, mine, up, down, up_later, down_later):
    towers = [lax.rem(place[1] + step, TOWERS) for step in range(TOWERS)]
    targets = (
        (mine, 0),
        (mine, BOTH),
        (up_later, 0),
        (up, BOTH),
        (up, 0),
        (down, BOTH),
        (down, 0),
        (down_later, 0),
    )
    ws = [
        weight_rows([functools.partial(lambda b, h: w_ref[b, kind, h], b) for b in range(4)])
        for kind in range(2)
    ]
    for step in range(TOWERS):
        for w, (first, count) in zip(ws, ((0, VBLK), (VBLK, AUDIO_ROWS))):
            both = [ref[towers[step], pl.ds(first, count), :] for ref in (own, sibling)]
            y = nn_dot(jnp.concatenate(both, axis=0), w).astype(jnp.bfloat16)
            for i in range(2):
                out, at = targets[2 * step + i]
                out[pl.ds(at + first, count), :] = y[i * count : (i + 1) * count]


def project_cross(place, own, sibling, w, after):
    width = w.shape[-1]
    tile = width // 3
    return pl.pallas_call(
        project_cross_kernel,
        out_shape=[jax.ShapeDtypeStruct((n * BOTH, width), jnp.bfloat16) for n in (2, 2, 2, 1, 1)],
        grid_spec=pltpu.PrefetchScalarGridSpec(
            num_scalar_prefetch=1,
            grid=(3,),
            in_specs=[
                full(own.shape),
                full(own.shape),
                pl.BlockSpec(w.shape[:-1] + (tile,), lambda i, place: (0, 0, 0, 0, i)),
                ANY,
                ANY,
            ],
            out_specs=[
                pl.BlockSpec((n * BOTH, tile), lambda i, place: (0, i)) for n in (2, 2, 2, 1, 1)
            ],
        ),
        compiler_params=pltpu.CompilerParams(vmem_limit_bytes=60 * MIB),
        cost_estimate=BRIEF,
        name="project_cross",
    )(place, own, sibling, w, *after)


def project_self_kernel(place, own, sibling, w_ref, *refs):
    mine, up, down, up_later, down_later, gain, video_out, audio_out, sibling_out = refs
    a = jnp.concatenate(
        [jnp.concatenate([ref[t] for t in range(TOWERS)], axis=1) for ref in (own, sibling)], axis=0
    )
    w = jnp.concatenate(
        [
            weight_rows([functools.partial(lambda b, h: w_ref[b * TOWERS + lax.rem(place[1] - t + TOWERS, TOWERS), h], b) for b in range(4)])
            for t in range(TOWERS)
        ],
        axis=0,
    )
    acc = nn_dot(a, w)
    top = [mine[pl.ds(0, BOTH), :], down[pl.ds(0, BOTH), :], up_later[...]]
    bottom = [mine[pl.ds(BOTH, BOTH), :], up[pl.ds(BOTH, BOTH), :], down_later[...]]
    base = jnp.concatenate(
        [functools.reduce(jnp.add, [x.astype(jnp.float32) for x in xs]) for xs in (top, bottom)], axis=0
    )
    video, audio = [], []
    for i in range(2):
        video.append(gain[0:1] * (acc[i * VBLK : (i + 1) * VBLK] + base[i * BOTH : i * BOTH + VBLK]))
        audio.append(gain[1:2] * base[i * BOTH + VBLK : (i + 1) * BOTH])
    video_out[...] = video[0].astype(jnp.bfloat16)
    audio_out[...] = audio[0][:ABLK].astype(jnp.bfloat16)
    sibling_out[pl.ds(0, VBLK), :] = video[1].astype(jnp.bfloat16)
    sibling_out[pl.ds(VBLK, AUDIO_ROWS), :] = audio[1].astype(jnp.bfloat16)


def project_self(place, own, sibling, w, base, gains):
    width = w.shape[-1]
    tile = width // 3
    out = lambda rows: pl.BlockSpec((rows, tile), lambda i, place: (0, place[4] * 3 + i))
    return pl.pallas_call(
        project_self_kernel,
        out_shape=[
            jax.ShapeDtypeStruct((VBLK, 2 * width), jnp.bfloat16),
            jax.ShapeDtypeStruct((ABLK, 2 * width), jnp.bfloat16),
            jax.ShapeDtypeStruct((BOTH, width), jnp.bfloat16),
        ],
        grid_spec=pltpu.PrefetchScalarGridSpec(
            num_scalar_prefetch=1,
            grid=(3,),
            in_specs=[
                full(own.shape),
                full(own.shape),
                pl.BlockSpec(w.shape[:-1] + (tile,), lambda i, place: (0, 0, 0, i)),
            ]
            + [pl.BlockSpec((n * BOTH, tile), lambda i, place: (0, i)) for n in (2, 2, 2, 1, 1)]
            + [pl.BlockSpec((2, tile), lambda i, place: (0, place[4] * 3 + i))],
            out_specs=[out(VBLK), out(ABLK), pl.BlockSpec((BOTH, tile), lambda i, place: (0, i))],
        ),
        compiler_params=pltpu.CompilerParams(vmem_limit_bytes=24 * MIB),
        cost_estimate=BRIEF,
        name="project_self",
    )(place, own, sibling, w, *base, gains)


def assemble_kernel(place, video_in, audio_in, theirs, video, audio):
    video[...] = theirs[pl.ds(0, VBLK), :]
    audio[...] = theirs[pl.ds(VBLK, AUDIO_ROWS), :].astype(jnp.float32)[:ABLK].astype(jnp.bfloat16)


def assemble(place, video, audio, theirs):
    width = theirs.shape[1]

    def column(i, place):
        return (0, 1 - place[4])

    return pl.pallas_call(
        assemble_kernel,
        out_shape=[jax.ShapeDtypeStruct(x.shape, x.dtype) for x in (video, audio)],
        grid_spec=pltpu.PrefetchScalarGridSpec(
            num_scalar_prefetch=1,
            grid=(1,),
            in_specs=[ANY, ANY, full(theirs.shape)],
            out_specs=[pl.BlockSpec((VBLK, width), column), pl.BlockSpec((ABLK, width), column)],
        ),
        input_output_aliases={1: 0, 2: 1},
        compiler_params=pltpu.CompilerParams(vmem_limit_bytes=16 * MIB),
        name="assemble",
    )(place, video, audio, theirs)


def gate_kernel(*refs):
    pass


def gate(value, *after):
    return pl.pallas_call(
        gate_kernel,
        out_shape=jax.ShapeDtypeStruct(value.shape, value.dtype),
        in_specs=[ANY] * (1 + len(after)),
        out_specs=ANY,
        input_output_aliases={0: 0},
        compiler_params=pltpu.CompilerParams(vmem_limit_bytes=60 * MIB),
        name="gate",
    )(value, *after)


def exchange_towers(value):
    return lax.all_to_all(value, "tower", split_axis=0, concat_axis=0, tiled=True)


def add(a, b):
    return (a.astype(jnp.float32) + b.astype(jnp.float32)).astype(jnp.bfloat16)


def shift_tower(value, step):
    return lax.ppermute(value, "tower", [(i, (i + step) % TOWERS) for i in range(TOWERS)])


def hop(value):
    total = 2 * CHIPS
    return lax.ppermute(value, "ctx", [(i, (i + 2 - 4 * (i % 2)) % total) for i in range(total)])


def swap_core(value):
    return lax.ppermute(value, "ctx", [(i, i ^ 1) for i in range(2 * CHIPS)])


def shards(video_q, video_k, video_v, audio_q, audio_k, audio_v, margin, out_weight, gate_gains):
    ctx = lax.axis_index("ctx")
    tower = lax.axis_index("tower")
    core = lax.rem(ctx, 2)
    place = jnp.stack([ctx, tower, ctx // 4, edge_tower(ctx), core]).astype(jnp.int32)
    gains = gate_gains[0]
    margins = margin[0]

    parts, w_self, w_rest, *audio = pack(
        place, video_k[0], video_v[0], video_q[0], audio_k[0], audio_v[0], audio_q[0], out_weight
    )
    w_rest = lax.all_gather(w_rest, "batch", axis=0, tiled=False)
    query = exchange_towers(parts)
    own = query[:, :2]
    sibling = swap_core(own)
    near, far = hop(own), hop(sibling)
    mains = [audio[0]] + [send_main(audio[step], step) for step in (1, 2, 3)]
    halos = [audio[4]] + [send_halo(audio[4 + step], step) for step in (1, 2, 3)]
    w_self = gate(w_self, *mains[1:])
    w_parts = jnp.stack([w_self] + [shift_tower(w_self, step) for step in (1, 2, 3)])
    w_self = lax.all_gather(w_parts, "batch", axis=0, tiled=False)
    w_self = w_self.reshape((16,) + w_self.shape[2:])

    acc, top, total, token = flash(query, [own, sibling], None, False)
    near, far = gate(near, token, *mains[1:], *halos[1:]), gate(far, token)
    crossed = cross(place, margins, query, mains, halos, own, sibling, far)

    tokens = [token]
    after = (crossed,)
    for step in range(1, 4):
        now = [near, far, swap_core(near), swap_core(far)]
        near, far = hop(near), (hop(far) if step < 3 else None)
        acc, top, total, token = flash(query, now, (acc, top, total), False, after)
        tokens.append(token)
        after = ()
        if step == 1:
            rest, up, down, up_later, down_later = project_cross(
                place, crossed, swap_core(crossed), w_rest, (token, w_parts)
            )
            after = (rest,)
            up, down = shift_tower(up, 1), shift_tower(down, -1)
            up_later = add(up_later, up[:BOTH])
            down_later = add(down_later, down[BOTH:])
        near = gate(near, tokens[step - 1])
        if step < 3:
            far = gate(far, tokens[step - 1])
    after = (up_later, down_later)
    up_later, down_later = shift_tower(up_later, 1), shift_tower(down_later, -1)
    video_self = flash(query, [near, swap_core(near)], (acc, top, total), True, after)
    base = (rest, up, down, up_later, down_later)

    self_all = exchange_towers(video_self.reshape(TOWERS, VBLK, GW))
    video_out, audio_out, theirs = project_self(place, self_all, swap_core(self_all), w_self, base, gains)
    video_out, audio_out = assemble(place, video_out, audio_out, swap_core(theirs))
    return (video_out[None], audio_out[None])


def solution(mesh):
    return jax.shard_map(
        shards,
        mesh=mesh,
        in_specs=(
            P("batch", ("ctx", "tower"), None),
            P("batch", ("ctx", "tower"), None),
            P("batch", ("ctx", "tower"), None),
            P("batch", "tower", None),
            P("batch", "tower", None),
            P("batch", "tower", None),
            P("batch", None, None),
            P(None, "tower", "batch", None),
            P("batch", None, None),
        ),
        out_specs=(P("batch", ("ctx", "tower"), None), P("batch", ("ctx", "tower"), None)),
        check_vma=False,
    )
```

```python
import functools

import jax
import jax.numpy as jnp
from jax import lax
from jax.experimental import pallas as pl
from jax.experimental.pallas import tpu as pltpu
from jax.sharding import PartitionSpec as P

H = 12
HD = 128
VBLK = 128
ABLK = 24
TOWERS = 4
CHIPS = 8
LOCAL = H // TOWERS
GW = LOCAL * HD
NEG = -1e30
SCALE2 = HD**-0.5 * 1.4426950408889634
MIB = 1024 * 1024


def nt_dot(a, b):
    return lax.dot_general(a, b, (((1,), (1,)), ((), ())), preferred_element_type=jnp.float32)


def nn_dot(a, b):
    return jnp.dot(a, b, preferred_element_type=jnp.float32)


def full(shape):
    return pl.BlockSpec(shape, lambda *_: (0,) * len(shape))


BRIEF = pl.CostEstimate(flops=1, bytes_accessed=1, transcendentals=0)
ANY = pl.BlockSpec(memory_space=pl.ANY)


def start_copies(pairs, sem, first):
    copies = [pltpu.make_async_copy(a, b, sem.at[first + i]) for i, (a, b) in enumerate(pairs)]
    for copy in copies:
        copy.start()
    return copies


WIN = 192
HALO = 48
QROWS = 96
QAT = 2 * WIN
HAT = QAT + QROWS
AROWS = HAT + 2 * HALO


def main_first(ctx):
    return jnp.clip(lax.rem(ctx, 4) * QROWS - HALO, 0, 384 - WIN)


def edge_tower(ctx):
    phase = lax.rem(ctx, 4)
    edge = jnp.where(phase == 0, ctx // 4 - 1, ctx // 4 + 1)
    return jnp.where(((phase == 0) | (phase == 3)) & (edge >= 0) & (edge < TOWERS), edge, -1)


def pack_kernel(
    place, k_ref, v_ref, q_ref, ak_ref, av_ref, aq_ref, w_ref,
    out, self_out, rest_out, main0, main1, main2, main3, halo0, halo1, halo2, halo3,
    rows, turned, audio, w_rows, sem,
):
    ctx, tower = place[0], place[1]
    phase = lax.rem(ctx, 4)
    main = pl.ds(pl.multiple_of(main_first(ctx), 16), WIN)
    mine = pl.ds(pl.multiple_of(phase * QROWS, 16), QROWS)
    halo = pl.ds(pl.multiple_of(jnp.where(phase == 0, 384 - HALO, 0), 16), HALO)
    half = w_ref.shape[3] // 2
    columns = pl.ds(pl.multiple_of(place[4] * half, 128), half)
    coming = start_copies([(ref, rows.at[i]) for i, ref in enumerate((k_ref, v_ref, q_ref))], sem, 0)
    coming_w = start_copies([(w_ref.at[:, :, :, columns], w_rows)], sem, 3)
    coming_audio = start_copies(
        [
            (ak_ref.at[main], audio.at[pl.ds(0, WIN)]),
            (av_ref.at[main], audio.at[pl.ds(WIN, WIN)]),
            (aq_ref.at[mine], audio.at[pl.ds(QAT, QROWS)]),
            (ak_ref.at[halo], audio.at[pl.ds(HAT, HALO)]),
            (av_ref.at[halo], audio.at[pl.ds(HAT + HALO, HALO)]),
        ],
        sem,
        4,
    )
    heads = [(g, h) for g in range(TOWERS) for h in range(LOCAL)]
    going = []
    for i in (1, 2):
        coming[i].wait()
        pairs = [
            (rows.at[i, :, pl.ds((g * LOCAL + h) * HD, HD)], out.at[g, i, h]) for g, h in heads
        ]
        going += start_copies(pairs, sem, 9 + (i - 1) * H)
    coming[0].wait()
    for g, h in heads:
        block = rows[0, :, pl.ds((g * LOCAL + h) * HD, HD)]
        turned[g, h] = block.astype(jnp.float32).T.astype(jnp.bfloat16)
    going += start_copies([(turned.at[g], out.at[g, 0]) for g in range(TOWERS)], sem, 33)
    coming_w[0].wait()
    going += start_copies([(w_rows.at[0], self_out), (w_rows.at[pl.ds(1, 2)], rest_out)], sem, 37)
    for copy in coming_audio:
        copy.wait()
    pairs = []
    for step, (main_out, halo_out) in enumerate(
        ((main0, halo0), (main1, halo1), (main2, halo2), (main3, halo3))
    ):
        group = pl.ds(pl.multiple_of(lax.rem(tower + step, TOWERS) * GW, 128), GW)
        pairs.append((audio.at[pl.ds(0, HAT), group], main_out))
        pairs.append((audio.at[pl.ds(HAT, 2 * HALO), group], halo_out))
    going += start_copies(pairs, sem, 39)
    for copy in going:
        copy.wait()


def pack(place, k, v, q, ak, av, aq, w):
    rows = k.shape[0]
    narrow = (LOCAL, w.shape[2], w.shape[3] // 2)
    shapes = [(TOWERS, 3, LOCAL, rows, HD), narrow, (2,) + narrow]
    shapes += [(HAT, GW)] * TOWERS + [(2 * HALO, GW)] * TOWERS
    return pl.pallas_call(
        pack_kernel,
        out_shape=[jax.ShapeDtypeStruct(shape, jnp.bfloat16) for shape in shapes],
        grid_spec=pltpu.PrefetchScalarGridSpec(
            num_scalar_prefetch=1,
            grid=(1,),
            in_specs=[ANY] * 7,
            out_specs=[ANY] * len(shapes),
            scratch_shapes=[
                pltpu.VMEM((3,) + k.shape, jnp.bfloat16),
                pltpu.VMEM((TOWERS, LOCAL, HD, rows), jnp.bfloat16),
                pltpu.VMEM((AROWS, aq.shape[1]), jnp.bfloat16),
                pltpu.VMEM((3,) + narrow, jnp.bfloat16),
                pltpu.SemaphoreType.DMA((47,)),
            ],
        ),
        compiler_params=pltpu.CompilerParams(vmem_limit_bytes=60 * MIB),
        name="pack",
    )(place, k, v, q, ak, av, aq, w)


def ctx_towers(pairs):
    return [(c * TOWERS + s, c * TOWERS + d) for c, s, d in pairs]


def send_main(value, step):
    pairs = [(c, c // 4, (c // 4 + step) % TOWERS) for c in range(16)]
    return lax.ppermute(value, ("ctx", "tower"), ctx_towers(pairs))


def send_halo(value, step):
    pairs = []
    for c in range(16):
        source = c // 4 - 1 if c % 4 == 0 else c // 4 + 1
        if c % 4 in (0, 3) and 0 <= source < TOWERS:
            pairs.append((c, source, (source + step) % TOWERS))
    return lax.ppermute(value, ("ctx", "tower"), ctx_towers(pairs))


def keys_of(kv_ref):
    return jnp.concatenate([kv_ref[r, 0, 0] for r in range(TOWERS)], axis=1)


def rows_of(kv_ref, which):
    return jnp.concatenate([kv_ref[r, which, 0] for r in range(TOWERS)], axis=0)


def lane_tiles(x):
    return [x[:, i : i + HD] for i in range(0, x.shape[1], HD)]


def flash_kernel(kv_count, first, last, after, *refs):
    q_ref = refs[0]
    kv_refs = refs[1 : 1 + kv_count]
    rest = refs[1 + kv_count :]
    rest = rest[: len(rest) - (1 if last else 4) - after] + rest[len(rest) - (1 if last else 4) :]
    if first:
        outs = rest
    else:
        acc_in, top_in, total_in = rest[:3]
        outs = rest[3:]
    size = 2 * VBLK
    tiles = [slice(i * size, (i + 1) * size) for i in range(2)]
    query = rows_of(q_ref, 0)
    keys = [keys_of(kv) for kv in kv_refs]
    all_scores = [[nn_dot(query[rows], k) for k in keys] for rows in tiles]
    for rows, scores in zip(tiles, all_scores):
        top = functools.reduce(jnp.maximum, [t for s in scores for t in lane_tiles(s)])
        top = jnp.max(top, axis=1, keepdims=True) * SCALE2
        if first:
            top = jnp.broadcast_to(top, (size, HD))
            acc = total = None
        else:
            top = jnp.maximum(top, top_in[rows])
            factor = jnp.exp2(top_in[rows] - top)
            acc = acc_in[rows] * factor
            total = total_in[rows] * factor
        wide = jnp.concatenate([top] * TOWERS, axis=1)
        for s, kv in zip(scores, kv_refs):
            weights = jnp.exp2(s * SCALE2 - wide)
            part = functools.reduce(jnp.add, lane_tiles(weights))
            total = part if total is None else total + part
            part = nn_dot(weights.astype(jnp.bfloat16), rows_of(kv, 1))
            acc = part if acc is None else acc + part
        if last:
            outs[0][rows] = (acc / jnp.sum(total, axis=1, keepdims=True)).astype(jnp.bfloat16)
        else:
            outs[0][rows] = acc
            outs[1][rows] = top
            outs[2][rows] = total
            outs[3][...] = total[:8]


QUERY = pl.BlockSpec((TOWERS, 1, 1, VBLK, HD), lambda h, *_: (0, 2, h, 0, 0))
SHARD = pl.BlockSpec((TOWERS, 2, 1, VBLK, HD), lambda h, *_: (0, 0, h, 0, 0))


def flash(query, kvs, state, last, after=()):
    rows = TOWERS * VBLK
    keys = rows * len(kvs)
    wide = jax.ShapeDtypeStruct((rows, GW), jnp.float32)
    head = pl.BlockSpec((rows, HD), lambda h: (0, h))
    if last:
        out_shape = jax.ShapeDtypeStruct((rows, GW), jnp.bfloat16)
        out_specs = head
    else:
        out_shape = [wide, wide, wide, jax.ShapeDtypeStruct((8, HD), jnp.float32)]
        out_specs = [head, head, head, pl.BlockSpec((8, HD), lambda h: (0, 0))]
    return pl.pallas_call(
        functools.partial(flash_kernel, len(kvs), state is None, last, len(after)),
        out_shape=out_shape,
        grid=(LOCAL,),
        in_specs=[QUERY] + [SHARD] * len(kvs) + ([] if state is None else [head] * 3) + [ANY] * len(after),
        out_specs=out_specs,
        compiler_params=pltpu.CompilerParams(vmem_limit_bytes=60 * MIB),
        cost_estimate=BRIEF,
        name="flash",
    )(query, *kvs, *(() if state is None else state), *after)


AUDIO_ROWS = 32
BOTH = VBLK + AUDIO_ROWS


def weighted(scores, values):
    weights = jnp.exp2(scores - jnp.max(scores, axis=1, keepdims=True)).astype(jnp.bfloat16)
    result = nn_dot(weights, jnp.concatenate([values, jnp.ones_like(values)], axis=1))
    return result[:, :HD] / result[:, HD:]


def audio_rows(place, margin, main, own, sibling, third):
    ctx = place[0]
    core = lax.rem(ctx, 2)
    row_block = lax.broadcasted_iota(jnp.int32, (QROWS, 1), 0) // ABLK + ctx * 4
    query = main[QAT:]
    pieces = [(own, r, ctx * 4 + r) for r in range(TOWERS)]
    after = lax.rem(ctx + 1, 16) * 4
    before = lax.rem(ctx + 15, 16) * 4 + 2
    for r in range(2):
        pieces.append((sibling, 2 * core + r, jnp.where(core == 0, after, before) + r))
        pieces.append((third, 2 - 2 * core + r, jnp.where(core == 0, before, after) + r))
    keys = jnp.concatenate([ref[r, 0, 0] for ref, r, _ in pieces], axis=1)
    values = jnp.concatenate([ref[r, 1, 0] for ref, r, _ in pieces], axis=0)
    raw = nn_dot(query, keys) * SCALE2
    scores = []
    for i, (_, _, block) in enumerate(pieces):
        hit = (
            (row_block == margin[block, 0])
            | (row_block == margin[block, 1])
            | (row_block == margin[block, 2])
        )
        scores.append(jnp.where(hit, raw[:, i * VBLK : (i + 1) * VBLK], NEG))
    scores = jnp.concatenate(scores, axis=1)
    return weighted(scores, values)


def cross_kernel(place, margin, q_ref, *refs):
    mains, halos, (own, sibling, third, out) = refs[:4], refs[4:8], refs[8:]
    main = functools.reduce(
        jnp.add, [ref[...] for ref in mains[1:]], jnp.where(place[1] == place[2], mains[0][...], 0)
    )
    halo = functools.reduce(
        jnp.add, [ref[...] for ref in halos[1:]], jnp.where(place[1] == place[3], halos[0][...], 0)
    )
    ctx = place[0]
    phase = lax.rem(ctx, 4)
    base = (ctx - phase) * 4
    lane = lax.broadcasted_iota(jnp.int32, (1, 256), 1)
    halo_base = jnp.where(phase == 0, base - 2, jnp.where(phase == 3, base + 16, -100))
    main_base = base + lax.div(main_first(ctx), ABLK)
    ids = jnp.where(lane < WIN, lane // ABLK + main_base, lane // ABLK - WIN // ABLK + halo_base)
    ids = jnp.where(lane < WIN + HALO, ids, -100)
    spare = jnp.zeros((256 - WIN - HALO, HD), jnp.bfloat16)
    keys = jnp.concatenate([main[:WIN], halo[:HALO], spare], axis=0)
    values = jnp.concatenate(
        [main[WIN:QAT], halo[HALO:], spare], axis=0
    )
    scores = nt_dot(rows_of(q_ref, 0), keys) * SCALE2
    parts = []
    for r in range(TOWERS):
        block = ctx * 4 + r
        hit = (ids == margin[block, 0]) | (ids == margin[block, 1]) | (ids == margin[block, 2])
        parts.append(jnp.where(hit, scores[r * VBLK : (r + 1) * VBLK], NEG))
    scores = jnp.concatenate(parts, axis=0)
    result = weighted(scores, values).astype(jnp.bfloat16)
    mixed = audio_rows(place, margin, main, own, sibling, third)
    for r in range(TOWERS):
        out[r, pl.ds(0, VBLK), :] = result[r * VBLK : (r + 1) * VBLK]
        padded = jnp.concatenate(
            [mixed[r * ABLK : (r + 1) * ABLK], jnp.zeros((AUDIO_ROWS - ABLK, HD), jnp.float32)], axis=0
        )
        out[r, pl.ds(VBLK, AUDIO_ROWS), :] = padded.astype(jnp.bfloat16)


def cross(place, margin, query, mains, halos, own, sibling, third):
    rows = TOWERS * VBLK
    return pl.pallas_call(
        cross_kernel,
        out_shape=jax.ShapeDtypeStruct((TOWERS, BOTH, GW), jnp.bfloat16),
        grid_spec=pltpu.PrefetchScalarGridSpec(
            num_scalar_prefetch=2,
            grid=(LOCAL,),
            in_specs=[
                QUERY,
            ]
            + [pl.BlockSpec((HAT, HD), lambda h, *_: (0, h))] * TOWERS
            + [pl.BlockSpec((2 * HALO, HD), lambda h, *_: (0, h))] * TOWERS
            + [SHARD] * 3,
            out_specs=pl.BlockSpec((TOWERS, BOTH, HD), lambda h, *_: (0, 0, h)),
        ),
        compiler_params=pltpu.CompilerParams(vmem_limit_bytes=60 * MIB),
        cost_estimate=BRIEF,
        name="cross",
    )(place, margin, query, *mains, *halos, own, sibling, third)


def weight_rows(pieces):
    return jnp.concatenate([piece(h) for h in range(LOCAL) for piece in pieces], axis=0)


def project_cross_kernel(place, own, sibling, w_ref, _, __, mine, up, down, up_later, down_later):
    towers = [lax.rem(place[1] + step, TOWERS) for step in range(TOWERS)]
    targets = (
        (mine, 0),
        (mine, BOTH),
        (up_later, 0),
        (up, BOTH),
        (up, 0),
        (down, BOTH),
        (down, 0),
        (down_later, 0),
    )
    ws = [
        weight_rows([functools.partial(lambda b, h: w_ref[b, kind, h], b) for b in range(4)])
        for kind in range(2)
    ]
    for step in range(TOWERS):
        for w, (first, count) in zip(ws, ((0, VBLK), (VBLK, AUDIO_ROWS))):
            both = [ref[towers[step], pl.ds(first, count), :] for ref in (own, sibling)]
            y = nn_dot(jnp.concatenate(both, axis=0), w).astype(jnp.bfloat16)
            for i in range(2):
                out, at = targets[2 * step + i]
                out[pl.ds(at + first, count), :] = y[i * count : (i + 1) * count]


def project_cross(place, own, sibling, w, after):
    width = w.shape[-1]
    tile = width // 3
    return pl.pallas_call(
        project_cross_kernel,
        out_shape=[jax.ShapeDtypeStruct((n * BOTH, width), jnp.bfloat16) for n in (2, 2, 2, 1, 1)],
        grid_spec=pltpu.PrefetchScalarGridSpec(
            num_scalar_prefetch=1,
            grid=(3,),
            in_specs=[
                full(own.shape),
                full(own.shape),
                pl.BlockSpec(w.shape[:-1] + (tile,), lambda i, place: (0, 0, 0, 0, i)),
                ANY,
                ANY,
            ],
            out_specs=[
                pl.BlockSpec((n * BOTH, tile), lambda i, place: (0, i)) for n in (2, 2, 2, 1, 1)
            ],
        ),
        compiler_params=pltpu.CompilerParams(vmem_limit_bytes=60 * MIB),
        cost_estimate=BRIEF,
        name="project_cross",
    )(place, own, sibling, w, *after)


def project_self_kernel(place, own, sibling, w_ref, *refs):
    mine, up, down, up_later, down_later, gain, video_out, audio_out, sibling_out = refs
    a = jnp.concatenate(
        [jnp.concatenate([ref[t] for t in range(TOWERS)], axis=1) for ref in (own, sibling)], axis=0
    )
    w = jnp.concatenate(
        [
            weight_rows([functools.partial(lambda b, h: w_ref[b * TOWERS + lax.rem(place[1] - t + TOWERS, TOWERS), h], b) for b in range(4)])
            for t in range(TOWERS)
        ],
        axis=0,
    )
    acc = nn_dot(a, w)
    top = [mine[pl.ds(0, BOTH), :], down[pl.ds(0, BOTH), :], up_later[...]]
    bottom = [mine[pl.ds(BOTH, BOTH), :], up[pl.ds(BOTH, BOTH), :], down_later[...]]
    base = jnp.concatenate(
        [functools.reduce(jnp.add, [x.astype(jnp.float32) for x in xs]) for xs in (top, bottom)], axis=0
    )
    video, audio = [], []
    for i in range(2):
        video.append(gain[0:1] * (acc[i * VBLK : (i + 1) * VBLK] + base[i * BOTH : i * BOTH + VBLK]))
        audio.append(gain[1:2] * base[i * BOTH + VBLK : (i + 1) * BOTH])
    video_out[...] = video[0].astype(jnp.bfloat16)
    audio_out[...] = audio[0][:ABLK].astype(jnp.bfloat16)
    sibling_out[pl.ds(0, VBLK), :] = video[1].astype(jnp.bfloat16)
    sibling_out[pl.ds(VBLK, AUDIO_ROWS), :] = audio[1].astype(jnp.bfloat16)


def project_self(place, own, sibling, w, base, gains):
    width = w.shape[-1]
    tile = width // 3
    out = lambda rows: pl.BlockSpec((rows, tile), lambda i, place: (0, place[4] * 3 + i))
    return pl.pallas_call(
        project_self_kernel,
        out_shape=[
            jax.ShapeDtypeStruct((VBLK, 2 * width), jnp.bfloat16),
            jax.ShapeDtypeStruct((ABLK, 2 * width), jnp.bfloat16),
            jax.ShapeDtypeStruct((BOTH, width), jnp.bfloat16),
        ],
        grid_spec=pltpu.PrefetchScalarGridSpec(
            num_scalar_prefetch=1,
            grid=(3,),
            in_specs=[
                full(own.shape),
                full(own.shape),
                pl.BlockSpec(w.shape[:-1] + (tile,), lambda i, place: (0, 0, 0, i)),
            ]
            + [pl.BlockSpec((n * BOTH, tile), lambda i, place: (0, i)) for n in (2, 2, 2, 1, 1)]
            + [pl.BlockSpec((2, tile), lambda i, place: (0, place[4] * 3 + i))],
            out_specs=[out(VBLK), out(ABLK), pl.BlockSpec((BOTH, tile), lambda i, place: (0, i))],
        ),
        compiler_params=pltpu.CompilerParams(vmem_limit_bytes=24 * MIB),
        cost_estimate=BRIEF,
        name="project_self",
    )(place, own, sibling, w, *base, gains)


def assemble_kernel(place, video_in, audio_in, theirs, video, audio):
    video[...] = theirs[pl.ds(0, VBLK), :]
    audio[...] = theirs[pl.ds(VBLK, AUDIO_ROWS), :].astype(jnp.float32)[:ABLK].astype(jnp.bfloat16)


def assemble(place, video, audio, theirs):
    width = theirs.shape[1]

    def column(i, place):
        return (0, 1 - place[4])

    return pl.pallas_call(
        assemble_kernel,
        out_shape=[jax.ShapeDtypeStruct(x.shape, x.dtype) for x in (video, audio)],
        grid_spec=pltpu.PrefetchScalarGridSpec(
            num_scalar_prefetch=1,
            grid=(1,),
            in_specs=[ANY, ANY, full(theirs.shape)],
            out_specs=[pl.BlockSpec((VBLK, width), column), pl.BlockSpec((ABLK, width), column)],
        ),
        input_output_aliases={1: 0, 2: 1},
        compiler_params=pltpu.CompilerParams(vmem_limit_bytes=16 * MIB),
        name="assemble",
    )(place, video, audio, theirs)


def gate_kernel(*refs):
    pass


def gate(value, *after):
    return pl.pallas_call(
        gate_kernel,
        out_shape=jax.ShapeDtypeStruct(value.shape, value.dtype),
        in_specs=[ANY] * (1 + len(after)),
        out_specs=ANY,
        input_output_aliases={0: 0},
        compiler_params=pltpu.CompilerParams(vmem_limit_bytes=60 * MIB),
        name="gate",
    )(value, *after)


def exchange_towers(value):
    return lax.all_to_all(value, "tower", split_axis=0, concat_axis=0, tiled=True)


def add(a, b):
    return (a.astype(jnp.float32) + b.astype(jnp.float32)).astype(jnp.bfloat16)


def shift_tower(value, step):
    return lax.ppermute(value, "tower", [(i, (i + step) % TOWERS) for i in range(TOWERS)])


def hop(value):
    total = 2 * CHIPS
    return lax.ppermute(value, "ctx", [(i, (i + 2 - 4 * (i % 2)) % total) for i in range(total)])


def swap_core(value):
    return lax.ppermute(value, "ctx", [(i, i ^ 1) for i in range(2 * CHIPS)])


def shards(video_q, video_k, video_v, audio_q, audio_k, audio_v, margin, out_weight, gate_gains):
    ctx = lax.axis_index("ctx")
    tower = lax.axis_index("tower")
    core = lax.rem(ctx, 2)
    place = jnp.stack([ctx, tower, ctx // 4, edge_tower(ctx), core]).astype(jnp.int32)
    gains = gate_gains[0]
    margins = margin[0]

    parts, w_self, w_rest, *audio = pack(
        place, video_k[0], video_v[0], video_q[0], audio_k[0], audio_v[0], audio_q[0], out_weight
    )
    w_rest = lax.all_gather(w_rest, "batch", axis=0, tiled=False)
    query = exchange_towers(parts)
    own = query[:, :2]
    sibling = swap_core(own)
    near, far = hop(own), hop(sibling)
    audio = [gate(rows, own) for rows in audio]
    mains = [audio[0]] + [send_main(audio[step], step) for step in (1, 2, 3)]
    halos = [audio[4]] + [send_halo(audio[4 + step], step) for step in (1, 2, 3)]

    acc, top, total, token = flash(query, [own, sibling], None, False)
    near, far = gate(near, token, *mains[1:], *halos[1:]), gate(far, token)
    crossed = cross(place, margins, query, mains, halos, own, sibling, far)
    w_self = gate(w_self, token, *mains[1:])
    w_parts = jnp.stack([w_self] + [shift_tower(w_self, step) for step in (1, 2, 3)])
    w_self = lax.all_gather(w_parts, "batch", axis=0, tiled=False)
    w_self = w_self.reshape((16,) + w_self.shape[2:])

    tokens = [token]
    after = (crossed,)
    for step in range(1, 4):
        now = [near, far, swap_core(near), swap_core(far)]
        near, far = hop(near), (hop(far) if step < 3 else None)
        acc, top, total, token = flash(query, now, (acc, top, total), False, after)
        tokens.append(token)
        after = ()
        if step == 1:
            rest, up, down, up_later, down_later = project_cross(
                place, crossed, swap_core(crossed), w_rest, (token, w_parts)
            )
            after = (rest,)
            up, down = shift_tower(up, 1), shift_tower(down, -1)
        near = gate(near, tokens[step - 1])
        if step < 3:
            far = gate(far, tokens[step - 1])
    up_later = add(gate(up_later, token), up[:BOTH])
    down_later = add(gate(down_later, token), down[BOTH:])
    after = (up_later, down_later)
    up_later, down_later = shift_tower(up_later, 1), shift_tower(down_later, -1)
    video_self = flash(query, [near, swap_core(near)], (acc, top, total), True, after)
    base = (rest, up, down, up_later, down_later)

    self_all = exchange_towers(video_self.reshape(TOWERS, VBLK, GW))
    video_out, audio_out, theirs = project_self(place, self_all, swap_core(self_all), w_self, base, gains)
    video_out, audio_out = assemble(place, video_out, audio_out, swap_core(theirs))
    return (video_out[None], audio_out[None])


def solution(mesh):
    return jax.shard_map(
        shards,
        mesh=mesh,
        in_specs=(
            P("batch", ("ctx", "tower"), None),
            P("batch", ("ctx", "tower"), None),
            P("batch", ("ctx", "tower"), None),
            P("batch", "tower", None),
            P("batch", "tower", None),
            P("batch", "tower", None),
            P("batch", None, None),
            P(None, "tower", "batch", None),
            P("batch", None, None),
        ),
        out_specs=(P("batch", ("ctx", "tower"), None), P("batch", ("ctx", "tower"), None)),
        check_vma=False,
    )
```

```python
import functools

import jax
import jax.numpy as jnp
from jax import lax
from jax.experimental import pallas as pl
from jax.experimental.pallas import tpu as pltpu
from jax.sharding import PartitionSpec as P

H = 12
HD = 128
VBLK = 128
ABLK = 24
TOWERS = 4
CHIPS = 8
LOCAL = H // TOWERS
GW = LOCAL * HD
NEG = -1e30
SCALE2 = HD**-0.5 * 1.4426950408889634
MIB = 1024 * 1024


def nt_dot(a, b):
    return lax.dot_general(a, b, (((1,), (1,)), ((), ())), preferred_element_type=jnp.float32)


def nn_dot(a, b):
    return jnp.dot(a, b, preferred_element_type=jnp.float32)


def full(shape):
    return pl.BlockSpec(shape, lambda *_: (0,) * len(shape))


BRIEF = pl.CostEstimate(flops=1, bytes_accessed=1, transcendentals=0)
ANY = pl.BlockSpec(memory_space=pl.ANY)


def start_copies(pairs, sem, first):
    copies = [pltpu.make_async_copy(a, b, sem.at[first + i]) for i, (a, b) in enumerate(pairs)]
    for copy in copies:
        copy.start()
    return copies


WIN = 192
HALO = 48
QROWS = 96
QAT = 2 * WIN
HAT = QAT + QROWS
AROWS = HAT + 2 * HALO


def main_first(ctx):
    return jnp.clip(lax.rem(ctx, 4) * QROWS - HALO, 0, 384 - WIN)


def edge_tower(ctx):
    phase = lax.rem(ctx, 4)
    edge = jnp.where(phase == 0, ctx // 4 - 1, ctx // 4 + 1)
    return jnp.where(((phase == 0) | (phase == 3)) & (edge >= 0) & (edge < TOWERS), edge, -1)


def pack_kernel(
    place, k_ref, v_ref, q_ref, ak_ref, av_ref, aq_ref, w_ref,
    out, self_out, rest_out, main0, main1, main2, main3, halo0, halo1, halo2, halo3,
    rows, turned, audio, w_rows, sem,
):
    ctx, tower = place[0], place[1]
    phase = lax.rem(ctx, 4)
    main = pl.ds(pl.multiple_of(main_first(ctx), 16), WIN)
    mine = pl.ds(pl.multiple_of(phase * QROWS, 16), QROWS)
    halo = pl.ds(pl.multiple_of(jnp.where(phase == 0, 384 - HALO, 0), 16), HALO)
    half = w_ref.shape[3] // 2
    columns = pl.ds(pl.multiple_of(place[4] * half, 128), half)
    coming = start_copies([(ref, rows.at[i]) for i, ref in enumerate((k_ref, v_ref, q_ref))], sem, 0)
    coming_w = start_copies([(w_ref.at[:, :, :, columns], w_rows)], sem, 3)
    coming_audio = start_copies(
        [
            (ak_ref.at[main], audio.at[pl.ds(0, WIN)]),
            (av_ref.at[main], audio.at[pl.ds(WIN, WIN)]),
            (aq_ref.at[mine], audio.at[pl.ds(QAT, QROWS)]),
            (ak_ref.at[halo], audio.at[pl.ds(HAT, HALO)]),
            (av_ref.at[halo], audio.at[pl.ds(HAT + HALO, HALO)]),
        ],
        sem,
        4,
    )
    heads = [(g, h) for g in range(TOWERS) for h in range(LOCAL)]
    going = []
    for i in (1, 2):
        coming[i].wait()
        pairs = [
            (rows.at[i, :, pl.ds((g * LOCAL + h) * HD, HD)], out.at[g, i, h]) for g, h in heads
        ]
        going += start_copies(pairs, sem, 9 + (i - 1) * H)
    coming[0].wait()
    for g, h in heads:
        block = rows[0, :, pl.ds((g * LOCAL + h) * HD, HD)]
        turned[g, h] = block.astype(jnp.float32).T.astype(jnp.bfloat16)
    going += start_copies([(turned.at[g], out.at[g, 0]) for g in range(TOWERS)], sem, 33)
    coming_w[0].wait()
    going += start_copies([(w_rows.at[0], self_out), (w_rows.at[pl.ds(1, 2)], rest_out)], sem, 37)
    for copy in coming_audio:
        copy.wait()
    pairs = []
    for step, (main_out, halo_out) in enumerate(
        ((main0, halo0), (main1, halo1), (main2, halo2), (main3, halo3))
    ):
        group = pl.ds(pl.multiple_of(lax.rem(tower + step, TOWERS) * GW, 128), GW)
        pairs.append((audio.at[pl.ds(0, HAT), group], main_out))
        pairs.append((audio.at[pl.ds(HAT, 2 * HALO), group], halo_out))
    going += start_copies(pairs, sem, 39)
    for copy in going:
        copy.wait()


def pack(place, k, v, q, ak, av, aq, w):
    rows = k.shape[0]
    narrow = (LOCAL, w.shape[2], w.shape[3] // 2)
    shapes = [(TOWERS, 3, LOCAL, rows, HD), narrow, (2,) + narrow]
    shapes += [(HAT, GW)] * TOWERS + [(2 * HALO, GW)] * TOWERS
    return pl.pallas_call(
        pack_kernel,
        out_shape=[jax.ShapeDtypeStruct(shape, jnp.bfloat16) for shape in shapes],
        grid_spec=pltpu.PrefetchScalarGridSpec(
            num_scalar_prefetch=1,
            grid=(1,),
            in_specs=[ANY] * 7,
            out_specs=[ANY] * len(shapes),
            scratch_shapes=[
                pltpu.VMEM((3,) + k.shape, jnp.bfloat16),
                pltpu.VMEM((TOWERS, LOCAL, HD, rows), jnp.bfloat16),
                pltpu.VMEM((AROWS, aq.shape[1]), jnp.bfloat16),
                pltpu.VMEM((3,) + narrow, jnp.bfloat16),
                pltpu.SemaphoreType.DMA((47,)),
            ],
        ),
        compiler_params=pltpu.CompilerParams(vmem_limit_bytes=60 * MIB),
        name="pack",
    )(place, k, v, q, ak, av, aq, w)


def ctx_towers(pairs):
    return [(c * TOWERS + s, c * TOWERS + d) for c, s, d in pairs]


def send_main(value, step):
    pairs = [(c, c // 4, (c // 4 + step) % TOWERS) for c in range(16)]
    return lax.ppermute(value, ("ctx", "tower"), ctx_towers(pairs))


def send_halo(value, step):
    pairs = []
    for c in range(16):
        source = c // 4 - 1 if c % 4 == 0 else c // 4 + 1
        if c % 4 in (0, 3) and 0 <= source < TOWERS:
            pairs.append((c, source, (source + step) % TOWERS))
    return lax.ppermute(value, ("ctx", "tower"), ctx_towers(pairs))


def keys_of(kv_ref):
    return jnp.concatenate([kv_ref[r, 0, 0] for r in range(TOWERS)], axis=1)


def rows_of(kv_ref, which):
    return jnp.concatenate([kv_ref[r, which, 0] for r in range(TOWERS)], axis=0)


def lane_tiles(x):
    return [x[:, i : i + HD] for i in range(0, x.shape[1], HD)]


def flash_kernel(kv_count, first, last, after, *refs):
    q_ref = refs[0]
    kv_refs = refs[1 : 1 + kv_count]
    rest = refs[1 + kv_count :]
    rest = rest[: len(rest) - (1 if last else 4) - after] + rest[len(rest) - (1 if last else 4) :]
    if first:
        outs = rest
    else:
        acc_in, top_in, total_in = rest[:3]
        outs = rest[3:]
    size = 2 * VBLK
    tiles = [slice(i * size, (i + 1) * size) for i in range(2)]
    query = rows_of(q_ref, 0)
    keys = [keys_of(kv) for kv in kv_refs]
    all_scores = [[nn_dot(query[rows], k) for k in keys] for rows in tiles]
    for rows, scores in zip(tiles, all_scores):
        top = functools.reduce(jnp.maximum, [t for s in scores for t in lane_tiles(s)])
        top = jnp.max(top, axis=1, keepdims=True) * SCALE2
        if first:
            top = jnp.broadcast_to(top, (size, HD))
            acc = total = None
        else:
            top = jnp.maximum(top, top_in[rows])
            factor = jnp.exp2(top_in[rows] - top)
            acc = acc_in[rows] * factor
            total = total_in[rows] * factor
        wide = jnp.concatenate([top] * TOWERS, axis=1)
        for s, kv in zip(scores, kv_refs):
            weights = jnp.exp2(s * SCALE2 - wide)
            part = functools.reduce(jnp.add, lane_tiles(weights))
            total = part if total is None else total + part
            part = nn_dot(weights.astype(jnp.bfloat16), rows_of(kv, 1))
            acc = part if acc is None else acc + part
        if last:
            outs[0][rows] = (acc / jnp.sum(total, axis=1, keepdims=True)).astype(jnp.bfloat16)
        else:
            outs[0][rows] = acc
            outs[1][rows] = top
            outs[2][rows] = total
            outs[3][...] = total[:8]


QUERY = pl.BlockSpec((TOWERS, 1, 1, VBLK, HD), lambda h, *_: (0, 2, h, 0, 0))
SHARD = pl.BlockSpec((TOWERS, 2, 1, VBLK, HD), lambda h, *_: (0, 0, h, 0, 0))


def flash(query, kvs, state, last, after=()):
    rows = TOWERS * VBLK
    keys = rows * len(kvs)
    wide = jax.ShapeDtypeStruct((rows, GW), jnp.float32)
    head = pl.BlockSpec((rows, HD), lambda h: (0, h))
    if last:
        out_shape = jax.ShapeDtypeStruct((rows, GW), jnp.bfloat16)
        out_specs = head
    else:
        out_shape = [wide, wide, wide, jax.ShapeDtypeStruct((8, HD), jnp.float32)]
        out_specs = [head, head, head, pl.BlockSpec((8, HD), lambda h: (0, 0))]
    return pl.pallas_call(
        functools.partial(flash_kernel, len(kvs), state is None, last, len(after)),
        out_shape=out_shape,
        grid=(LOCAL,),
        in_specs=[QUERY] + [SHARD] * len(kvs) + ([] if state is None else [head] * 3) + [ANY] * len(after),
        out_specs=out_specs,
        compiler_params=pltpu.CompilerParams(vmem_limit_bytes=60 * MIB),
        cost_estimate=BRIEF,
        name="flash",
    )(query, *kvs, *(() if state is None else state), *after)


AUDIO_ROWS = 32
BOTH = VBLK + AUDIO_ROWS


def weighted(scores, values):
    weights = jnp.exp2(scores - jnp.max(scores, axis=1, keepdims=True)).astype(jnp.bfloat16)
    result = nn_dot(weights, jnp.concatenate([values, jnp.ones_like(values)], axis=1))
    return result[:, :HD] / result[:, HD:]


def audio_rows(place, margin, main, own, sibling, third):
    ctx = place[0]
    core = lax.rem(ctx, 2)
    row_block = lax.broadcasted_iota(jnp.int32, (QROWS, 1), 0) // ABLK + ctx * 4
    query = main[QAT:]
    pieces = [(own, r, ctx * 4 + r) for r in range(TOWERS)]
    after = lax.rem(ctx + 1, 16) * 4
    before = lax.rem(ctx + 15, 16) * 4 + 2
    for r in range(2):
        pieces.append((sibling, 2 * core + r, jnp.where(core == 0, after, before) + r))
        pieces.append((third, 2 - 2 * core + r, jnp.where(core == 0, before, after) + r))
    keys = jnp.concatenate([ref[r, 0, 0] for ref, r, _ in pieces], axis=1)
    values = jnp.concatenate([ref[r, 1, 0] for ref, r, _ in pieces], axis=0)
    raw = nn_dot(query, keys) * SCALE2
    scores = []
    for i, (_, _, block) in enumerate(pieces):
        hit = (
            (row_block == margin[block, 0])
            | (row_block == margin[block, 1])
            | (row_block == margin[block, 2])
        )
        scores.append(jnp.where(hit, raw[:, i * VBLK : (i + 1) * VBLK], NEG))
    scores = jnp.concatenate(scores, axis=1)
    return weighted(scores, values)


def cross_kernel(place, margin, q_ref, *refs):
    mains, halos, (own, sibling, third, out) = refs[:4], refs[4:8], refs[8:]
    main = functools.reduce(
        jnp.add, [ref[...] for ref in mains[1:]], jnp.where(place[1] == place[2], mains[0][...], 0)
    )
    halo = functools.reduce(
        jnp.add, [ref[...] for ref in halos[1:]], jnp.where(place[1] == place[3], halos[0][...], 0)
    )
    ctx = place[0]
    phase = lax.rem(ctx, 4)
    base = (ctx - phase) * 4
    lane = lax.broadcasted_iota(jnp.int32, (1, 256), 1)
    halo_base = jnp.where(phase == 0, base - 2, jnp.where(phase == 3, base + 16, -100))
    main_base = base + lax.div(main_first(ctx), ABLK)
    ids = jnp.where(lane < WIN, lane // ABLK + main_base, lane // ABLK - WIN // ABLK + halo_base)
    ids = jnp.where(lane < WIN + HALO, ids, -100)
    spare = jnp.zeros((256 - WIN - HALO, HD), jnp.bfloat16)
    keys = jnp.concatenate([main[:WIN], halo[:HALO], spare], axis=0)
    values = jnp.concatenate(
        [main[WIN:QAT], halo[HALO:], spare], axis=0
    )
    scores = nt_dot(rows_of(q_ref, 0), keys) * SCALE2
    parts = []
    for r in range(TOWERS):
        block = ctx * 4 + r
        hit = (ids == margin[block, 0]) | (ids == margin[block, 1]) | (ids == margin[block, 2])
        parts.append(jnp.where(hit, scores[r * VBLK : (r + 1) * VBLK], NEG))
    scores = jnp.concatenate(parts, axis=0)
    result = weighted(scores, values).astype(jnp.bfloat16)
    mixed = audio_rows(place, margin, main, own, sibling, third)
    for r in range(TOWERS):
        out[r, pl.ds(0, VBLK), :] = result[r * VBLK : (r + 1) * VBLK]
        padded = jnp.concatenate(
            [mixed[r * ABLK : (r + 1) * ABLK], jnp.zeros((AUDIO_ROWS - ABLK, HD), jnp.float32)], axis=0
        )
        out[r, pl.ds(VBLK, AUDIO_ROWS), :] = padded.astype(jnp.bfloat16)


def cross(place, margin, query, mains, halos, own, sibling, third):
    rows = TOWERS * VBLK
    return pl.pallas_call(
        cross_kernel,
        out_shape=jax.ShapeDtypeStruct((TOWERS, BOTH, GW), jnp.bfloat16),
        grid_spec=pltpu.PrefetchScalarGridSpec(
            num_scalar_prefetch=2,
            grid=(LOCAL,),
            in_specs=[
                QUERY,
            ]
            + [pl.BlockSpec((HAT, HD), lambda h, *_: (0, h))] * TOWERS
            + [pl.BlockSpec((2 * HALO, HD), lambda h, *_: (0, h))] * TOWERS
            + [SHARD] * 3,
            out_specs=pl.BlockSpec((TOWERS, BOTH, HD), lambda h, *_: (0, 0, h)),
        ),
        compiler_params=pltpu.CompilerParams(vmem_limit_bytes=60 * MIB),
        cost_estimate=BRIEF,
        name="cross",
    )(place, margin, query, *mains, *halos, own, sibling, third)


def weight_rows(pieces):
    return jnp.concatenate([piece(h) for h in range(LOCAL) for piece in pieces], axis=0)


def project_cross_kernel(place, own, sibling, w_ref, _, __, mine, up, down, up_later, down_later):
    towers = [lax.rem(place[1] + step, TOWERS) for step in range(TOWERS)]
    targets = (
        (mine, 0),
        (mine, BOTH),
        (up_later, 0),
        (up, BOTH),
        (up, 0),
        (down, BOTH),
        (down, 0),
        (down_later, 0),
    )
    ws = [
        weight_rows([functools.partial(lambda b, h: w_ref[b, kind, h], b) for b in range(4)])
        for kind in range(2)
    ]
    for step in range(TOWERS):
        for w, (first, count) in zip(ws, ((0, VBLK), (VBLK, AUDIO_ROWS))):
            both = [ref[towers[step], pl.ds(first, count), :] for ref in (own, sibling)]
            y = nn_dot(jnp.concatenate(both, axis=0), w).astype(jnp.bfloat16)
            for i in range(2):
                out, at = targets[2 * step + i]
                out[pl.ds(at + first, count), :] = y[i * count : (i + 1) * count]


def project_cross(place, own, sibling, w, after):
    width = w.shape[-1]
    tile = width // 3
    return pl.pallas_call(
        project_cross_kernel,
        out_shape=[jax.ShapeDtypeStruct((n * BOTH, width), jnp.bfloat16) for n in (2, 2, 2, 1, 1)],
        grid_spec=pltpu.PrefetchScalarGridSpec(
            num_scalar_prefetch=1,
            grid=(3,),
            in_specs=[
                full(own.shape),
                full(own.shape),
                pl.BlockSpec(w.shape[:-1] + (tile,), lambda i, place: (0, 0, 0, 0, i)),
                ANY,
                ANY,
            ],
            out_specs=[
                pl.BlockSpec((n * BOTH, tile), lambda i, place: (0, i)) for n in (2, 2, 2, 1, 1)
            ],
        ),
        compiler_params=pltpu.CompilerParams(vmem_limit_bytes=60 * MIB),
        cost_estimate=BRIEF,
        name="project_cross",
    )(place, own, sibling, w, *after)


def project_self_kernel(place, own, sibling, w_ref, *refs):
    mine, up, down, up_later, down_later, gain, video_out, audio_out, sibling_out = refs
    a = jnp.concatenate(
        [jnp.concatenate([ref[t] for t in range(TOWERS)], axis=1) for ref in (own, sibling)], axis=0
    )
    w = jnp.concatenate(
        [
            weight_rows([functools.partial(lambda b, h: w_ref[b * TOWERS + t, h], b) for b in range(4)])
            for t in range(TOWERS)
        ],
        axis=0,
    )
    acc = nn_dot(a, w)
    top = [mine[pl.ds(0, BOTH), :], down[pl.ds(0, BOTH), :], up_later[...]]
    bottom = [mine[pl.ds(BOTH, BOTH), :], up[pl.ds(BOTH, BOTH), :], down_later[...]]
    base = jnp.concatenate(
        [functools.reduce(jnp.add, [x.astype(jnp.float32) for x in xs]) for xs in (top, bottom)], axis=0
    )
    video, audio = [], []
    for i in range(2):
        video.append(gain[0:1] * (acc[i * VBLK : (i + 1) * VBLK] + base[i * BOTH : i * BOTH + VBLK]))
        audio.append(gain[1:2] * base[i * BOTH + VBLK : (i + 1) * BOTH])
    video_out[...] = video[0].astype(jnp.bfloat16)
    audio_out[...] = audio[0][:ABLK].astype(jnp.bfloat16)
    sibling_out[pl.ds(0, VBLK), :] = video[1].astype(jnp.bfloat16)
    sibling_out[pl.ds(VBLK, AUDIO_ROWS), :] = audio[1].astype(jnp.bfloat16)


def project_self(place, own, sibling, w, base, gains):
    width = w.shape[-1]
    tile = width // 3
    out = lambda rows: pl.BlockSpec((rows, tile), lambda i, place: (0, place[4] * 3 + i))
    return pl.pallas_call(
        project_self_kernel,
        out_shape=[
            jax.ShapeDtypeStruct((VBLK, 2 * width), jnp.bfloat16),
            jax.ShapeDtypeStruct((ABLK, 2 * width), jnp.bfloat16),
            jax.ShapeDtypeStruct((BOTH, width), jnp.bfloat16),
        ],
        grid_spec=pltpu.PrefetchScalarGridSpec(
            num_scalar_prefetch=1,
            grid=(3,),
            in_specs=[
                full(own.shape),
                full(own.shape),
                pl.BlockSpec(w.shape[:-1] + (tile,), lambda i, place: (0, 0, 0, i)),
            ]
            + [pl.BlockSpec((n * BOTH, tile), lambda i, place: (0, i)) for n in (2, 2, 2, 1, 1)]
            + [pl.BlockSpec((2, tile), lambda i, place: (0, place[4] * 3 + i))],
            out_specs=[out(VBLK), out(ABLK), pl.BlockSpec((BOTH, tile), lambda i, place: (0, i))],
        ),
        compiler_params=pltpu.CompilerParams(vmem_limit_bytes=24 * MIB),
        cost_estimate=BRIEF,
        name="project_self",
    )(place, own, sibling, w, *base, gains)


def assemble_kernel(place, video_in, audio_in, theirs, video, audio):
    video[...] = theirs[pl.ds(0, VBLK), :]
    audio[...] = theirs[pl.ds(VBLK, AUDIO_ROWS), :].astype(jnp.float32)[:ABLK].astype(jnp.bfloat16)


def assemble(place, video, audio, theirs):
    width = theirs.shape[1]

    def column(i, place):
        return (0, 1 - place[4])

    return pl.pallas_call(
        assemble_kernel,
        out_shape=[jax.ShapeDtypeStruct(x.shape, x.dtype) for x in (video, audio)],
        grid_spec=pltpu.PrefetchScalarGridSpec(
            num_scalar_prefetch=1,
            grid=(1,),
            in_specs=[ANY, ANY, full(theirs.shape)],
            out_specs=[pl.BlockSpec((VBLK, width), column), pl.BlockSpec((ABLK, width), column)],
        ),
        input_output_aliases={1: 0, 2: 1},
        compiler_params=pltpu.CompilerParams(vmem_limit_bytes=16 * MIB),
        name="assemble",
    )(place, video, audio, theirs)


def gate_kernel(*refs):
    pass


def gate(value, *after):
    return pl.pallas_call(
        gate_kernel,
        out_shape=jax.ShapeDtypeStruct(value.shape, value.dtype),
        in_specs=[ANY] * (1 + len(after)),
        out_specs=ANY,
        input_output_aliases={0: 0},
        compiler_params=pltpu.CompilerParams(vmem_limit_bytes=60 * MIB),
        name="gate",
    )(value, *after)


def exchange_towers(value):
    return lax.all_to_all(value, "tower", split_axis=0, concat_axis=0, tiled=True)


def add(a, b):
    return (a.astype(jnp.float32) + b.astype(jnp.float32)).astype(jnp.bfloat16)


def shift_tower(value, step):
    return lax.ppermute(value, "tower", [(i, (i + step) % TOWERS) for i in range(TOWERS)])


def hop(value):
    total = 2 * CHIPS
    return lax.ppermute(value, "ctx", [(i, (i + 2 - 4 * (i % 2)) % total) for i in range(total)])


def swap_core(value):
    return lax.ppermute(value, "ctx", [(i, i ^ 1) for i in range(2 * CHIPS)])


def shards(video_q, video_k, video_v, audio_q, audio_k, audio_v, margin, out_weight, gate_gains):
    ctx = lax.axis_index("ctx")
    tower = lax.axis_index("tower")
    core = lax.rem(ctx, 2)
    place = jnp.stack([ctx, tower, ctx // 4, edge_tower(ctx), core]).astype(jnp.int32)
    gains = gate_gains[0]
    margins = margin[0]

    parts, w_self, w_rest, *audio = pack(
        place, video_k[0], video_v[0], video_q[0], audio_k[0], audio_v[0], audio_q[0], out_weight
    )
    w_rest = lax.all_gather(w_rest, "batch", axis=0, tiled=False)
    w_self = lax.all_gather(w_self, ("batch", "tower"), axis=0, tiled=False)
    query = exchange_towers(parts)
    own = query[:, :2]
    sibling = swap_core(own)
    near, far = hop(own), hop(sibling)
    audio = [gate(rows, own) for rows in audio]
    mains = [audio[0]] + [send_main(audio[step], step) for step in (1, 2, 3)]
    halos = [audio[4]] + [send_halo(audio[4 + step], step) for step in (1, 2, 3)]

    acc, top, total, token = flash(query, [own, sibling], None, False)
    near, far = gate(near, token, *mains[1:], *halos[1:]), gate(far, token)
    crossed = cross(place, margins, query, mains, halos, own, sibling, far)

    tokens = [token]
    after = (crossed,)
    for step in range(1, 4):
        now = [near, far, swap_core(near), swap_core(far)]
        near, far = hop(near), (hop(far) if step < 3 else None)
        acc, top, total, token = flash(query, now, (acc, top, total), False, after)
        tokens.append(token)
        after = ()
        if step == 1:
            rest, up, down, up_later, down_later = project_cross(
                place, crossed, swap_core(crossed), w_rest, (token, token)
            )
            after = (rest,)
            up, down = shift_tower(up, 1), shift_tower(down, -1)
        near = gate(near, tokens[step - 1])
        if step < 3:
            far = gate(far, tokens[step - 1])
    video_self = flash(query, [near, swap_core(near)], (acc, top, total), True)
    up_later = add(gate(up_later, video_self), up[:BOTH])
    down_later = add(gate(down_later, video_self), down[BOTH:])
    up_later, down_later = shift_tower(up_later, 1), shift_tower(down_later, -1)
    base = (rest, up, down, up_later, down_later)

    self_all = exchange_towers(video_self.reshape(TOWERS, VBLK, GW))
    video_out, audio_out, theirs = project_self(place, self_all, swap_core(self_all), w_self, base, gains)
    video_out, audio_out = assemble(place, video_out, audio_out, swap_core(theirs))
    return (video_out[None], audio_out[None])


def solution(mesh):
    return jax.shard_map(
        shards,
        mesh=mesh,
        in_specs=(
            P("batch", ("ctx", "tower"), None),
            P("batch", ("ctx", "tower"), None),
            P("batch", ("ctx", "tower"), None),
            P("batch", "tower", None),
            P("batch", "tower", None),
            P("batch", "tower", None),
            P("batch", None, None),
            P(None, "tower", "batch", None),
            P("batch", None, None),
        ),
        out_specs=(P("batch", ("ctx", "tower"), None), P("batch", ("ctx", "tower"), None)),
        check_vma=False,
    )
```

```python
import functools

import jax
import jax.numpy as jnp
from jax import lax
from jax.experimental import pallas as pl
from jax.experimental.pallas import tpu as pltpu
from jax.sharding import PartitionSpec as P

H = 12
HD = 128
VBLK = 128
ABLK = 24
TOWERS = 4
CHIPS = 8
LOCAL = H // TOWERS
GW = LOCAL * HD
NEG = -1e30
SCALE2 = HD**-0.5 * 1.4426950408889634
MIB = 1024 * 1024


def nt_dot(a, b):
    return lax.dot_general(a, b, (((1,), (1,)), ((), ())), preferred_element_type=jnp.float32)


def nn_dot(a, b):
    return jnp.dot(a, b, preferred_element_type=jnp.float32)


def full(shape):
    return pl.BlockSpec(shape, lambda *_: (0,) * len(shape))


BRIEF = pl.CostEstimate(flops=1, bytes_accessed=1, transcendentals=0)
ANY = pl.BlockSpec(memory_space=pl.ANY)


def start_copies(pairs, sem, first):
    copies = [pltpu.make_async_copy(a, b, sem.at[first + i]) for i, (a, b) in enumerate(pairs)]
    for copy in copies:
        copy.start()
    return copies


WIN = 192
HALO = 48
QROWS = 96
QAT = 2 * WIN
HAT = QAT + QROWS
AROWS = HAT + 2 * HALO


def main_first(ctx):
    return jnp.clip(lax.rem(ctx, 4) * QROWS - HALO, 0, 384 - WIN)


def edge_tower(ctx):
    phase = lax.rem(ctx, 4)
    edge = jnp.where(phase == 0, ctx // 4 - 1, ctx // 4 + 1)
    return jnp.where(((phase == 0) | (phase == 3)) & (edge >= 0) & (edge < TOWERS), edge, -1)


def pack_kernel(
    place, k_ref, v_ref, q_ref, ak_ref, av_ref, aq_ref, w_ref,
    out, self_out, rest_out, main0, main1, main2, main3, halo0, halo1, halo2, halo3,
    rows, turned, audio, w_rows, sem,
):
    ctx, tower = place[0], place[1]
    phase = lax.rem(ctx, 4)
    main = pl.ds(pl.multiple_of(main_first(ctx), 16), WIN)
    mine = pl.ds(pl.multiple_of(phase * QROWS, 16), QROWS)
    halo = pl.ds(pl.multiple_of(jnp.where(phase == 0, 384 - HALO, 0), 16), HALO)
    half = w_ref.shape[3] // 2
    columns = pl.ds(pl.multiple_of(place[4] * half, 128), half)
    coming = start_copies([(ref, rows.at[i]) for i, ref in enumerate((k_ref, v_ref, q_ref))], sem, 0)
    coming_w = start_copies([(w_ref.at[:, :, :, columns], w_rows)], sem, 3)
    coming_audio = start_copies(
        [
            (ak_ref.at[main], audio.at[pl.ds(0, WIN)]),
            (av_ref.at[main], audio.at[pl.ds(WIN, WIN)]),
            (aq_ref.at[mine], audio.at[pl.ds(QAT, QROWS)]),
            (ak_ref.at[halo], audio.at[pl.ds(HAT, HALO)]),
            (av_ref.at[halo], audio.at[pl.ds(HAT + HALO, HALO)]),
        ],
        sem,
        4,
    )
    heads = [(g, h) for g in range(TOWERS) for h in range(LOCAL)]
    going = []
    for i in (1, 2):
        coming[i].wait()
        pairs = [
            (rows.at[i, :, pl.ds((g * LOCAL + h) * HD, HD)], out.at[g, i, h]) for g, h in heads
        ]
        going += start_copies(pairs, sem, 9 + (i - 1) * H)
    coming[0].wait()
    for g, h in heads:
        block = rows[0, :, pl.ds((g * LOCAL + h) * HD, HD)]
        turned[g, h] = block.astype(jnp.float32).T.astype(jnp.bfloat16)
    going += start_copies([(turned.at[g], out.at[g, 0]) for g in range(TOWERS)], sem, 33)
    coming_w[0].wait()
    going += start_copies([(w_rows.at[0], self_out), (w_rows.at[pl.ds(1, 2)], rest_out)], sem, 37)
    for copy in coming_audio:
        copy.wait()
    pairs = []
    for step, (main_out, halo_out) in enumerate(
        ((main0, halo0), (main1, halo1), (main2, halo2), (main3, halo3))
    ):
        group = pl.ds(pl.multiple_of(lax.rem(tower + step, TOWERS) * GW, 128), GW)
        pairs.append((audio.at[pl.ds(0, HAT), group], main_out))
        pairs.append((audio.at[pl.ds(HAT, 2 * HALO), group], halo_out))
    going += start_copies(pairs, sem, 39)
    for copy in going:
        copy.wait()


def pack(place, k, v, q, ak, av, aq, w):
    rows = k.shape[0]
    narrow = (LOCAL, w.shape[2], w.shape[3] // 2)
    shapes = [(TOWERS, 3, LOCAL, rows, HD), narrow, (2,) + narrow]
    shapes += [(HAT, GW)] * TOWERS + [(2 * HALO, GW)] * TOWERS
    return pl.pallas_call(
        pack_kernel,
        out_shape=[jax.ShapeDtypeStruct(shape, jnp.bfloat16) for shape in shapes],
        grid_spec=pltpu.PrefetchScalarGridSpec(
            num_scalar_prefetch=1,
            grid=(1,),
            in_specs=[ANY] * 7,
            out_specs=[ANY] * len(shapes),
            scratch_shapes=[
                pltpu.VMEM((3,) + k.shape, jnp.bfloat16),
                pltpu.VMEM((TOWERS, LOCAL, HD, rows), jnp.bfloat16),
                pltpu.VMEM((AROWS, aq.shape[1]), jnp.bfloat16),
                pltpu.VMEM((3,) + narrow, jnp.bfloat16),
                pltpu.SemaphoreType.DMA((47,)),
            ],
        ),
        compiler_params=pltpu.CompilerParams(vmem_limit_bytes=60 * MIB),
        name="pack",
    )(place, k, v, q, ak, av, aq, w)


def ctx_towers(pairs):
    return [(c * TOWERS + s, c * TOWERS + d) for c, s, d in pairs]


def send_main(value, step):
    pairs = [(c, c // 4, (c // 4 + step) % TOWERS) for c in range(16)]
    return lax.ppermute(value, ("ctx", "tower"), ctx_towers(pairs))


def send_halo(value, step):
    pairs = []
    for c in range(16):
        source = c // 4 - 1 if c % 4 == 0 else c // 4 + 1
        if c % 4 in (0, 3) and 0 <= source < TOWERS:
            pairs.append((c, source, (source + step) % TOWERS))
    return lax.ppermute(value, ("ctx", "tower"), ctx_towers(pairs))


def keys_of(kv_ref):
    return jnp.concatenate([kv_ref[r, 0, 0] for r in range(TOWERS)], axis=1)


def rows_of(kv_ref, which):
    return jnp.concatenate([kv_ref[r, which, 0] for r in range(TOWERS)], axis=0)


def lane_tiles(x):
    return [x[:, i : i + HD] for i in range(0, x.shape[1], HD)]


def flash_kernel(kv_count, first, last, after, *refs):
    q_ref = refs[0]
    kv_refs = refs[1 : 1 + kv_count]
    rest = refs[1 + kv_count :]
    rest = rest[: len(rest) - (1 if last else 4) - after] + rest[len(rest) - (1 if last else 4) :]
    if first:
        outs = rest
    else:
        acc_in, top_in, total_in = rest[:3]
        outs = rest[3:]
    size = 2 * VBLK
    tiles = [slice(i * size, (i + 1) * size) for i in range(2)]
    query = rows_of(q_ref, 0)
    keys = [keys_of(kv) for kv in kv_refs]
    all_scores = [[nn_dot(query[rows], k) for k in keys] for rows in tiles]
    for rows, scores in zip(tiles, all_scores):
        top = functools.reduce(jnp.maximum, [t for s in scores for t in lane_tiles(s)])
        top = jnp.max(top, axis=1, keepdims=True) * SCALE2
        if first:
            top = jnp.broadcast_to(top, (size, HD))
            acc = total = None
        else:
            top = jnp.maximum(top, top_in[rows])
            factor = jnp.exp2(top_in[rows] - top)
            acc = acc_in[rows] * factor
            total = total_in[rows] * factor
        wide = jnp.concatenate([top] * TOWERS, axis=1)
        for s, kv in zip(scores, kv_refs):
            weights = jnp.exp2(s * SCALE2 - wide)
            part = functools.reduce(jnp.add, lane_tiles(weights))
            total = part if total is None else total + part
            part = nn_dot(weights.astype(jnp.bfloat16), rows_of(kv, 1))
            acc = part if acc is None else acc + part
        if last:
            outs[0][rows] = (acc / jnp.sum(total, axis=1, keepdims=True)).astype(jnp.bfloat16)
        else:
            outs[0][rows] = acc
            outs[1][rows] = top
            outs[2][rows] = total
            outs[3][...] = total[:8]


QUERY = pl.BlockSpec((TOWERS, 1, 1, VBLK, HD), lambda h, *_: (0, 2, h, 0, 0))
SHARD = pl.BlockSpec((TOWERS, 2, 1, VBLK, HD), lambda h, *_: (0, 0, h, 0, 0))


def flash(query, kvs, state, last, after=()):
    rows = TOWERS * VBLK
    keys = rows * len(kvs)
    wide = jax.ShapeDtypeStruct((rows, GW), jnp.float32)
    head = pl.BlockSpec((rows, HD), lambda h: (0, h))
    if last:
        out_shape = jax.ShapeDtypeStruct((rows, GW), jnp.bfloat16)
        out_specs = head
    else:
        out_shape = [wide, wide, wide, jax.ShapeDtypeStruct((8, HD), jnp.float32)]
        out_specs = [head, head, head, pl.BlockSpec((8, HD), lambda h: (0, 0))]
    return pl.pallas_call(
        functools.partial(flash_kernel, len(kvs), state is None, last, len(after)),
        out_shape=out_shape,
        grid=(LOCAL,),
        in_specs=[QUERY] + [SHARD] * len(kvs) + ([] if state is None else [head] * 3) + [ANY] * len(after),
        out_specs=out_specs,
        compiler_params=pltpu.CompilerParams(vmem_limit_bytes=(32 if last else 60) * MIB),
        cost_estimate=BRIEF,
        name="flash",
    )(query, *kvs, *(() if state is None else state), *after)


AUDIO_ROWS = 32
BOTH = VBLK + AUDIO_ROWS


def weighted(scores, values):
    weights = jnp.exp2(scores - jnp.max(scores, axis=1, keepdims=True)).astype(jnp.bfloat16)
    result = nn_dot(weights, jnp.concatenate([values, jnp.ones_like(values)], axis=1))
    return result[:, :HD] / result[:, HD:]


def audio_rows(place, margin, main, own, sibling, third):
    ctx = place[0]
    core = lax.rem(ctx, 2)
    row_block = lax.broadcasted_iota(jnp.int32, (QROWS, 1), 0) // ABLK + ctx * 4
    query = main[QAT:]
    pieces = [(own, r, ctx * 4 + r) for r in range(TOWERS)]
    after = lax.rem(ctx + 1, 16) * 4
    before = lax.rem(ctx + 15, 16) * 4 + 2
    for r in range(2):
        pieces.append((sibling, 2 * core + r, jnp.where(core == 0, after, before) + r))
        pieces.append((third, 2 - 2 * core + r, jnp.where(core == 0, before, after) + r))
    keys = jnp.concatenate([ref[r, 0, 0] for ref, r, _ in pieces], axis=1)
    values = jnp.concatenate([ref[r, 1, 0] for ref, r, _ in pieces], axis=0)
    raw = nn_dot(query, keys) * SCALE2
    scores = []
    for i, (_, _, block) in enumerate(pieces):
        hit = (
            (row_block == margin[block, 0])
            | (row_block == margin[block, 1])
            | (row_block == margin[block, 2])
        )
        scores.append(jnp.where(hit, raw[:, i * VBLK : (i + 1) * VBLK], NEG))
    scores = jnp.concatenate(scores, axis=1)
    return weighted(scores, values)


def cross_kernel(place, margin, q_ref, *refs):
    mains, halos, (own, sibling, third, out) = refs[:4], refs[4:8], refs[8:]
    main = functools.reduce(
        jnp.add, [ref[...] for ref in mains[1:]], jnp.where(place[1] == place[2], mains[0][...], 0)
    )
    halo = functools.reduce(
        jnp.add, [ref[...] for ref in halos[1:]], jnp.where(place[1] == place[3], halos[0][...], 0)
    )
    ctx = place[0]
    phase = lax.rem(ctx, 4)
    base = (ctx - phase) * 4
    lane = lax.broadcasted_iota(jnp.int32, (1, 256), 1)
    halo_base = jnp.where(phase == 0, base - 2, jnp.where(phase == 3, base + 16, -100))
    main_base = base + lax.div(main_first(ctx), ABLK)
    ids = jnp.where(lane < WIN, lane // ABLK + main_base, lane // ABLK - WIN // ABLK + halo_base)
    ids = jnp.where(lane < WIN + HALO, ids, -100)
    spare = jnp.zeros((256 - WIN - HALO, HD), jnp.bfloat16)
    keys = jnp.concatenate([main[:WIN], halo[:HALO], spare], axis=0)
    values = jnp.concatenate(
        [main[WIN:QAT], halo[HALO:], spare], axis=0
    )
    scores = nt_dot(rows_of(q_ref, 0), keys) * SCALE2
    parts = []
    for r in range(TOWERS):
        block = ctx * 4 + r
        hit = (ids == margin[block, 0]) | (ids == margin[block, 1]) | (ids == margin[block, 2])
        parts.append(jnp.where(hit, scores[r * VBLK : (r + 1) * VBLK], NEG))
    scores = jnp.concatenate(parts, axis=0)
    result = weighted(scores, values).astype(jnp.bfloat16)
    mixed = audio_rows(place, margin, main, own, sibling, third)
    for r in range(TOWERS):
        out[r, pl.ds(0, VBLK), :] = result[r * VBLK : (r + 1) * VBLK]
        padded = jnp.concatenate(
            [mixed[r * ABLK : (r + 1) * ABLK], jnp.zeros((AUDIO_ROWS - ABLK, HD), jnp.float32)], axis=0
        )
        out[r, pl.ds(VBLK, AUDIO_ROWS), :] = padded.astype(jnp.bfloat16)


def cross(place, margin, query, mains, halos, own, sibling, third):
    rows = TOWERS * VBLK
    return pl.pallas_call(
        cross_kernel,
        out_shape=jax.ShapeDtypeStruct((TOWERS, BOTH, GW), jnp.bfloat16),
        grid_spec=pltpu.PrefetchScalarGridSpec(
            num_scalar_prefetch=2,
            grid=(LOCAL,),
            in_specs=[
                QUERY,
            ]
            + [pl.BlockSpec((HAT, HD), lambda h, *_: (0, h))] * TOWERS
            + [pl.BlockSpec((2 * HALO, HD), lambda h, *_: (0, h))] * TOWERS
            + [SHARD] * 3,
            out_specs=pl.BlockSpec((TOWERS, BOTH, HD), lambda h, *_: (0, 0, h)),
        ),
        compiler_params=pltpu.CompilerParams(vmem_limit_bytes=60 * MIB),
        cost_estimate=BRIEF,
        name="cross",
    )(place, margin, query, *mains, *halos, own, sibling, third)


def weight_rows(pieces):
    return jnp.concatenate([piece(h) for h in range(LOCAL) for piece in pieces], axis=0)


def project_cross_kernel(place, own, sibling, w_ref, _, __, mine, up, down, up_later, down_later):
    towers = [lax.rem(place[1] + step, TOWERS) for step in range(TOWERS)]
    targets = (
        (mine, 0),
        (mine, BOTH),
        (up_later, 0),
        (up, BOTH),
        (up, 0),
        (down, BOTH),
        (down, 0),
        (down_later, 0),
    )
    ws = [
        weight_rows([functools.partial(lambda b, h: w_ref[b, kind, h], b) for b in range(4)])
        for kind in range(2)
    ]
    for step in range(TOWERS):
        for w, (first, count) in zip(ws, ((0, VBLK), (VBLK, AUDIO_ROWS))):
            both = [ref[towers[step], pl.ds(first, count), :] for ref in (own, sibling)]
            y = nn_dot(jnp.concatenate(both, axis=0), w).astype(jnp.bfloat16)
            for i in range(2):
                out, at = targets[2 * step + i]
                out[pl.ds(at + first, count), :] = y[i * count : (i + 1) * count]


def project_cross(place, own, sibling, w, after):
    width = w.shape[-1]
    tile = width // 3
    return pl.pallas_call(
        project_cross_kernel,
        out_shape=[jax.ShapeDtypeStruct((n * BOTH, width), jnp.bfloat16) for n in (2, 2, 2, 1, 1)],
        grid_spec=pltpu.PrefetchScalarGridSpec(
            num_scalar_prefetch=1,
            grid=(3,),
            in_specs=[
                full(own.shape),
                full(own.shape),
                pl.BlockSpec(w.shape[:-1] + (tile,), lambda i, place: (0, 0, 0, 0, i)),
                ANY,
                ANY,
            ],
            out_specs=[
                pl.BlockSpec((n * BOTH, tile), lambda i, place: (0, i)) for n in (2, 2, 2, 1, 1)
            ],
        ),
        compiler_params=pltpu.CompilerParams(vmem_limit_bytes=60 * MIB),
        cost_estimate=BRIEF,
        name="project_cross",
    )(place, own, sibling, w, *after)


def project_self_kernel(place, own, sibling, w_ref, *refs):
    mine, up, down, up_later, down_later, gain, video_out, audio_out, sibling_out = refs
    a = jnp.concatenate(
        [jnp.concatenate([ref[t] for t in range(TOWERS)], axis=1) for ref in (own, sibling)], axis=0
    )
    w = jnp.concatenate(
        [
            weight_rows([functools.partial(lambda b, h: w_ref[b * TOWERS + t, h], b) for b in range(4)])
            for t in range(TOWERS)
        ],
        axis=0,
    )
    acc = nn_dot(a, w)
    top = [mine[pl.ds(0, BOTH), :], down[pl.ds(0, BOTH), :], up_later[...]]
    bottom = [mine[pl.ds(BOTH, BOTH), :], up[pl.ds(BOTH, BOTH), :], down_later[...]]
    base = jnp.concatenate(
        [functools.reduce(jnp.add, [x.astype(jnp.float32) for x in xs]) for xs in (top, bottom)], axis=0
    )
    video, audio = [], []
    for i in range(2):
        video.append(gain[0:1] * (acc[i * VBLK : (i + 1) * VBLK] + base[i * BOTH : i * BOTH + VBLK]))
        audio.append(gain[1:2] * base[i * BOTH + VBLK : (i + 1) * BOTH])
    video_out[...] = video[0].astype(jnp.bfloat16)
    audio_out[...] = audio[0][:ABLK].astype(jnp.bfloat16)
    sibling_out[pl.ds(0, VBLK), :] = video[1].astype(jnp.bfloat16)
    sibling_out[pl.ds(VBLK, AUDIO_ROWS), :] = audio[1].astype(jnp.bfloat16)


def project_self(place, own, sibling, w, base, gains):
    width = w.shape[-1]
    tile = width // 3
    out = lambda rows: pl.BlockSpec((rows, tile), lambda i, place: (0, place[4] * 3 + i))
    return pl.pallas_call(
        project_self_kernel,
        out_shape=[
            jax.ShapeDtypeStruct((VBLK, 2 * width), jnp.bfloat16),
            jax.ShapeDtypeStruct((ABLK, 2 * width), jnp.bfloat16),
            jax.ShapeDtypeStruct((BOTH, width), jnp.bfloat16),
        ],
        grid_spec=pltpu.PrefetchScalarGridSpec(
            num_scalar_prefetch=1,
            grid=(3,),
            in_specs=[
                full(own.shape),
                full(own.shape),
                pl.BlockSpec(w.shape[:-1] + (tile,), lambda i, place: (0, 0, 0, i)),
            ]
            + [pl.BlockSpec((n * BOTH, tile), lambda i, place: (0, i)) for n in (2, 2, 2, 1, 1)]
            + [pl.BlockSpec((2, tile), lambda i, place: (0, place[4] * 3 + i))],
            out_specs=[out(VBLK), out(ABLK), pl.BlockSpec((BOTH, tile), lambda i, place: (0, i))],
        ),
        compiler_params=pltpu.CompilerParams(vmem_limit_bytes=24 * MIB),
        cost_estimate=BRIEF,
        name="project_self",
    )(place, own, sibling, w, *base, gains)


def assemble_kernel(place, video_in, audio_in, theirs, video, audio):
    video[...] = theirs[pl.ds(0, VBLK), :]
    audio[...] = theirs[pl.ds(VBLK, AUDIO_ROWS), :].astype(jnp.float32)[:ABLK].astype(jnp.bfloat16)


def assemble(place, video, audio, theirs):
    width = theirs.shape[1]

    def column(i, place):
        return (0, 1 - place[4])

    return pl.pallas_call(
        assemble_kernel,
        out_shape=[jax.ShapeDtypeStruct(x.shape, x.dtype) for x in (video, audio)],
        grid_spec=pltpu.PrefetchScalarGridSpec(
            num_scalar_prefetch=1,
            grid=(1,),
            in_specs=[ANY, ANY, full(theirs.shape)],
            out_specs=[pl.BlockSpec((VBLK, width), column), pl.BlockSpec((ABLK, width), column)],
        ),
        input_output_aliases={1: 0, 2: 1},
        compiler_params=pltpu.CompilerParams(vmem_limit_bytes=16 * MIB),
        name="assemble",
    )(place, video, audio, theirs)


def gate_kernel(*refs):
    pass


def gate(value, *after):
    return pl.pallas_call(
        gate_kernel,
        out_shape=jax.ShapeDtypeStruct(value.shape, value.dtype),
        in_specs=[ANY] * (1 + len(after)),
        out_specs=ANY,
        input_output_aliases={0: 0},
        compiler_params=pltpu.CompilerParams(vmem_limit_bytes=60 * MIB),
        name="gate",
    )(value, *after)


def exchange_towers(value):
    return lax.all_to_all(value, "tower", split_axis=0, concat_axis=0, tiled=True)


def add_later_kernel(up, down, up_later, down_later, _, up_out, down_out):
    for a, b, out in ((up, up_later, up_out), (down, down_later, down_out)):
        out[...] = (a[...].astype(jnp.float32) + b[...].astype(jnp.float32)).astype(jnp.bfloat16)


def add_later(up, down, up_later, down_later, after):
    rows, width = up_later.shape
    tile = width // 3
    first = pl.BlockSpec((rows, tile), lambda i: (0, i))
    second = pl.BlockSpec((rows, tile), lambda i: (1, i))
    return pl.pallas_call(
        add_later_kernel,
        out_shape=[jax.ShapeDtypeStruct(up_later.shape, up_later.dtype)] * 2,
        grid=(3,),
        in_specs=[first, second, first, first, ANY],
        out_specs=[first, first],
        compiler_params=pltpu.CompilerParams(vmem_limit_bytes=24 * MIB),
        cost_estimate=BRIEF,
        name="add_later",
    )(up, down, up_later, down_later, after)


def shift_tower(value, step):
    return lax.ppermute(value, "tower", [(i, (i + step) % TOWERS) for i in range(TOWERS)])


def hop(value):
    total = 2 * CHIPS
    return lax.ppermute(value, "ctx", [(i, (i + 2 - 4 * (i % 2)) % total) for i in range(total)])


def swap_core(value):
    return lax.ppermute(value, "ctx", [(i, i ^ 1) for i in range(2 * CHIPS)])


def shards(video_q, video_k, video_v, audio_q, audio_k, audio_v, margin, out_weight, gate_gains):
    ctx = lax.axis_index("ctx")
    tower = lax.axis_index("tower")
    core = lax.rem(ctx, 2)
    place = jnp.stack([ctx, tower, ctx // 4, edge_tower(ctx), core]).astype(jnp.int32)
    gains = gate_gains[0]
    margins = margin[0]

    parts, w_self, w_rest, *audio = pack(
        place, video_k[0], video_v[0], video_q[0], audio_k[0], audio_v[0], audio_q[0], out_weight
    )
    w_rest = lax.all_gather(w_rest, "batch", axis=0, tiled=False)
    w_self = lax.all_gather(w_self, ("batch", "tower"), axis=0, tiled=False)
    query = exchange_towers(parts)
    own = query[:, :2]
    sibling = swap_core(own)
    near, far = hop(own), hop(sibling)
    audio = [gate(rows, sibling) for rows in audio]
    mains = [audio[0]] + [send_main(audio[step], step) for step in (1, 2, 3)]
    halos = [audio[4]] + [send_halo(audio[4 + step], step) for step in (1, 2, 3)]

    acc, top, total, token = flash(query, [own, sibling], None, False)
    near, far = gate(near, token, *mains[1:], *halos[1:]), gate(far, token)
    crossed = cross(place, margins, query, mains, halos, own, sibling, far)

    tokens = [token]
    after = (crossed,)
    for step in range(1, 4):
        now = [near, far, swap_core(near), swap_core(far)]
        near, far = hop(near), (hop(far) if step < 3 else None)
        acc, top, total, token = flash(query, now, (acc, top, total), False, after)
        tokens.append(token)
        after = ()
        if step == 1:
            rest, up, down, up_later, down_later = project_cross(
                place, crossed, swap_core(crossed), w_rest, (token, token)
            )
            after = (rest,)
            up, down = shift_tower(up, 1), shift_tower(down, -1)
        behind = crossed if step == 1 else tokens[step - 1]
        near = gate(near, behind)
        if step < 3:
            far = gate(far, behind)
    video_self = flash(query, [near, swap_core(near)], (acc, top, total), True, (w_self,))
    up_later, down_later = add_later(up, down, up_later, down_later, video_self)
    up_later, down_later = shift_tower(up_later, 1), shift_tower(down_later, -1)
    base = (rest, up, down, up_later, down_later)

    self_all = exchange_towers(video_self.reshape(TOWERS, VBLK, GW))
    video_out, audio_out, theirs = project_self(place, self_all, swap_core(self_all), w_self, base, gains)
    video_out, audio_out = assemble(place, video_out, audio_out, swap_core(theirs))
    return (video_out[None], audio_out[None])


def solution(mesh):
    return jax.shard_map(
        shards,
        mesh=mesh,
        in_specs=(
            P("batch", ("ctx", "tower"), None),
            P("batch", ("ctx", "tower"), None),
            P("batch", ("ctx", "tower"), None),
            P("batch", "tower", None),
            P("batch", "tower", None),
            P("batch", "tower", None),
            P("batch", None, None),
            P(None, "tower", "batch", None),
            P("batch", None, None),
        ),
        out_specs=(P("batch", ("ctx", "tower"), None), P("batch", ("ctx", "tower"), None)),
        check_vma=False,
    )
```

```python
import functools

import jax
import jax.numpy as jnp
from jax import lax
from jax.experimental import pallas as pl
from jax.experimental.pallas import tpu as pltpu
from jax.sharding import PartitionSpec as P

H = 12
HD = 128
VBLK = 128
ABLK = 24
TOWERS = 4
CHIPS = 8
LOCAL = H // TOWERS
GW = LOCAL * HD
NEG = -1e30
SCALE2 = HD**-0.5 * 1.4426950408889634
MIB = 1024 * 1024


def nt_dot(a, b):
    return lax.dot_general(a, b, (((1,), (1,)), ((), ())), preferred_element_type=jnp.float32)


def nn_dot(a, b):
    return jnp.dot(a, b, preferred_element_type=jnp.float32)


def full(shape):
    return pl.BlockSpec(shape, lambda *_: (0,) * len(shape))


BRIEF = pl.CostEstimate(flops=1, bytes_accessed=1, transcendentals=0)
ANY = pl.BlockSpec(memory_space=pl.ANY)


def start_copies(pairs, sem, first):
    copies = [pltpu.make_async_copy(a, b, sem.at[first + i]) for i, (a, b) in enumerate(pairs)]
    for copy in copies:
        copy.start()
    return copies


WIN = 192
HALO = 48
QROWS = 96
QAT = 2 * WIN
HAT = QAT + QROWS
AROWS = HAT + 2 * HALO


def main_first(ctx):
    return jnp.clip(lax.rem(ctx, 4) * QROWS - HALO, 0, 384 - WIN)


def edge_tower(ctx):
    phase = lax.rem(ctx, 4)
    edge = jnp.where(phase == 0, ctx // 4 - 1, ctx // 4 + 1)
    return jnp.where(((phase == 0) | (phase == 3)) & (edge >= 0) & (edge < TOWERS), edge, -1)


def pack_kernel(
    place, k_ref, v_ref, q_ref, ak_ref, av_ref, aq_ref, w_ref,
    out, self_out, rest_out, main0, main1, main2, main3, halo0, halo1, halo2, halo3,
    rows, turned, audio, w_rows, sem,
):
    ctx, tower = place[0], place[1]
    phase = lax.rem(ctx, 4)
    main = pl.ds(pl.multiple_of(main_first(ctx), 16), WIN)
    mine = pl.ds(pl.multiple_of(phase * QROWS, 16), QROWS)
    halo = pl.ds(pl.multiple_of(jnp.where(phase == 0, 384 - HALO, 0), 16), HALO)
    half = w_ref.shape[3] // 2
    columns = pl.ds(pl.multiple_of(place[4] * half, 128), half)
    coming = start_copies([(ref, rows.at[i]) for i, ref in enumerate((k_ref, v_ref, q_ref))], sem, 0)
    coming_w = start_copies([(w_ref.at[:, :, :, columns], w_rows)], sem, 3)
    coming_audio = start_copies(
        [
            (ak_ref.at[main], audio.at[pl.ds(0, WIN)]),
            (av_ref.at[main], audio.at[pl.ds(WIN, WIN)]),
            (aq_ref.at[mine], audio.at[pl.ds(QAT, QROWS)]),
            (ak_ref.at[halo], audio.at[pl.ds(HAT, HALO)]),
            (av_ref.at[halo], audio.at[pl.ds(HAT + HALO, HALO)]),
        ],
        sem,
        4,
    )
    heads = [(g, h) for g in range(TOWERS) for h in range(LOCAL)]
    going = []
    for i in (1, 2):
        coming[i].wait()
        pairs = [
            (rows.at[i, :, pl.ds((g * LOCAL + h) * HD, HD)], out.at[g, i, h]) for g, h in heads
        ]
        going += start_copies(pairs, sem, 9 + (i - 1) * H)
    coming[0].wait()
    for g, h in heads:
        block = rows[0, :, pl.ds((g * LOCAL + h) * HD, HD)]
        turned[g, h] = block.astype(jnp.float32).T.astype(jnp.bfloat16)
    going += start_copies([(turned.at[g], out.at[g, 0]) for g in range(TOWERS)], sem, 33)
    coming_w[0].wait()
    going += start_copies([(w_rows.at[0], self_out), (w_rows.at[pl.ds(1, 2)], rest_out)], sem, 37)
    for copy in coming_audio:
        copy.wait()
    pairs = []
    for step, (main_out, halo_out) in enumerate(
        ((main0, halo0), (main1, halo1), (main2, halo2), (main3, halo3))
    ):
        group = pl.ds(pl.multiple_of(lax.rem(tower + step, TOWERS) * GW, 128), GW)
        pairs.append((audio.at[pl.ds(0, HAT), group], main_out))
        pairs.append((audio.at[pl.ds(HAT, 2 * HALO), group], halo_out))
    going += start_copies(pairs, sem, 39)
    for copy in going:
        copy.wait()


def pack(place, k, v, q, ak, av, aq, w):
    rows = k.shape[0]
    narrow = (LOCAL, w.shape[2], w.shape[3] // 2)
    shapes = [(TOWERS, 3, LOCAL, rows, HD), narrow, (2,) + narrow]
    shapes += [(HAT, GW)] * TOWERS + [(2 * HALO, GW)] * TOWERS
    return pl.pallas_call(
        pack_kernel,
        out_shape=[jax.ShapeDtypeStruct(shape, jnp.bfloat16) for shape in shapes],
        grid_spec=pltpu.PrefetchScalarGridSpec(
            num_scalar_prefetch=1,
            grid=(1,),
            in_specs=[ANY] * 7,
            out_specs=[ANY] * len(shapes),
            scratch_shapes=[
                pltpu.VMEM((3,) + k.shape, jnp.bfloat16),
                pltpu.VMEM((TOWERS, LOCAL, HD, rows), jnp.bfloat16),
                pltpu.VMEM((AROWS, aq.shape[1]), jnp.bfloat16),
                pltpu.VMEM((3,) + narrow, jnp.bfloat16),
                pltpu.SemaphoreType.DMA((47,)),
            ],
        ),
        compiler_params=pltpu.CompilerParams(vmem_limit_bytes=60 * MIB),
        name="pack",
    )(place, k, v, q, ak, av, aq, w)


def ctx_towers(pairs):
    return [(c * TOWERS + s, c * TOWERS + d) for c, s, d in pairs]


def send_main(value, step):
    pairs = [(c, c // 4, (c // 4 + step) % TOWERS) for c in range(16)]
    return lax.ppermute(value, ("ctx", "tower"), ctx_towers(pairs))


def send_halo(value, step):
    pairs = []
    for c in range(16):
        source = c // 4 - 1 if c % 4 == 0 else c // 4 + 1
        if c % 4 in (0, 3) and 0 <= source < TOWERS:
            pairs.append((c, source, (source + step) % TOWERS))
    return lax.ppermute(value, ("ctx", "tower"), ctx_towers(pairs))


def keys_of(kv_ref):
    return jnp.concatenate([kv_ref[r, 0, 0] for r in range(TOWERS)], axis=1)


def rows_of(kv_ref, which):
    return jnp.concatenate([kv_ref[r, which, 0] for r in range(TOWERS)], axis=0)


def lane_tiles(x):
    return [x[:, i : i + HD] for i in range(0, x.shape[1], HD)]


def flash_kernel(kv_count, first, last, after, *refs):
    q_ref = refs[0]
    kv_refs = refs[1 : 1 + kv_count]
    rest = refs[1 + kv_count :]
    rest = rest[: len(rest) - (1 if last else 4) - after] + rest[len(rest) - (1 if last else 4) :]
    if first:
        outs = rest
    else:
        acc_in, top_in, total_in = rest[:3]
        outs = rest[3:]
    size = 2 * VBLK
    tiles = [slice(i * size, (i + 1) * size) for i in range(2)]
    query = rows_of(q_ref, 0)
    keys = [keys_of(kv) for kv in kv_refs]
    all_scores = [[nn_dot(query[rows], k) for k in keys] for rows in tiles]
    for rows, scores in zip(tiles, all_scores):
        top = functools.reduce(jnp.maximum, [t for s in scores for t in lane_tiles(s)])
        top = jnp.max(top, axis=1, keepdims=True) * SCALE2
        if first:
            top = jnp.broadcast_to(top, (size, HD))
            acc = total = None
        else:
            top = jnp.maximum(top, top_in[rows])
            factor = jnp.exp2(top_in[rows] - top)
            acc = acc_in[rows] * factor
            total = total_in[rows] * factor
        wide = jnp.concatenate([top] * TOWERS, axis=1)
        for s, kv in zip(scores, kv_refs):
            weights = jnp.exp2(s * SCALE2 - wide)
            part = functools.reduce(jnp.add, lane_tiles(weights))
            total = part if total is None else total + part
            part = nn_dot(weights.astype(jnp.bfloat16), rows_of(kv, 1))
            acc = part if acc is None else acc + part
        if last:
            outs[0][rows] = (acc / jnp.sum(total, axis=1, keepdims=True)).astype(jnp.bfloat16)
        else:
            outs[0][rows] = acc
            outs[1][rows] = top
            outs[2][rows] = total
            outs[3][...] = total[:8]


QUERY = pl.BlockSpec((TOWERS, 1, 1, VBLK, HD), lambda h, *_: (0, 2, h, 0, 0))
SHARD = pl.BlockSpec((TOWERS, 2, 1, VBLK, HD), lambda h, *_: (0, 0, h, 0, 0))


def flash(query, kvs, state, last, after=()):
    rows = TOWERS * VBLK
    keys = rows * len(kvs)
    wide = jax.ShapeDtypeStruct((rows, GW), jnp.float32)
    head = pl.BlockSpec((rows, HD), lambda h: (0, h))
    if last:
        out_shape = jax.ShapeDtypeStruct((rows, GW), jnp.bfloat16)
        out_specs = head
    else:
        out_shape = [wide, wide, wide, jax.ShapeDtypeStruct((8, HD), jnp.float32)]
        out_specs = [head, head, head, pl.BlockSpec((8, HD), lambda h: (0, 0))]
    return pl.pallas_call(
        functools.partial(flash_kernel, len(kvs), state is None, last, len(after)),
        out_shape=out_shape,
        grid=(LOCAL,),
        in_specs=[QUERY] + [SHARD] * len(kvs) + ([] if state is None else [head] * 3) + [ANY] * len(after),
        out_specs=out_specs,
        compiler_params=pltpu.CompilerParams(vmem_limit_bytes=60 * MIB),
        cost_estimate=BRIEF,
        name="flash",
    )(query, *kvs, *(() if state is None else state), *after)


AUDIO_ROWS = 32
BOTH = VBLK + AUDIO_ROWS


def weighted(scores, values):
    weights = jnp.exp2(scores - jnp.max(scores, axis=1, keepdims=True)).astype(jnp.bfloat16)
    result = nn_dot(weights, jnp.concatenate([values, jnp.ones_like(values)], axis=1))
    return result[:, :HD] / result[:, HD:]


def audio_rows(place, margin, main, own, sibling, third):
    ctx = place[0]
    core = lax.rem(ctx, 2)
    row_block = lax.broadcasted_iota(jnp.int32, (QROWS, 1), 0) // ABLK + ctx * 4
    query = main[QAT:]
    pieces = [(own, r, ctx * 4 + r) for r in range(TOWERS)]
    after = lax.rem(ctx + 1, 16) * 4
    before = lax.rem(ctx + 15, 16) * 4 + 2
    for r in range(2):
        pieces.append((sibling, 2 * core + r, jnp.where(core == 0, after, before) + r))
        pieces.append((third, 2 - 2 * core + r, jnp.where(core == 0, before, after) + r))
    keys = jnp.concatenate([ref[r, 0, 0] for ref, r, _ in pieces], axis=1)
    values = jnp.concatenate([ref[r, 1, 0] for ref, r, _ in pieces], axis=0)
    raw = nn_dot(query, keys) * SCALE2
    scores = []
    for i, (_, _, block) in enumerate(pieces):
        hit = (
            (row_block == margin[block, 0])
            | (row_block == margin[block, 1])
            | (row_block == margin[block, 2])
        )
        scores.append(jnp.where(hit, raw[:, i * VBLK : (i + 1) * VBLK], NEG))
    scores = jnp.concatenate(scores, axis=1)
    return weighted(scores, values)


def cross_kernel(place, margin, q_ref, *refs):
    mains, halos, (own, sibling, third, out) = refs[:4], refs[4:8], refs[8:]
    main = functools.reduce(
        jnp.add, [ref[...] for ref in mains[1:]], jnp.where(place[1] == place[2], mains[0][...], 0)
    )
    halo = functools.reduce(
        jnp.add, [ref[...] for ref in halos[1:]], jnp.where(place[1] == place[3], halos[0][...], 0)
    )
    ctx = place[0]
    phase = lax.rem(ctx, 4)
    base = (ctx - phase) * 4
    lane = lax.broadcasted_iota(jnp.int32, (1, 256), 1)
    halo_base = jnp.where(phase == 0, base - 2, jnp.where(phase == 3, base + 16, -100))
    main_base = base + lax.div(main_first(ctx), ABLK)
    ids = jnp.where(lane < WIN, lane // ABLK + main_base, lane // ABLK - WIN // ABLK + halo_base)
    ids = jnp.where(lane < WIN + HALO, ids, -100)
    spare = jnp.zeros((256 - WIN - HALO, HD), jnp.bfloat16)
    keys = jnp.concatenate([main[:WIN], halo[:HALO], spare], axis=0)
    values = jnp.concatenate(
        [main[WIN:QAT], halo[HALO:], spare], axis=0
    )
    scores = nt_dot(rows_of(q_ref, 0), keys) * SCALE2
    parts = []
    for r in range(TOWERS):
        block = ctx * 4 + r
        hit = (ids == margin[block, 0]) | (ids == margin[block, 1]) | (ids == margin[block, 2])
        parts.append(jnp.where(hit, scores[r * VBLK : (r + 1) * VBLK], NEG))
    scores = jnp.concatenate(parts, axis=0)
    result = weighted(scores, values).astype(jnp.bfloat16)
    mixed = audio_rows(place, margin, main, own, sibling, third)
    for r in range(TOWERS):
        out[r, pl.ds(0, VBLK), :] = result[r * VBLK : (r + 1) * VBLK]
        padded = jnp.concatenate(
            [mixed[r * ABLK : (r + 1) * ABLK], jnp.zeros((AUDIO_ROWS - ABLK, HD), jnp.float32)], axis=0
        )
        out[r, pl.ds(VBLK, AUDIO_ROWS), :] = padded.astype(jnp.bfloat16)


def cross(place, margin, query, mains, halos, own, sibling, third):
    rows = TOWERS * VBLK
    return pl.pallas_call(
        cross_kernel,
        out_shape=jax.ShapeDtypeStruct((TOWERS, BOTH, GW), jnp.bfloat16),
        grid_spec=pltpu.PrefetchScalarGridSpec(
            num_scalar_prefetch=2,
            grid=(LOCAL,),
            in_specs=[
                QUERY,
            ]
            + [pl.BlockSpec((HAT, HD), lambda h, *_: (0, h))] * TOWERS
            + [pl.BlockSpec((2 * HALO, HD), lambda h, *_: (0, h))] * TOWERS
            + [SHARD] * 3,
            out_specs=pl.BlockSpec((TOWERS, BOTH, HD), lambda h, *_: (0, 0, h)),
        ),
        compiler_params=pltpu.CompilerParams(vmem_limit_bytes=60 * MIB),
        cost_estimate=BRIEF,
        name="cross",
    )(place, margin, query, *mains, *halos, own, sibling, third)


def weight_rows(pieces):
    return jnp.concatenate([piece(h) for h in range(LOCAL) for piece in pieces], axis=0)


def project_cross_kernel(place, own, sibling, w_ref, _, __, mine, up, down, up_later, down_later):
    towers = [lax.rem(place[1] + step, TOWERS) for step in range(TOWERS)]
    targets = (
        (mine, 0),
        (mine, BOTH),
        (up_later, 0),
        (up, BOTH),
        (up, 0),
        (down, BOTH),
        (down, 0),
        (down_later, 0),
    )
    ws = [
        weight_rows([functools.partial(lambda b, h: w_ref[b, kind, h], b) for b in range(4)])
        for kind in range(2)
    ]
    for step in range(TOWERS):
        for w, (first, count) in zip(ws, ((0, VBLK), (VBLK, AUDIO_ROWS))):
            both = [ref[towers[step], pl.ds(first, count), :] for ref in (own, sibling)]
            y = nn_dot(jnp.concatenate(both, axis=0), w).astype(jnp.bfloat16)
            for i in range(2):
                out, at = targets[2 * step + i]
                out[pl.ds(at + first, count), :] = y[i * count : (i + 1) * count]


def project_cross(place, own, sibling, w, after):
    width = w.shape[-1]
    tile = width // 3
    return pl.pallas_call(
        project_cross_kernel,
        out_shape=[jax.ShapeDtypeStruct((n * BOTH, width), jnp.bfloat16) for n in (2, 2, 2, 1, 1)],
        grid_spec=pltpu.PrefetchScalarGridSpec(
            num_scalar_prefetch=1,
            grid=(3,),
            in_specs=[
                full(own.shape),
                full(own.shape),
                pl.BlockSpec(w.shape[:-1] + (tile,), lambda i, place: (0, 0, 0, 0, i)),
                ANY,
                ANY,
            ],
            out_specs=[
                pl.BlockSpec((n * BOTH, tile), lambda i, place: (0, i)) for n in (2, 2, 2, 1, 1)
            ],
        ),
        compiler_params=pltpu.CompilerParams(vmem_limit_bytes=60 * MIB),
        cost_estimate=BRIEF,
        name="project_cross",
    )(place, own, sibling, w, *after)


def project_self_kernel(place, own, sibling, w_ref, *refs):
    mine, up, down, up_later, down_later, gain, video_out, audio_out, sibling_out = refs
    a = jnp.concatenate(
        [jnp.concatenate([ref[t] for t in range(TOWERS)], axis=1) for ref in (own, sibling)], axis=0
    )
    w = jnp.concatenate(
        [
            weight_rows([functools.partial(lambda b, h: w_ref[b * TOWERS + t, h], b) for b in range(4)])
            for t in range(TOWERS)
        ],
        axis=0,
    )
    acc = nn_dot(a, w)
    top = [mine[pl.ds(0, BOTH), :], down[pl.ds(0, BOTH), :], up_later[...]]
    bottom = [mine[pl.ds(BOTH, BOTH), :], up[pl.ds(BOTH, BOTH), :], down_later[...]]
    base = jnp.concatenate(
        [functools.reduce(jnp.add, [x.astype(jnp.float32) for x in xs]) for xs in (top, bottom)], axis=0
    )
    video, audio = [], []
    for i in range(2):
        video.append(gain[0:1] * (acc[i * VBLK : (i + 1) * VBLK] + base[i * BOTH : i * BOTH + VBLK]))
        audio.append(gain[1:2] * base[i * BOTH + VBLK : (i + 1) * BOTH])
    video_out[...] = video[0].astype(jnp.bfloat16)
    audio_out[...] = audio[0][:ABLK].astype(jnp.bfloat16)
    sibling_out[pl.ds(0, VBLK), :] = video[1].astype(jnp.bfloat16)
    sibling_out[pl.ds(VBLK, AUDIO_ROWS), :] = audio[1].astype(jnp.bfloat16)


def project_self(place, own, sibling, w, base, gains):
    width = w.shape[-1]
    tile = width // 3
    out = lambda rows: pl.BlockSpec((rows, tile), lambda i, place: (0, place[4] * 3 + i))
    return pl.pallas_call(
        project_self_kernel,
        out_shape=[
            jax.ShapeDtypeStruct((VBLK, 2 * width), jnp.bfloat16),
            jax.ShapeDtypeStruct((ABLK, 2 * width), jnp.bfloat16),
            jax.ShapeDtypeStruct((BOTH, width), jnp.bfloat16),
        ],
        grid_spec=pltpu.PrefetchScalarGridSpec(
            num_scalar_prefetch=1,
            grid=(3,),
            in_specs=[
                full(own.shape),
                full(own.shape),
                pl.BlockSpec(w.shape[:-1] + (tile,), lambda i, place: (0, 0, 0, i)),
            ]
            + [pl.BlockSpec((n * BOTH, tile), lambda i, place: (0, i)) for n in (2, 2, 2, 1, 1)]
            + [pl.BlockSpec((2, tile), lambda i, place: (0, place[4] * 3 + i))],
            out_specs=[out(VBLK), out(ABLK), pl.BlockSpec((BOTH, tile), lambda i, place: (0, i))],
        ),
        compiler_params=pltpu.CompilerParams(vmem_limit_bytes=24 * MIB),
        cost_estimate=BRIEF,
        name="project_self",
    )(place, own, sibling, w, *base, gains)


def assemble_kernel(place, video_in, audio_in, theirs, video, audio):
    video[...] = theirs[pl.ds(0, VBLK), :]
    audio[...] = theirs[pl.ds(VBLK, AUDIO_ROWS), :].astype(jnp.float32)[:ABLK].astype(jnp.bfloat16)


def assemble(place, video, audio, theirs):
    width = theirs.shape[1]

    def column(i, place):
        return (0, 1 - place[4])

    return pl.pallas_call(
        assemble_kernel,
        out_shape=[jax.ShapeDtypeStruct(x.shape, x.dtype) for x in (video, audio)],
        grid_spec=pltpu.PrefetchScalarGridSpec(
            num_scalar_prefetch=1,
            grid=(1,),
            in_specs=[ANY, ANY, full(theirs.shape)],
            out_specs=[pl.BlockSpec((VBLK, width), column), pl.BlockSpec((ABLK, width), column)],
        ),
        input_output_aliases={1: 0, 2: 1},
        compiler_params=pltpu.CompilerParams(vmem_limit_bytes=16 * MIB),
        name="assemble",
    )(place, video, audio, theirs)


def gate_kernel(*refs):
    pass


def gate(value, *after):
    return pl.pallas_call(
        gate_kernel,
        out_shape=jax.ShapeDtypeStruct(value.shape, value.dtype),
        in_specs=[ANY] * (1 + len(after)),
        out_specs=ANY,
        input_output_aliases={0: 0},
        compiler_params=pltpu.CompilerParams(vmem_limit_bytes=60 * MIB),
        name="gate",
    )(value, *after)


def exchange_towers(value):
    return lax.all_to_all(value, "tower", split_axis=0, concat_axis=0, tiled=True)


def add_later_kernel(up, down, up_later, down_later, _, up_out, down_out):
    for a, b, out in ((up, up_later, up_out), (down, down_later, down_out)):
        out[...] = (a[...].astype(jnp.float32) + b[...].astype(jnp.float32)).astype(jnp.bfloat16)


def add_later(up, down, up_later, down_later, after):
    rows, width = up_later.shape
    tile = width // 3
    first = pl.BlockSpec((rows, tile), lambda i: (0, i))
    second = pl.BlockSpec((rows, tile), lambda i: (1, i))
    return pl.pallas_call(
        add_later_kernel,
        out_shape=[jax.ShapeDtypeStruct(up_later.shape, up_later.dtype)] * 2,
        grid=(3,),
        in_specs=[first, second, first, first, ANY],
        out_specs=[first, first],
        compiler_params=pltpu.CompilerParams(vmem_limit_bytes=24 * MIB),
        cost_estimate=BRIEF,
        name="add_later",
    )(up, down, up_later, down_later, after)


def shift_tower(value, step):
    return lax.ppermute(value, "tower", [(i, (i + step) % TOWERS) for i in range(TOWERS)])


def hop(value):
    total = 2 * CHIPS
    return lax.ppermute(value, "ctx", [(i, (i + 2 - 4 * (i % 2)) % total) for i in range(total)])


def swap_core(value):
    return lax.ppermute(value, "ctx", [(i, i ^ 1) for i in range(2 * CHIPS)])


def shards(video_q, video_k, video_v, audio_q, audio_k, audio_v, margin, out_weight, gate_gains):
    ctx = lax.axis_index("ctx")
    tower = lax.axis_index("tower")
    core = lax.rem(ctx, 2)
    place = jnp.stack([ctx, tower, ctx // 4, edge_tower(ctx), core]).astype(jnp.int32)
    gains = gate_gains[0]
    margins = margin[0]

    parts, w_self, w_rest, *audio = pack(
        place, video_k[0], video_v[0], video_q[0], audio_k[0], audio_v[0], audio_q[0], out_weight
    )
    w_rest = lax.all_gather(w_rest, "batch", axis=0, tiled=False)
    w_self = lax.all_gather(w_self, ("batch", "tower"), axis=0, tiled=False)
    query = exchange_towers(parts)
    own = query[:, :2]
    sibling = swap_core(own)
    near, far = hop(own), hop(sibling)
    mains = [audio[0]] + [send_main(gate(audio[step], sibling), step) for step in (1, 2, 3)]

    acc, top, total, token = flash(query, [own, sibling], None, False)
    halos = [audio[4]] + [send_halo(gate(audio[4 + step], token), step) for step in (1, 2, 3)]
    near, far = gate(near, token, *mains[1:], *halos[1:]), gate(far, token)
    crossed = cross(place, margins, query, mains, halos, own, sibling, far)

    rest, up, down, up_later, down_later = project_cross(
        place, crossed, swap_core(crossed), w_rest, (token, token)
    )
    up, down = shift_tower(up, 1), shift_tower(down, -1)

    behind = [crossed]
    after = (rest,)
    for step in range(1, 4):
        now = [near, far, swap_core(near), swap_core(far)]
        near, far = hop(near), (hop(far) if step < 3 else None)
        acc, top, total, token = flash(query, now, (acc, top, total), False, after)
        behind.append(token)
        after = ()
        near = gate(near, behind[step - 1])
        if step < 3:
            far = gate(far, behind[step - 1])
    video_self = flash(query, [near, swap_core(near)], (acc, top, total), True)
    up_later, down_later = add_later(up, down, up_later, down_later, video_self)
    up_later, down_later = shift_tower(up_later, 1), shift_tower(down_later, -1)
    base = (rest, up, down, up_later, down_later)

    self_all = exchange_towers(video_self.reshape(TOWERS, VBLK, GW))
    video_out, audio_out, theirs = project_self(place, self_all, swap_core(self_all), w_self, base, gains)
    video_out, audio_out = assemble(place, video_out, audio_out, swap_core(theirs))
    return (video_out[None], audio_out[None])


def solution(mesh):
    return jax.shard_map(
        shards,
        mesh=mesh,
        in_specs=(
            P("batch", ("ctx", "tower"), None),
            P("batch", ("ctx", "tower"), None),
            P("batch", ("ctx", "tower"), None),
            P("batch", "tower", None),
            P("batch", "tower", None),
            P("batch", "tower", None),
            P("batch", None, None),
            P(None, "tower", "batch", None),
            P("batch", None, None),
        ),
        out_specs=(P("batch", ("ctx", "tower"), None), P("batch", ("ctx", "tower"), None)),
        check_vma=False,
    )
```

```python
import functools

import jax
import jax.numpy as jnp
from jax import lax
from jax.experimental import pallas as pl
from jax.experimental.pallas import tpu as pltpu
from jax.sharding import PartitionSpec as P

H = 12
HD = 128
VBLK = 128
ABLK = 24
TOWERS = 4
CHIPS = 8
LOCAL = H // TOWERS
GW = LOCAL * HD
NEG = -1e30
SCALE2 = HD**-0.5 * 1.4426950408889634
MIB = 1024 * 1024


def nt_dot(a, b):
    return lax.dot_general(a, b, (((1,), (1,)), ((), ())), preferred_element_type=jnp.float32)


def nn_dot(a, b):
    return jnp.dot(a, b, preferred_element_type=jnp.float32)


def full(shape):
    return pl.BlockSpec(shape, lambda *_: (0,) * len(shape))


BRIEF = pl.CostEstimate(flops=1, bytes_accessed=1, transcendentals=0)
ANY = pl.BlockSpec(memory_space=pl.ANY)


def start_copies(pairs, sem, first):
    copies = [pltpu.make_async_copy(a, b, sem.at[first + i]) for i, (a, b) in enumerate(pairs)]
    for copy in copies:
        copy.start()
    return copies


WIN = 192
HALO = 48
QROWS = 96
QAT = 2 * WIN
HAT = QAT + QROWS
AROWS = HAT + 2 * HALO


def main_first(ctx):
    return jnp.clip(lax.rem(ctx, 4) * QROWS - HALO, 0, 384 - WIN)


def edge_tower(ctx):
    phase = lax.rem(ctx, 4)
    edge = jnp.where(phase == 0, ctx // 4 - 1, ctx // 4 + 1)
    return jnp.where(((phase == 0) | (phase == 3)) & (edge >= 0) & (edge < TOWERS), edge, -1)


def pack_kernel(
    place, k_ref, v_ref, q_ref, ak_ref, av_ref, aq_ref, w_ref,
    out, self_out, rest_out, main0, main1, main2, main3, halo0, halo1, halo2, halo3,
    rows, turned, audio, w_rows, sem,
):
    ctx, tower = place[0], place[1]
    phase = lax.rem(ctx, 4)
    main = pl.ds(pl.multiple_of(main_first(ctx), 16), WIN)
    mine = pl.ds(pl.multiple_of(phase * QROWS, 16), QROWS)
    halo = pl.ds(pl.multiple_of(jnp.where(phase == 0, 384 - HALO, 0), 16), HALO)
    half = w_ref.shape[3] // 2
    columns = pl.ds(pl.multiple_of(place[4] * half, 128), half)
    coming = start_copies([(ref, rows.at[i]) for i, ref in enumerate((k_ref, v_ref, q_ref))], sem, 0)
    coming_w = start_copies([(w_ref.at[:, :, :, columns], w_rows)], sem, 3)
    coming_audio = start_copies(
        [
            (ak_ref.at[main], audio.at[pl.ds(0, WIN)]),
            (av_ref.at[main], audio.at[pl.ds(WIN, WIN)]),
            (aq_ref.at[mine], audio.at[pl.ds(QAT, QROWS)]),
            (ak_ref.at[halo], audio.at[pl.ds(HAT, HALO)]),
            (av_ref.at[halo], audio.at[pl.ds(HAT + HALO, HALO)]),
        ],
        sem,
        4,
    )
    heads = [(g, h) for g in range(TOWERS) for h in range(LOCAL)]
    going = []
    for i in (1, 2):
        coming[i].wait()
        pairs = [
            (rows.at[i, :, pl.ds((g * LOCAL + h) * HD, HD)], out.at[g, i, h]) for g, h in heads
        ]
        going += start_copies(pairs, sem, 9 + (i - 1) * H)
    coming[0].wait()
    for g, h in heads:
        block = rows[0, :, pl.ds((g * LOCAL + h) * HD, HD)]
        turned[g, h] = block.astype(jnp.float32).T.astype(jnp.bfloat16)
    going += start_copies([(turned.at[g], out.at[g, 0]) for g in range(TOWERS)], sem, 33)
    coming_w[0].wait()
    going += start_copies([(w_rows.at[0], self_out), (w_rows.at[pl.ds(1, 2)], rest_out)], sem, 37)
    for copy in coming_audio:
        copy.wait()
    pairs = []
    for step, (main_out, halo_out) in enumerate(
        ((main0, halo0), (main1, halo1), (main2, halo2), (main3, halo3))
    ):
        group = pl.ds(pl.multiple_of(lax.rem(tower + step, TOWERS) * GW, 128), GW)
        pairs.append((audio.at[pl.ds(0, HAT), group], main_out))
        pairs.append((audio.at[pl.ds(HAT, 2 * HALO), group], halo_out))
    going += start_copies(pairs, sem, 39)
    for copy in going:
        copy.wait()


def pack(place, k, v, q, ak, av, aq, w):
    rows = k.shape[0]
    narrow = (LOCAL, w.shape[2], w.shape[3] // 2)
    shapes = [(TOWERS, 3, LOCAL, rows, HD), narrow, (2,) + narrow]
    shapes += [(HAT, GW)] * TOWERS + [(2 * HALO, GW)] * TOWERS
    return pl.pallas_call(
        pack_kernel,
        out_shape=[jax.ShapeDtypeStruct(shape, jnp.bfloat16) for shape in shapes],
        grid_spec=pltpu.PrefetchScalarGridSpec(
            num_scalar_prefetch=1,
            grid=(1,),
            in_specs=[ANY] * 7,
            out_specs=[ANY] * len(shapes),
            scratch_shapes=[
                pltpu.VMEM((3,) + k.shape, jnp.bfloat16),
                pltpu.VMEM((TOWERS, LOCAL, HD, rows), jnp.bfloat16),
                pltpu.VMEM((AROWS, aq.shape[1]), jnp.bfloat16),
                pltpu.VMEM((3,) + narrow, jnp.bfloat16),
                pltpu.SemaphoreType.DMA((47,)),
            ],
        ),
        compiler_params=pltpu.CompilerParams(vmem_limit_bytes=60 * MIB),
        name="pack",
    )(place, k, v, q, ak, av, aq, w)


def ctx_towers(pairs):
    return [(c * TOWERS + s, c * TOWERS + d) for c, s, d in pairs]


def send_main(value, step):
    pairs = [(c, c // 4, (c // 4 + step) % TOWERS) for c in range(16)]
    return lax.ppermute(value, ("ctx", "tower"), ctx_towers(pairs))


def send_halo(value, step):
    pairs = []
    for c in range(16):
        source = c // 4 - 1 if c % 4 == 0 else c // 4 + 1
        if c % 4 in (0, 3) and 0 <= source < TOWERS:
            pairs.append((c, source, (source + step) % TOWERS))
    return lax.ppermute(value, ("ctx", "tower"), ctx_towers(pairs))


def keys_of(kv_ref):
    return jnp.concatenate([kv_ref[r, 0, 0] for r in range(TOWERS)], axis=1)


def rows_of(kv_ref, which):
    return jnp.concatenate([kv_ref[r, which, 0] for r in range(TOWERS)], axis=0)


def lane_tiles(x):
    return [x[:, i : i + HD] for i in range(0, x.shape[1], HD)]


def flash_kernel(kv_count, first, last, after, *refs):
    q_ref = refs[0]
    kv_refs = refs[1 : 1 + kv_count]
    rest = refs[1 + kv_count :]
    rest = rest[: len(rest) - (1 if last else 4) - after] + rest[len(rest) - (1 if last else 4) :]
    if first:
        outs = rest
    else:
        acc_in, top_in, total_in = rest[:3]
        outs = rest[3:]
    size = 2 * VBLK
    tiles = [slice(i * size, (i + 1) * size) for i in range(2)]
    query = rows_of(q_ref, 0)
    keys = [keys_of(kv) for kv in kv_refs]
    all_scores = [[nn_dot(query[rows], k) for k in keys] for rows in tiles]
    for rows, scores in zip(tiles, all_scores):
        top = functools.reduce(jnp.maximum, [t for s in scores for t in lane_tiles(s)])
        top = jnp.max(top, axis=1, keepdims=True) * SCALE2
        if first:
            top = jnp.broadcast_to(top, (size, HD))
            acc = total = None
        else:
            top = jnp.maximum(top, top_in[rows])
            factor = jnp.exp2(top_in[rows] - top)
            acc = acc_in[rows] * factor
            total = total_in[rows] * factor
        wide = jnp.concatenate([top] * TOWERS, axis=1)
        for s, kv in zip(scores, kv_refs):
            weights = jnp.exp2(s * SCALE2 - wide)
            part = functools.reduce(jnp.add, lane_tiles(weights))
            total = part if total is None else total + part
            part = nn_dot(weights.astype(jnp.bfloat16), rows_of(kv, 1))
            acc = part if acc is None else acc + part
        if last:
            outs[0][rows] = (acc / jnp.sum(total, axis=1, keepdims=True)).astype(jnp.bfloat16)
        else:
            outs[0][rows] = acc
            outs[1][rows] = top
            outs[2][rows] = total
            outs[3][...] = total[:8]


QUERY = pl.BlockSpec((TOWERS, 1, 1, VBLK, HD), lambda h, *_: (0, 2, h, 0, 0))
SHARD = pl.BlockSpec((TOWERS, 2, 1, VBLK, HD), lambda h, *_: (0, 0, h, 0, 0))


def flash(query, kvs, state, last, after=()):
    rows = TOWERS * VBLK
    keys = rows * len(kvs)
    wide = jax.ShapeDtypeStruct((rows, GW), jnp.float32)
    head = pl.BlockSpec((rows, HD), lambda h: (0, h))
    if last:
        out_shape = jax.ShapeDtypeStruct((rows, GW), jnp.bfloat16)
        out_specs = head
    else:
        out_shape = [wide, wide, wide, jax.ShapeDtypeStruct((8, HD), jnp.float32)]
        out_specs = [head, head, head, pl.BlockSpec((8, HD), lambda h: (0, 0))]
    return pl.pallas_call(
        functools.partial(flash_kernel, len(kvs), state is None, last, len(after)),
        out_shape=out_shape,
        grid=(LOCAL,),
        in_specs=[QUERY] + [SHARD] * len(kvs) + ([] if state is None else [head] * 3) + [ANY] * len(after),
        out_specs=out_specs,
        compiler_params=pltpu.CompilerParams(vmem_limit_bytes=60 * MIB),
        cost_estimate=BRIEF,
        name="flash",
    )(query, *kvs, *(() if state is None else state), *after)


AUDIO_ROWS = 32
BOTH = VBLK + AUDIO_ROWS


def weighted(scores, values):
    weights = jnp.exp2(scores - jnp.max(scores, axis=1, keepdims=True)).astype(jnp.bfloat16)
    result = nn_dot(weights, jnp.concatenate([values, jnp.ones_like(values)], axis=1))
    return result[:, :HD] / result[:, HD:]


def audio_rows(place, margin, main, own, sibling, third):
    ctx = place[0]
    core = lax.rem(ctx, 2)
    row_block = lax.broadcasted_iota(jnp.int32, (QROWS, 1), 0) // ABLK + ctx * 4
    query = main[QAT:]
    pieces = [(own, r, ctx * 4 + r) for r in range(TOWERS)]
    after = lax.rem(ctx + 1, 16) * 4
    before = lax.rem(ctx + 15, 16) * 4 + 2
    for r in range(2):
        pieces.append((sibling, 2 * core + r, jnp.where(core == 0, after, before) + r))
        pieces.append((third, 2 - 2 * core + r, jnp.where(core == 0, before, after) + r))
    keys = jnp.concatenate([ref[r, 0, 0] for ref, r, _ in pieces], axis=1)
    values = jnp.concatenate([ref[r, 1, 0] for ref, r, _ in pieces], axis=0)
    raw = nn_dot(query, keys) * SCALE2
    scores = []
    for i, (_, _, block) in enumerate(pieces):
        hit = (
            (row_block == margin[block, 0])
            | (row_block == margin[block, 1])
            | (row_block == margin[block, 2])
        )
        scores.append(jnp.where(hit, raw[:, i * VBLK : (i + 1) * VBLK], NEG))
    scores = jnp.concatenate(scores, axis=1)
    return weighted(scores, values)


def cross_kernel(place, margin, q_ref, *refs):
    mains, halos, (own, sibling, third, out) = refs[:4], refs[4:8], refs[8:]
    main = functools.reduce(
        jnp.add, [ref[...] for ref in mains[1:]], jnp.where(place[1] == place[2], mains[0][...], 0)
    )
    halo = functools.reduce(
        jnp.add, [ref[...] for ref in halos[1:]], jnp.where(place[1] == place[3], halos[0][...], 0)
    )
    ctx = place[0]
    phase = lax.rem(ctx, 4)
    base = (ctx - phase) * 4
    lane = lax.broadcasted_iota(jnp.int32, (1, 256), 1)
    halo_base = jnp.where(phase == 0, base - 2, jnp.where(phase == 3, base + 16, -100))
    main_base = base + lax.div(main_first(ctx), ABLK)
    ids = jnp.where(lane < WIN, lane // ABLK + main_base, lane // ABLK - WIN // ABLK + halo_base)
    ids = jnp.where(lane < WIN + HALO, ids, -100)
    spare = jnp.zeros((256 - WIN - HALO, HD), jnp.bfloat16)
    keys = jnp.concatenate([main[:WIN], halo[:HALO], spare], axis=0)
    values = jnp.concatenate(
        [main[WIN:QAT], halo[HALO:], spare], axis=0
    )
    scores = nt_dot(rows_of(q_ref, 0), keys) * SCALE2
    parts = []
    for r in range(TOWERS):
        block = ctx * 4 + r
        hit = (ids == margin[block, 0]) | (ids == margin[block, 1]) | (ids == margin[block, 2])
        parts.append(jnp.where(hit, scores[r * VBLK : (r + 1) * VBLK], NEG))
    scores = jnp.concatenate(parts, axis=0)
    result = weighted(scores, values).astype(jnp.bfloat16)
    mixed = audio_rows(place, margin, main, own, sibling, third)
    for r in range(TOWERS):
        out[r, pl.ds(0, VBLK), :] = result[r * VBLK : (r + 1) * VBLK]
        padded = jnp.concatenate(
            [mixed[r * ABLK : (r + 1) * ABLK], jnp.zeros((AUDIO_ROWS - ABLK, HD), jnp.float32)], axis=0
        )
        out[r, pl.ds(VBLK, AUDIO_ROWS), :] = padded.astype(jnp.bfloat16)


def cross(place, margin, query, mains, halos, own, sibling, third):
    rows = TOWERS * VBLK
    return pl.pallas_call(
        cross_kernel,
        out_shape=jax.ShapeDtypeStruct((TOWERS, BOTH, GW), jnp.bfloat16),
        grid_spec=pltpu.PrefetchScalarGridSpec(
            num_scalar_prefetch=2,
            grid=(LOCAL,),
            in_specs=[
                QUERY,
            ]
            + [pl.BlockSpec((HAT, HD), lambda h, *_: (0, h))] * TOWERS
            + [pl.BlockSpec((2 * HALO, HD), lambda h, *_: (0, h))] * TOWERS
            + [SHARD] * 3,
            out_specs=pl.BlockSpec((TOWERS, BOTH, HD), lambda h, *_: (0, 0, h)),
        ),
        compiler_params=pltpu.CompilerParams(vmem_limit_bytes=60 * MIB),
        cost_estimate=BRIEF,
        name="cross",
    )(place, margin, query, *mains, *halos, own, sibling, third)


def weight_rows(pieces):
    return jnp.concatenate([piece(h) for h in range(LOCAL) for piece in pieces], axis=0)


def project_cross_kernel(place, own, sibling, w_ref, _, __, mine, up, down, up_first, down_first):
    towers = [lax.rem(place[1] + step, TOWERS) for step in range(TOWERS)]
    targets = (
        (mine, 0),
        (mine, BOTH),
        (up, 0),
        (up, BOTH),
        (up_first, 0),
        (down_first, 0),
        (down, 0),
        (down, BOTH),
    )
    ws = [
        weight_rows([functools.partial(lambda b, h: w_ref[b, kind, h], b) for b in range(4)])
        for kind in range(2)
    ]
    for step in range(TOWERS):
        for w, (first, count) in zip(ws, ((0, VBLK), (VBLK, AUDIO_ROWS))):
            both = [ref[towers[step], pl.ds(first, count), :] for ref in (own, sibling)]
            y = nn_dot(jnp.concatenate(both, axis=0), w).astype(jnp.bfloat16)
            for i in range(2):
                out, at = targets[2 * step + i]
                out[pl.ds(at + first, count), :] = y[i * count : (i + 1) * count]


def project_cross(place, own, sibling, w, after):
    width = w.shape[-1]
    tile = width // 3
    return pl.pallas_call(
        project_cross_kernel,
        out_shape=[jax.ShapeDtypeStruct((n * BOTH, width), jnp.bfloat16) for n in (2, 2, 2, 1, 1)],
        grid_spec=pltpu.PrefetchScalarGridSpec(
            num_scalar_prefetch=1,
            grid=(3,),
            in_specs=[
                full(own.shape),
                full(own.shape),
                pl.BlockSpec(w.shape[:-1] + (tile,), lambda i, place: (0, 0, 0, 0, i)),
                ANY,
                ANY,
            ],
            out_specs=[
                pl.BlockSpec((n * BOTH, tile), lambda i, place: (0, i)) for n in (2, 2, 2, 1, 1)
            ],
        ),
        compiler_params=pltpu.CompilerParams(vmem_limit_bytes=60 * MIB),
        cost_estimate=BRIEF,
        name="project_cross",
    )(place, own, sibling, w, *after)


def project_self_kernel(place, own, sibling, w_ref, *refs):
    mine, up, down, gain, video_out, audio_out, sibling_out = refs
    a = jnp.concatenate(
        [jnp.concatenate([ref[t] for t in range(TOWERS)], axis=1) for ref in (own, sibling)], axis=0
    )
    w = jnp.concatenate(
        [
            weight_rows([functools.partial(lambda b, h: w_ref[b * TOWERS + t, h], b) for b in range(4)])
            for t in range(TOWERS)
        ],
        axis=0,
    )
    acc = nn_dot(a, w)
    base = functools.reduce(jnp.add, [ref[...].astype(jnp.float32) for ref in (mine, up, down)])
    video, audio = [], []
    for i in range(2):
        video.append(gain[0:1] * (acc[i * VBLK : (i + 1) * VBLK] + base[i * BOTH : i * BOTH + VBLK]))
        audio.append(gain[1:2] * base[i * BOTH + VBLK : (i + 1) * BOTH])
    video_out[...] = video[0].astype(jnp.bfloat16)
    audio_out[...] = audio[0][:ABLK].astype(jnp.bfloat16)
    sibling_out[pl.ds(0, VBLK), :] = video[1].astype(jnp.bfloat16)
    sibling_out[pl.ds(VBLK, AUDIO_ROWS), :] = audio[1].astype(jnp.bfloat16)


def project_self(place, own, sibling, w, base, gains):
    width = w.shape[-1]
    tile = width // 3
    out = lambda rows: pl.BlockSpec((rows, tile), lambda i, place: (0, place[4] * 3 + i))
    return pl.pallas_call(
        project_self_kernel,
        out_shape=[
            jax.ShapeDtypeStruct((VBLK, 2 * width), jnp.bfloat16),
            jax.ShapeDtypeStruct((ABLK, 2 * width), jnp.bfloat16),
            jax.ShapeDtypeStruct((BOTH, width), jnp.bfloat16),
        ],
        grid_spec=pltpu.PrefetchScalarGridSpec(
            num_scalar_prefetch=1,
            grid=(3,),
            in_specs=[
                full(own.shape),
                full(own.shape),
                pl.BlockSpec(w.shape[:-1] + (tile,), lambda i, place: (0, 0, 0, i)),
            ]
            + [pl.BlockSpec((2 * BOTH, tile), lambda i, place: (0, i))] * 3
            + [pl.BlockSpec((2, tile), lambda i, place: (0, place[4] * 3 + i))],
            out_specs=[out(VBLK), out(ABLK), pl.BlockSpec((BOTH, tile), lambda i, place: (0, i))],
        ),
        compiler_params=pltpu.CompilerParams(vmem_limit_bytes=60 * MIB),
        cost_estimate=BRIEF,
        name="project_self",
    )(place, own, sibling, w, *base, gains)


def assemble_kernel(place, video_in, audio_in, theirs, video, audio):
    video[...] = theirs[pl.ds(0, VBLK), :]
    audio[...] = theirs[pl.ds(VBLK, AUDIO_ROWS), :].astype(jnp.float32)[:ABLK].astype(jnp.bfloat16)


def assemble(place, video, audio, theirs):
    width = theirs.shape[1]

    def column(i, place):
        return (0, 1 - place[4])

    return pl.pallas_call(
        assemble_kernel,
        out_shape=[jax.ShapeDtypeStruct(x.shape, x.dtype) for x in (video, audio)],
        grid_spec=pltpu.PrefetchScalarGridSpec(
            num_scalar_prefetch=1,
            grid=(1,),
            in_specs=[ANY, ANY, full(theirs.shape)],
            out_specs=[pl.BlockSpec((VBLK, width), column), pl.BlockSpec((ABLK, width), column)],
        ),
        input_output_aliases={1: 0, 2: 1},
        compiler_params=pltpu.CompilerParams(vmem_limit_bytes=16 * MIB),
        name="assemble",
    )(place, video, audio, theirs)


def gate_kernel(*refs):
    pass


def gate(value, *after):
    return pl.pallas_call(
        gate_kernel,
        out_shape=jax.ShapeDtypeStruct(value.shape, value.dtype),
        in_specs=[ANY] * (1 + len(after)),
        out_specs=ANY,
        input_output_aliases={0: 0},
        compiler_params=pltpu.CompilerParams(vmem_limit_bytes=60 * MIB),
        name="gate",
    )(value, *after)


def exchange_towers(value):
    return lax.all_to_all(value, "tower", split_axis=0, concat_axis=0, tiled=True)


def add_kernel(up, down, up_first, down_first, up_out, down_out):
    for a, b, out in ((up, up_first, up_out), (down, down_first, down_out)):
        out[...] = (a[...].astype(jnp.float32) + b[...].astype(jnp.float32)).astype(jnp.bfloat16)


def add_halves(up, down, up_first, down_first):
    rows, width = up_first.shape
    tile = width // 3
    first = pl.BlockSpec((rows, tile), lambda i: (0, i))
    second = pl.BlockSpec((rows, tile), lambda i: (1, i))
    return pl.pallas_call(
        add_kernel,
        out_shape=[jax.ShapeDtypeStruct(up.shape, up.dtype)] * 2,
        grid=(3,),
        in_specs=[first, second, first, first],
        out_specs=[first, second],
        input_output_aliases={0: 0, 1: 1},
        compiler_params=pltpu.CompilerParams(vmem_limit_bytes=60 * MIB),
        cost_estimate=BRIEF,
        name="add_halves",
    )(up, down, up_first, down_first)


def shift_tower(value, step):
    return lax.ppermute(value, "tower", [(i, (i + step) % TOWERS) for i in range(TOWERS)])


def hop(value):
    total = 2 * CHIPS
    return lax.ppermute(value, "ctx", [(i, (i + 2 - 4 * (i % 2)) % total) for i in range(total)])


def swap_core(value):
    return lax.ppermute(value, "ctx", [(i, i ^ 1) for i in range(2 * CHIPS)])


def shards(video_q, video_k, video_v, audio_q, audio_k, audio_v, margin, out_weight, gate_gains):
    ctx = lax.axis_index("ctx")
    tower = lax.axis_index("tower")
    core = lax.rem(ctx, 2)
    place = jnp.stack([ctx, tower, ctx // 4, edge_tower(ctx), core]).astype(jnp.int32)
    gains = gate_gains[0]
    margins = margin[0]

    parts, w_self, w_rest, *audio = pack(
        place, video_k[0], video_v[0], video_q[0], audio_k[0], audio_v[0], audio_q[0], out_weight
    )
    w_rest = lax.all_gather(w_rest, "batch", axis=0, tiled=False)
    w_self = lax.all_gather(w_self, ("batch", "tower"), axis=0, tiled=False)
    query = exchange_towers(parts)
    own = query[:, :2]
    sibling = swap_core(own)
    near, far = hop(own), hop(sibling)
    mains = [audio[0]] + [send_main(gate(audio[step], sibling), step) for step in (1, 2, 3)]

    acc, top, total, token = flash(query, [own, sibling], None, False)
    halos = [audio[4]] + [send_halo(gate(audio[4 + step], token), step) for step in (1, 2, 3)]
    near, far = gate(near, token, *mains[1:], *halos[1:]), gate(far, token)
    crossed = cross(place, margins, query, mains, halos, own, sibling, far)

    rest, up, down, up_first, down_first = project_cross(
        place, crossed, swap_core(crossed), w_rest, (token, token)
    )
    up_first, down_first = shift_tower(up_first, 1), shift_tower(down_first, -1)

    behind = [crossed]
    after = (rest,)
    for step in range(1, 4):
        if step == 3:
            up, down = add_halves(up, down, up_first, down_first)
            after = (up, down)
        now = [near, far, swap_core(near), swap_core(far)]
        near, far = hop(near), (hop(far) if step < 3 else None)
        acc, top, total, token = flash(query, now, (acc, top, total), False, after)
        behind.append(token)
        after = ()
        near = gate(near, behind[step - 1])
        if step < 3:
            far = gate(far, behind[step - 1])
    video_self = flash(query, [near, swap_core(near)], (acc, top, total), True)
    base = (rest, shift_tower(up, 1), shift_tower(down, -1))

    self_all = exchange_towers(video_self.reshape(TOWERS, VBLK, GW))
    video_out, audio_out, theirs = project_self(place, self_all, swap_core(self_all), w_self, base, gains)
    video_out, audio_out = assemble(place, video_out, audio_out, swap_core(theirs))
    return (video_out[None], audio_out[None])


def solution(mesh):
    return jax.shard_map(
        shards,
        mesh=mesh,
        in_specs=(
            P("batch", ("ctx", "tower"), None),
            P("batch", ("ctx", "tower"), None),
            P("batch", ("ctx", "tower"), None),
            P("batch", "tower", None),
            P("batch", "tower", None),
            P("batch", "tower", None),
            P("batch", None, None),
            P(None, "tower", "batch", None),
            P("batch", None, None),
        ),
        out_specs=(P("batch", ("ctx", "tower"), None), P("batch", ("ctx", "tower"), None)),
        check_vma=False,
    )
```

```python
import functools

import jax
import jax.numpy as jnp
from jax import lax
from jax.experimental import pallas as pl
from jax.experimental.pallas import tpu as pltpu
from jax.sharding import PartitionSpec as P

H = 12
HD = 128
VBLK = 128
ABLK = 24
TOWERS = 4
CHIPS = 8
LOCAL = H // TOWERS
GW = LOCAL * HD
NEG = -1e30
SCALE2 = HD**-0.5 * 1.4426950408889634
MIB = 1024 * 1024


def nt_dot(a, b):
    return lax.dot_general(a, b, (((1,), (1,)), ((), ())), preferred_element_type=jnp.float32)


def nn_dot(a, b):
    return jnp.dot(a, b, preferred_element_type=jnp.float32)


def full(shape):
    return pl.BlockSpec(shape, lambda *_: (0,) * len(shape))


BRIEF = pl.CostEstimate(flops=1, bytes_accessed=1, transcendentals=0)
ANY = pl.BlockSpec(memory_space=pl.ANY)


def start_copies(pairs, sem, first):
    copies = [pltpu.make_async_copy(a, b, sem.at[first + i]) for i, (a, b) in enumerate(pairs)]
    for copy in copies:
        copy.start()
    return copies


WIN = 192
HALO = 48
QROWS = 96
QAT = 2 * WIN
HAT = QAT + QROWS
AROWS = HAT + 2 * HALO


def main_first(ctx):
    return jnp.clip(lax.rem(ctx, 4) * QROWS - HALO, 0, 384 - WIN)


def edge_tower(ctx):
    phase = lax.rem(ctx, 4)
    edge = jnp.where(phase == 0, ctx // 4 - 1, ctx // 4 + 1)
    return jnp.where(((phase == 0) | (phase == 3)) & (edge >= 0) & (edge < TOWERS), edge, -1)


def pack_kernel(
    place, k_ref, v_ref, q_ref, ak_ref, av_ref, aq_ref, w_ref,
    out, self_out, rest_out, main0, main1, main2, main3, halo0, halo1, halo2, halo3,
    rows, turned, audio, w_rows, sem,
):
    ctx, tower = place[0], place[1]
    phase = lax.rem(ctx, 4)
    main = pl.ds(pl.multiple_of(main_first(ctx), 16), WIN)
    mine = pl.ds(pl.multiple_of(phase * QROWS, 16), QROWS)
    halo = pl.ds(pl.multiple_of(jnp.where(phase == 0, 384 - HALO, 0), 16), HALO)
    half = w_ref.shape[3] // 2
    columns = pl.ds(pl.multiple_of(place[4] * half, 128), half)
    coming = start_copies([(ref, rows.at[i]) for i, ref in enumerate((k_ref, v_ref, q_ref))], sem, 0)
    coming_w = start_copies([(w_ref.at[:, :, :, columns], w_rows)], sem, 3)
    coming_audio = start_copies(
        [
            (ak_ref.at[main], audio.at[pl.ds(0, WIN)]),
            (av_ref.at[main], audio.at[pl.ds(WIN, WIN)]),
            (aq_ref.at[mine], audio.at[pl.ds(QAT, QROWS)]),
            (ak_ref.at[halo], audio.at[pl.ds(HAT, HALO)]),
            (av_ref.at[halo], audio.at[pl.ds(HAT + HALO, HALO)]),
        ],
        sem,
        4,
    )
    heads = [(g, h) for g in range(TOWERS) for h in range(LOCAL)]
    going = []
    for i in (1, 2):
        coming[i].wait()
        pairs = [
            (rows.at[i, :, pl.ds((g * LOCAL + h) * HD, HD)], out.at[g, i, h]) for g, h in heads
        ]
        going += start_copies(pairs, sem, 9 + (i - 1) * H)
    coming[0].wait()
    for g, h in heads:
        block = rows[0, :, pl.ds((g * LOCAL + h) * HD, HD)]
        turned[g, h] = block.astype(jnp.float32).T.astype(jnp.bfloat16)
    going += start_copies([(turned.at[g], out.at[g, 0]) for g in range(TOWERS)], sem, 33)
    coming_w[0].wait()
    going += start_copies([(w_rows.at[0], self_out), (w_rows.at[pl.ds(1, 2)], rest_out)], sem, 37)
    for copy in coming_audio:
        copy.wait()
    pairs = []
    for step, (main_out, halo_out) in enumerate(
        ((main0, halo0), (main1, halo1), (main2, halo2), (main3, halo3))
    ):
        group = pl.ds(pl.multiple_of(lax.rem(tower + step, TOWERS) * GW, 128), GW)
        pairs.append((audio.at[pl.ds(0, HAT), group], main_out))
        pairs.append((audio.at[pl.ds(HAT, 2 * HALO), group], halo_out))
    going += start_copies(pairs, sem, 39)
    for copy in going:
        copy.wait()


def pack(place, k, v, q, ak, av, aq, w):
    rows = k.shape[0]
    narrow = (LOCAL, w.shape[2], w.shape[3] // 2)
    shapes = [(TOWERS, 3, LOCAL, rows, HD), narrow, (2,) + narrow]
    shapes += [(HAT, GW)] * TOWERS + [(2 * HALO, GW)] * TOWERS
    return pl.pallas_call(
        pack_kernel,
        out_shape=[jax.ShapeDtypeStruct(shape, jnp.bfloat16) for shape in shapes],
        grid_spec=pltpu.PrefetchScalarGridSpec(
            num_scalar_prefetch=1,
            grid=(1,),
            in_specs=[ANY] * 7,
            out_specs=[ANY] * len(shapes),
            scratch_shapes=[
                pltpu.VMEM((3,) + k.shape, jnp.bfloat16),
                pltpu.VMEM((TOWERS, LOCAL, HD, rows), jnp.bfloat16),
                pltpu.VMEM((AROWS, aq.shape[1]), jnp.bfloat16),
                pltpu.VMEM((3,) + narrow, jnp.bfloat16),
                pltpu.SemaphoreType.DMA((47,)),
            ],
        ),
        compiler_params=pltpu.CompilerParams(vmem_limit_bytes=60 * MIB),
        name="pack",
    )(place, k, v, q, ak, av, aq, w)


def ctx_towers(pairs):
    return [(c * TOWERS + s, c * TOWERS + d) for c, s, d in pairs]


def send_main(value, step):
    pairs = [(c, c // 4, (c // 4 + step) % TOWERS) for c in range(16)]
    return lax.ppermute(value, ("ctx", "tower"), ctx_towers(pairs))


def send_halo(value, step):
    pairs = []
    for c in range(16):
        source = c // 4 - 1 if c % 4 == 0 else c // 4 + 1
        if c % 4 in (0, 3) and 0 <= source < TOWERS:
            pairs.append((c, source, (source + step) % TOWERS))
    return lax.ppermute(value, ("ctx", "tower"), ctx_towers(pairs))


def keys_of(kv_ref):
    return jnp.concatenate([kv_ref[r, 0, 0] for r in range(TOWERS)], axis=1)


def rows_of(kv_ref, which):
    return jnp.concatenate([kv_ref[r, which, 0] for r in range(TOWERS)], axis=0)


def lane_tiles(x):
    return [x[:, i : i + HD] for i in range(0, x.shape[1], HD)]


def flash_kernel(kv_count, first, last, after, *refs):
    q_ref = refs[0]
    kv_refs = [ref.at[i] for ref in refs[1 : 1 + kv_count] for i in range(ref.shape[0])]
    rest = refs[1 + kv_count :]
    rest = rest[: len(rest) - (1 if last else 4) - after] + rest[len(rest) - (1 if last else 4) :]
    if first:
        outs = rest
    else:
        acc_in, top_in, total_in = rest[:3]
        outs = rest[3:]
    size = 2 * VBLK
    tiles = [slice(i * size, (i + 1) * size) for i in range(2)]
    query = rows_of(q_ref, 0)
    keys = [keys_of(kv) for kv in kv_refs]
    all_scores = [[nn_dot(query[rows], k) for k in keys] for rows in tiles]
    for rows, scores in zip(tiles, all_scores):
        top = functools.reduce(jnp.maximum, [t for s in scores for t in lane_tiles(s)])
        top = jnp.max(top, axis=1, keepdims=True) * SCALE2
        if first:
            top = jnp.broadcast_to(top, (size, HD))
            acc = total = None
        else:
            top = jnp.maximum(top, top_in[rows])
            factor = jnp.exp2(top_in[rows] - top)
            acc = acc_in[rows] * factor
            total = total_in[rows] * factor
        wide = jnp.concatenate([top] * TOWERS, axis=1)
        for s, kv in zip(scores, kv_refs):
            weights = jnp.exp2(s * SCALE2 - wide)
            part = functools.reduce(jnp.add, lane_tiles(weights))
            total = part if total is None else total + part
            part = nn_dot(weights.astype(jnp.bfloat16), rows_of(kv, 1))
            acc = part if acc is None else acc + part
        if last:
            outs[0][rows] = (acc / jnp.sum(total, axis=1, keepdims=True)).astype(jnp.bfloat16)
        else:
            outs[0][rows] = acc
            outs[1][rows] = top
            outs[2][rows] = total
            outs[3][...] = total[:8]


QUERY = pl.BlockSpec((TOWERS, 1, 1, VBLK, HD), lambda h, *_: (0, 2, h, 0, 0))


def shards_spec(count):
    return pl.BlockSpec((count, TOWERS, 2, 1, VBLK, HD), lambda h, *_: (0, 0, 0, h, 0, 0))


def shard_spec(which):
    return pl.BlockSpec((None, TOWERS, 2, 1, VBLK, HD), lambda h, *_: (which, 0, 0, h, 0, 0))


def flash(query, kvs, state, last, after=()):
    rows = TOWERS * VBLK
    keys = rows * len(kvs)
    wide = jax.ShapeDtypeStruct((rows, GW), jnp.float32)
    head = pl.BlockSpec((rows, HD), lambda h: (0, h))
    if last:
        out_shape = jax.ShapeDtypeStruct((rows, GW), jnp.bfloat16)
        out_specs = head
    else:
        out_shape = [wide, wide, wide, jax.ShapeDtypeStruct((8, HD), jnp.float32)]
        out_specs = [head, head, head, pl.BlockSpec((8, HD), lambda h: (0, 0))]
    return pl.pallas_call(
        functools.partial(flash_kernel, len(kvs), state is None, last, len(after)),
        out_shape=out_shape,
        grid=(LOCAL,),
        in_specs=[QUERY] + [shards_spec(kv.shape[0]) for kv in kvs] + ([] if state is None else [head] * 3) + [ANY] * len(after),
        out_specs=out_specs,
        compiler_params=pltpu.CompilerParams(vmem_limit_bytes=60 * MIB),
        cost_estimate=BRIEF,
        name="flash",
    )(query, *kvs, *(() if state is None else state), *after)


AUDIO_ROWS = 32
BOTH = VBLK + AUDIO_ROWS


def weighted(scores, values):
    weights = jnp.exp2(scores - jnp.max(scores, axis=1, keepdims=True)).astype(jnp.bfloat16)
    result = nn_dot(weights, jnp.concatenate([values, jnp.ones_like(values)], axis=1))
    return result[:, :HD] / result[:, HD:]


def audio_rows(place, margin, main, own, sibling, third):
    ctx = place[0]
    core = lax.rem(ctx, 2)
    row_block = lax.broadcasted_iota(jnp.int32, (QROWS, 1), 0) // ABLK + ctx * 4
    query = main[QAT:]
    pieces = [(own, r, ctx * 4 + r) for r in range(TOWERS)]
    after = lax.rem(ctx + 1, 16) * 4
    before = lax.rem(ctx + 15, 16) * 4 + 2
    for r in range(2):
        pieces.append((sibling, 2 * core + r, jnp.where(core == 0, after, before) + r))
        pieces.append((third, 2 - 2 * core + r, jnp.where(core == 0, before, after) + r))
    keys = jnp.concatenate([ref[r, 0, 0] for ref, r, _ in pieces], axis=1)
    values = jnp.concatenate([ref[r, 1, 0] for ref, r, _ in pieces], axis=0)
    raw = nn_dot(query, keys) * SCALE2
    scores = []
    for i, (_, _, block) in enumerate(pieces):
        hit = (
            (row_block == margin[block, 0])
            | (row_block == margin[block, 1])
            | (row_block == margin[block, 2])
        )
        scores.append(jnp.where(hit, raw[:, i * VBLK : (i + 1) * VBLK], NEG))
    scores = jnp.concatenate(scores, axis=1)
    return weighted(scores, values)


def cross_kernel(place, margin, q_ref, *refs):
    mains, halos, (own, sibling, third, out) = refs[:4], refs[4:8], refs[8:]
    main = functools.reduce(
        jnp.add, [ref[...] for ref in mains[1:]], jnp.where(place[1] == place[2], mains[0][...], 0)
    )
    halo = functools.reduce(
        jnp.add, [ref[...] for ref in halos[1:]], jnp.where(place[1] == place[3], halos[0][...], 0)
    )
    ctx = place[0]
    phase = lax.rem(ctx, 4)
    base = (ctx - phase) * 4
    lane = lax.broadcasted_iota(jnp.int32, (1, 256), 1)
    halo_base = jnp.where(phase == 0, base - 2, jnp.where(phase == 3, base + 16, -100))
    main_base = base + lax.div(main_first(ctx), ABLK)
    ids = jnp.where(lane < WIN, lane // ABLK + main_base, lane // ABLK - WIN // ABLK + halo_base)
    ids = jnp.where(lane < WIN + HALO, ids, -100)
    spare = jnp.zeros((256 - WIN - HALO, HD), jnp.bfloat16)
    keys = jnp.concatenate([main[:WIN], halo[:HALO], spare], axis=0)
    values = jnp.concatenate(
        [main[WIN:QAT], halo[HALO:], spare], axis=0
    )
    scores = nt_dot(rows_of(q_ref, 0), keys) * SCALE2
    parts = []
    for r in range(TOWERS):
        block = ctx * 4 + r
        hit = (ids == margin[block, 0]) | (ids == margin[block, 1]) | (ids == margin[block, 2])
        parts.append(jnp.where(hit, scores[r * VBLK : (r + 1) * VBLK], NEG))
    scores = jnp.concatenate(parts, axis=0)
    result = weighted(scores, values).astype(jnp.bfloat16)
    mixed = audio_rows(place, margin, main, own, sibling, third)
    for r in range(TOWERS):
        out[r, pl.ds(0, VBLK), :] = result[r * VBLK : (r + 1) * VBLK]
        padded = jnp.concatenate(
            [mixed[r * ABLK : (r + 1) * ABLK], jnp.zeros((AUDIO_ROWS - ABLK, HD), jnp.float32)], axis=0
        )
        out[r, pl.ds(VBLK, AUDIO_ROWS), :] = padded.astype(jnp.bfloat16)


def cross(place, margin, query, mains, halos, here, behind):
    rows = TOWERS * VBLK
    return pl.pallas_call(
        cross_kernel,
        out_shape=jax.ShapeDtypeStruct((TOWERS, BOTH, GW), jnp.bfloat16),
        grid_spec=pltpu.PrefetchScalarGridSpec(
            num_scalar_prefetch=2,
            grid=(LOCAL,),
            in_specs=[
                QUERY,
            ]
            + [pl.BlockSpec((HAT, HD), lambda h, *_: (0, h))] * TOWERS
            + [pl.BlockSpec((2 * HALO, HD), lambda h, *_: (0, h))] * TOWERS
            + [shard_spec(0), shard_spec(1), shard_spec(1)],
            out_specs=pl.BlockSpec((TOWERS, BOTH, HD), lambda h, *_: (0, 0, h)),
        ),
        compiler_params=pltpu.CompilerParams(vmem_limit_bytes=60 * MIB),
        cost_estimate=BRIEF,
        name="cross",
    )(place, margin, query, *mains, *halos, here, here, behind)


def weight_rows(pieces):
    return jnp.concatenate([piece(h) for h in range(LOCAL) for piece in pieces], axis=0)


def project_cross_kernel(place, own, sibling, w_ref, _, __, mine, up, down, up_first, down_first):
    towers = [lax.rem(place[1] + step, TOWERS) for step in range(TOWERS)]
    targets = (
        (mine, 0),
        (mine, BOTH),
        (up, 0),
        (up, BOTH),
        (up_first, 0),
        (down_first, 0),
        (down, 0),
        (down, BOTH),
    )
    ws = [
        weight_rows([functools.partial(lambda b, h: w_ref[b, kind, h], b) for b in range(4)])
        for kind in range(2)
    ]
    for step in range(TOWERS):
        for w, (first, count) in zip(ws, ((0, VBLK), (VBLK, AUDIO_ROWS))):
            both = [ref[towers[step], pl.ds(first, count), :] for ref in (own, sibling)]
            y = nn_dot(jnp.concatenate(both, axis=0), w).astype(jnp.bfloat16)
            for i in range(2):
                out, at = targets[2 * step + i]
                out[pl.ds(at + first, count), :] = y[i * count : (i + 1) * count]


def project_cross(place, own, sibling, w, after):
    width = w.shape[-1]
    tile = width // 3
    return pl.pallas_call(
        project_cross_kernel,
        out_shape=[jax.ShapeDtypeStruct((n * BOTH, width), jnp.bfloat16) for n in (2, 2, 2, 1, 1)],
        grid_spec=pltpu.PrefetchScalarGridSpec(
            num_scalar_prefetch=1,
            grid=(3,),
            in_specs=[
                full(own.shape),
                full(own.shape),
                pl.BlockSpec(w.shape[:-1] + (tile,), lambda i, place: (0, 0, 0, 0, i)),
                ANY,
                ANY,
            ],
            out_specs=[
                pl.BlockSpec((n * BOTH, tile), lambda i, place: (0, i)) for n in (2, 2, 2, 1, 1)
            ],
        ),
        compiler_params=pltpu.CompilerParams(vmem_limit_bytes=60 * MIB),
        cost_estimate=BRIEF,
        name="project_cross",
    )(place, own, sibling, w, *after)


def project_self_kernel(place, own, sibling, w_ref, *refs):
    mine, up, down, gain, video_out, audio_out, sibling_out = refs
    a = jnp.concatenate(
        [jnp.concatenate([ref[t] for t in range(TOWERS)], axis=1) for ref in (own, sibling)], axis=0
    )
    w = jnp.concatenate(
        [
            weight_rows([functools.partial(lambda b, h: w_ref[b * TOWERS + t, h], b) for b in range(4)])
            for t in range(TOWERS)
        ],
        axis=0,
    )
    acc = nn_dot(a, w)
    base = functools.reduce(jnp.add, [ref[...].astype(jnp.float32) for ref in (mine, up, down)])
    video, audio = [], []
    for i in range(2):
        video.append(gain[0:1] * (acc[i * VBLK : (i + 1) * VBLK] + base[i * BOTH : i * BOTH + VBLK]))
        audio.append(gain[1:2] * base[i * BOTH + VBLK : (i + 1) * BOTH])
    video_out[...] = video[0].astype(jnp.bfloat16)
    audio_out[...] = audio[0][:ABLK].astype(jnp.bfloat16)
    sibling_out[pl.ds(0, VBLK), :] = video[1].astype(jnp.bfloat16)
    sibling_out[pl.ds(VBLK, AUDIO_ROWS), :] = audio[1].astype(jnp.bfloat16)


def project_self(place, own, sibling, w, base, gains):
    width = w.shape[-1]
    tile = width // 3
    out = lambda rows: pl.BlockSpec((rows, tile), lambda i, place: (0, place[4] * 3 + i))
    return pl.pallas_call(
        project_self_kernel,
        out_shape=[
            jax.ShapeDtypeStruct((VBLK, 2 * width), jnp.bfloat16),
            jax.ShapeDtypeStruct((ABLK, 2 * width), jnp.bfloat16),
            jax.ShapeDtypeStruct((BOTH, width), jnp.bfloat16),
        ],
        grid_spec=pltpu.PrefetchScalarGridSpec(
            num_scalar_prefetch=1,
            grid=(3,),
            in_specs=[
                full(own.shape),
                full(own.shape),
                pl.BlockSpec(w.shape[:-1] + (tile,), lambda i, place: (0, 0, 0, i)),
            ]
            + [pl.BlockSpec((2 * BOTH, tile), lambda i, place: (0, i))] * 3
            + [pl.BlockSpec((2, tile), lambda i, place: (0, place[4] * 3 + i))],
            out_specs=[out(VBLK), out(ABLK), pl.BlockSpec((BOTH, tile), lambda i, place: (0, i))],
        ),
        compiler_params=pltpu.CompilerParams(vmem_limit_bytes=60 * MIB),
        cost_estimate=BRIEF,
        name="project_self",
    )(place, own, sibling, w, *base, gains)


def assemble_kernel(place, video_in, audio_in, theirs, video, audio):
    video[...] = theirs[pl.ds(0, VBLK), :]
    audio[...] = theirs[pl.ds(VBLK, AUDIO_ROWS), :].astype(jnp.float32)[:ABLK].astype(jnp.bfloat16)


def assemble(place, video, audio, theirs):
    width = theirs.shape[1]

    def column(i, place):
        return (0, 1 - place[4])

    return pl.pallas_call(
        assemble_kernel,
        out_shape=[jax.ShapeDtypeStruct(x.shape, x.dtype) for x in (video, audio)],
        grid_spec=pltpu.PrefetchScalarGridSpec(
            num_scalar_prefetch=1,
            grid=(1,),
            in_specs=[ANY, ANY, full(theirs.shape)],
            out_specs=[pl.BlockSpec((VBLK, width), column), pl.BlockSpec((ABLK, width), column)],
        ),
        input_output_aliases={1: 0, 2: 1},
        compiler_params=pltpu.CompilerParams(vmem_limit_bytes=16 * MIB),
        name="assemble",
    )(place, video, audio, theirs)


def gate_kernel(*refs):
    pass


def gate(value, *after):
    return pl.pallas_call(
        gate_kernel,
        out_shape=jax.ShapeDtypeStruct(value.shape, value.dtype),
        in_specs=[ANY] * (1 + len(after)),
        out_specs=ANY,
        input_output_aliases={0: 0},
        compiler_params=pltpu.CompilerParams(vmem_limit_bytes=60 * MIB),
        name="gate",
    )(value, *after)


def exchange_towers(value):
    return lax.all_to_all(value, "tower", split_axis=0, concat_axis=0, tiled=True)


def add_kernel(up, down, up_first, down_first, up_out, down_out):
    for a, b, out in ((up, up_first, up_out), (down, down_first, down_out)):
        out[...] = (a[...].astype(jnp.float32) + b[...].astype(jnp.float32)).astype(jnp.bfloat16)


def add_halves(up, down, up_first, down_first):
    rows, width = up_first.shape
    tile = width // 3
    first = pl.BlockSpec((rows, tile), lambda i: (0, i))
    second = pl.BlockSpec((rows, tile), lambda i: (1, i))
    return pl.pallas_call(
        add_kernel,
        out_shape=[jax.ShapeDtypeStruct(up.shape, up.dtype)] * 2,
        grid=(3,),
        in_specs=[first, second, first, first],
        out_specs=[first, second],
        input_output_aliases={0: 0, 1: 1},
        compiler_params=pltpu.CompilerParams(vmem_limit_bytes=60 * MIB),
        cost_estimate=BRIEF,
        name="add_halves",
    )(up, down, up_first, down_first)


def shift_tower(value, step):
    return lax.ppermute(value, "tower", [(i, (i + step) % TOWERS) for i in range(TOWERS)])


def hop(value):
    total = 2 * CHIPS
    return lax.ppermute(value, "ctx", [(i, (i + 2 - 4 * (i % 2)) % total) for i in range(total)])


def swap_core(value):
    return lax.ppermute(value, "ctx", [(i, i ^ 1) for i in range(2 * CHIPS)])


def shards(video_q, video_k, video_v, audio_q, audio_k, audio_v, margin, out_weight, gate_gains):
    ctx = lax.axis_index("ctx")
    tower = lax.axis_index("tower")
    core = lax.rem(ctx, 2)
    place = jnp.stack([ctx, tower, ctx // 4, edge_tower(ctx), core]).astype(jnp.int32)
    gains = gate_gains[0]
    margins = margin[0]

    parts, w_self, w_rest, *audio = pack(
        place, video_k[0], video_v[0], video_q[0], audio_k[0], audio_v[0], audio_q[0], out_weight
    )
    w_rest = lax.all_gather(w_rest, "batch", axis=0, tiled=False)
    w_self = lax.all_gather(w_self, ("batch", "tower"), axis=0, tiled=False)
    query = exchange_towers(parts)
    own = query[:, :2]
    sibling = swap_core(own)
    here = jnp.stack([own, sibling])
    ahead = hop(here)
    mains = [audio[0]] + [send_main(gate(audio[step], sibling), step) for step in (1, 2, 3)]

    acc, top, total, token = flash(query, [here], None, False)
    halos = [audio[4]] + [send_halo(gate(audio[4 + step], token), step) for step in (1, 2, 3)]
    ahead = gate(ahead, token, *mains[1:], *halos[1:])
    crossed = cross(place, margins, query, mains, halos, here, ahead)
    rest, up, down, up_first, down_first = project_cross(
        place, crossed, swap_core(crossed), w_rest, (token, token)
    )
    up_first, down_first = shift_tower(up_first, 1), shift_tower(down_first, -1)

    behind = [crossed]
    after = (rest,)
    for step in range(1, 4):
        now = [ahead, swap_core(ahead)]
        ahead = hop(ahead if step < 3 else ahead[:1])
        acc, top, total, token = flash(query, now, (acc, top, total), False, after)
        behind.append(token)
        after = ()
        ahead = gate(ahead, behind[step - 1])
    up, down = add_halves(gate(up, token), down, up_first, down_first)
    video_self = flash(query, [ahead, swap_core(ahead)], (acc, top, total), True, (up, down))
    base = (rest, shift_tower(up, 1), shift_tower(down, -1))

    self_all = exchange_towers(video_self.reshape(TOWERS, VBLK, GW))
    video_out, audio_out, theirs = project_self(place, self_all, swap_core(self_all), w_self, base, gains)
    video_out, audio_out = assemble(place, video_out, audio_out, swap_core(theirs))
    return (video_out[None], audio_out[None])


def solution(mesh):
    return jax.shard_map(
        shards,
        mesh=mesh,
        in_specs=(
            P("batch", ("ctx", "tower"), None),
            P("batch", ("ctx", "tower"), None),
            P("batch", ("ctx", "tower"), None),
            P("batch", "tower", None),
            P("batch", "tower", None),
            P("batch", "tower", None),
            P("batch", None, None),
            P(None, "tower", "batch", None),
            P("batch", None, None),
        ),
        out_specs=(P("batch", ("ctx", "tower"), None), P("batch", ("ctx", "tower"), None)),
        check_vma=False,
    )
```

```python
import functools

import jax
import jax.numpy as jnp
from jax import lax
from jax.experimental import pallas as pl
from jax.experimental.pallas import tpu as pltpu
from jax.sharding import PartitionSpec as P

H = 12
HD = 128
VBLK = 128
ABLK = 24
TOWERS = 4
CHIPS = 8
LOCAL = H // TOWERS
GW = LOCAL * HD
NEG = -1e30
SCALE2 = HD**-0.5 * 1.4426950408889634
MIB = 1024 * 1024


def nt_dot(a, b):
    return lax.dot_general(a, b, (((1,), (1,)), ((), ())), preferred_element_type=jnp.float32)


def nn_dot(a, b):
    return jnp.dot(a, b, preferred_element_type=jnp.float32)


def full(shape):
    return pl.BlockSpec(shape, lambda *_: (0,) * len(shape))


BRIEF = pl.CostEstimate(flops=1, bytes_accessed=1, transcendentals=0)
ANY = pl.BlockSpec(memory_space=pl.ANY)


def start_copies(pairs, sem, first):
    copies = [pltpu.make_async_copy(a, b, sem.at[first + i]) for i, (a, b) in enumerate(pairs)]
    for copy in copies:
        copy.start()
    return copies


WIN = 192
HALO = 48
QROWS = 96
QAT = 2 * WIN
HAT = QAT + QROWS
AROWS = HAT + 2 * HALO


def main_first(ctx):
    return jnp.clip(lax.rem(ctx, 4) * QROWS - HALO, 0, 384 - WIN)


def edge_tower(ctx):
    phase = lax.rem(ctx, 4)
    edge = jnp.where(phase == 0, ctx // 4 - 1, ctx // 4 + 1)
    return jnp.where(((phase == 0) | (phase == 3)) & (edge >= 0) & (edge < TOWERS), edge, -1)


def pack_kernel(
    place, k_ref, v_ref, q_ref, ak_ref, av_ref, aq_ref, w_ref,
    out, self_out, rest_out, main0, main1, main2, main3, halo0, halo1, halo2, halo3,
    rows, turned, audio, w_rows, sem,
):
    ctx, tower = place[0], place[1]
    phase = lax.rem(ctx, 4)
    main = pl.ds(pl.multiple_of(main_first(ctx), 16), WIN)
    mine = pl.ds(pl.multiple_of(phase * QROWS, 16), QROWS)
    halo = pl.ds(pl.multiple_of(jnp.where(phase == 0, 384 - HALO, 0), 16), HALO)
    half = w_ref.shape[3] // 2
    columns = pl.ds(pl.multiple_of(place[4] * half, 128), half)
    coming = start_copies([(ref, rows.at[i]) for i, ref in enumerate((k_ref, v_ref, q_ref))], sem, 0)
    coming_w = start_copies([(w_ref.at[:, :, :, columns], w_rows)], sem, 3)
    coming_audio = start_copies(
        [
            (ak_ref.at[main], audio.at[pl.ds(0, WIN)]),
            (av_ref.at[main], audio.at[pl.ds(WIN, WIN)]),
            (aq_ref.at[mine], audio.at[pl.ds(QAT, QROWS)]),
            (ak_ref.at[halo], audio.at[pl.ds(HAT, HALO)]),
            (av_ref.at[halo], audio.at[pl.ds(HAT + HALO, HALO)]),
        ],
        sem,
        4,
    )
    heads = [(g, h) for g in range(TOWERS) for h in range(LOCAL)]
    going = []
    for i in (1, 2):
        coming[i].wait()
        pairs = [
            (rows.at[i, :, pl.ds((g * LOCAL + h) * HD, HD)], out.at[g, i, h]) for g, h in heads
        ]
        going += start_copies(pairs, sem, 9 + (i - 1) * H)
    coming[0].wait()
    for g, h in heads:
        block = rows[0, :, pl.ds((g * LOCAL + h) * HD, HD)]
        turned[g, h] = block.astype(jnp.float32).T.astype(jnp.bfloat16)
    going += start_copies([(turned.at[g], out.at[g, 0]) for g in range(TOWERS)], sem, 33)
    coming_w[0].wait()
    going += start_copies([(w_rows.at[0], self_out), (w_rows.at[pl.ds(1, 2)], rest_out)], sem, 37)
    for copy in coming_audio:
        copy.wait()
    pairs = []
    for step, (main_out, halo_out) in enumerate(
        ((main0, halo0), (main1, halo1), (main2, halo2), (main3, halo3))
    ):
        group = pl.ds(pl.multiple_of(lax.rem(tower + step, TOWERS) * GW, 128), GW)
        pairs.append((audio.at[pl.ds(0, HAT), group], main_out))
        pairs.append((audio.at[pl.ds(HAT, 2 * HALO), group], halo_out))
    going += start_copies(pairs, sem, 39)
    for copy in going:
        copy.wait()


def pack(place, k, v, q, ak, av, aq, w):
    rows = k.shape[0]
    narrow = (LOCAL, w.shape[2], w.shape[3] // 2)
    shapes = [(TOWERS, 3, LOCAL, rows, HD), narrow, (2,) + narrow]
    shapes += [(HAT, GW)] * TOWERS + [(2 * HALO, GW)] * TOWERS
    return pl.pallas_call(
        pack_kernel,
        out_shape=[jax.ShapeDtypeStruct(shape, jnp.bfloat16) for shape in shapes],
        grid_spec=pltpu.PrefetchScalarGridSpec(
            num_scalar_prefetch=1,
            grid=(1,),
            in_specs=[ANY] * 7,
            out_specs=[ANY] * len(shapes),
            scratch_shapes=[
                pltpu.VMEM((3,) + k.shape, jnp.bfloat16),
                pltpu.VMEM((TOWERS, LOCAL, HD, rows), jnp.bfloat16),
                pltpu.VMEM((AROWS, aq.shape[1]), jnp.bfloat16),
                pltpu.VMEM((3,) + narrow, jnp.bfloat16),
                pltpu.SemaphoreType.DMA((47,)),
            ],
        ),
        compiler_params=pltpu.CompilerParams(vmem_limit_bytes=60 * MIB),
        name="pack",
    )(place, k, v, q, ak, av, aq, w)


def ctx_towers(pairs):
    return [(c * TOWERS + s, c * TOWERS + d) for c, s, d in pairs]


def send_main(value, step):
    pairs = [(c, c // 4, (c // 4 + step) % TOWERS) for c in range(16)]
    return lax.ppermute(value, ("ctx", "tower"), ctx_towers(pairs))


def send_halo(value, step):
    pairs = []
    for c in range(16):
        source = c // 4 - 1 if c % 4 == 0 else c // 4 + 1
        if c % 4 in (0, 3) and 0 <= source < TOWERS:
            pairs.append((c, source, (source + step) % TOWERS))
    return lax.ppermute(value, ("ctx", "tower"), ctx_towers(pairs))


def keys_of(kv_ref):
    return jnp.concatenate([kv_ref[r, 0, 0] for r in range(TOWERS)], axis=1)


def rows_of(kv_ref, which):
    return jnp.concatenate([kv_ref[r, which, 0] for r in range(TOWERS)], axis=0)


def lane_tiles(x):
    return [x[:, i : i + HD] for i in range(0, x.shape[1], HD)]


def flash_kernel(kv_count, first, last, after, *refs):
    q_ref = refs[0]
    kv_refs = [ref.at[i] for ref in refs[1 : 1 + kv_count] for i in range(ref.shape[0])]
    rest = refs[1 + kv_count :]
    rest = rest[: len(rest) - (1 if last else 4) - after] + rest[len(rest) - (1 if last else 4) :]
    if first:
        outs = rest
    else:
        acc_in, top_in, total_in = rest[:3]
        outs = rest[3:]
    size = 2 * VBLK
    tiles = [slice(i * size, (i + 1) * size) for i in range(2)]
    query = rows_of(q_ref, 0)
    keys = [keys_of(kv) for kv in kv_refs]
    all_scores = [[nn_dot(query[rows], k) for k in keys] for rows in tiles]
    for rows, scores in zip(tiles, all_scores):
        top = functools.reduce(jnp.maximum, [t for s in scores for t in lane_tiles(s)])
        top = jnp.max(top, axis=1, keepdims=True) * SCALE2
        if first:
            top = jnp.broadcast_to(top, (size, HD))
            acc = total = None
        else:
            top = jnp.maximum(top, top_in[rows])
            factor = jnp.exp2(top_in[rows] - top)
            acc = acc_in[rows] * factor
            total = total_in[rows] * factor
        wide = jnp.concatenate([top] * TOWERS, axis=1)
        for s, kv in zip(scores, kv_refs):
            weights = jnp.exp2(s * SCALE2 - wide)
            part = functools.reduce(jnp.add, lane_tiles(weights))
            total = part if total is None else total + part
            part = nn_dot(weights.astype(jnp.bfloat16), rows_of(kv, 1))
            acc = part if acc is None else acc + part
        if last:
            outs[0][rows] = (acc / jnp.sum(total, axis=1, keepdims=True)).astype(jnp.bfloat16)
        else:
            outs[0][rows] = acc
            outs[1][rows] = top
            outs[2][rows] = total
            outs[3][...] = total[:8]


QUERY = pl.BlockSpec((TOWERS, 1, 1, VBLK, HD), lambda h, *_: (0, 2, h, 0, 0))


def shards_spec(count):
    return pl.BlockSpec((count, TOWERS, 2, 1, VBLK, HD), lambda h, *_: (0, 0, 0, h, 0, 0))


def shard_spec(which):
    return pl.BlockSpec((None, TOWERS, 2, 1, VBLK, HD), lambda h, *_: (which, 0, 0, h, 0, 0))


def flash(query, kvs, state, last, after=()):
    rows = TOWERS * VBLK
    keys = rows * len(kvs)
    wide = jax.ShapeDtypeStruct((rows, GW), jnp.float32)
    head = pl.BlockSpec((rows, HD), lambda h: (0, h))
    if last:
        out_shape = jax.ShapeDtypeStruct((rows, GW), jnp.bfloat16)
        out_specs = head
    else:
        out_shape = [wide, wide, wide, jax.ShapeDtypeStruct((8, HD), jnp.float32)]
        out_specs = [head, head, head, pl.BlockSpec((8, HD), lambda h: (0, 0))]
    return pl.pallas_call(
        functools.partial(flash_kernel, len(kvs), state is None, last, len(after)),
        out_shape=out_shape,
        grid=(LOCAL,),
        in_specs=[QUERY] + [shards_spec(kv.shape[0]) for kv in kvs] + ([] if state is None else [head] * 3) + [ANY] * len(after),
        out_specs=out_specs,
        compiler_params=pltpu.CompilerParams(vmem_limit_bytes=60 * MIB),
        cost_estimate=BRIEF,
        name="flash",
    )(query, *kvs, *(() if state is None else state), *after)


AUDIO_ROWS = 32
BOTH = VBLK + AUDIO_ROWS


def weighted(scores, values):
    weights = jnp.exp2(scores - jnp.max(scores, axis=1, keepdims=True)).astype(jnp.bfloat16)
    result = nn_dot(weights, jnp.concatenate([values, jnp.ones_like(values)], axis=1))
    return result[:, :HD] / result[:, HD:]


def audio_rows(place, margin, main, own, sibling, third):
    ctx = place[0]
    core = lax.rem(ctx, 2)
    row_block = lax.broadcasted_iota(jnp.int32, (QROWS, 1), 0) // ABLK + ctx * 4
    query = main[QAT:]
    pieces = [(own, r, ctx * 4 + r) for r in range(TOWERS)]
    after = lax.rem(ctx + 1, 16) * 4
    before = lax.rem(ctx + 15, 16) * 4 + 2
    for r in range(2):
        pieces.append((sibling, 2 * core + r, jnp.where(core == 0, after, before) + r))
        pieces.append((third, 2 - 2 * core + r, jnp.where(core == 0, before, after) + r))
    keys = jnp.concatenate([ref[r, 0, 0] for ref, r, _ in pieces], axis=1)
    values = jnp.concatenate([ref[r, 1, 0] for ref, r, _ in pieces], axis=0)
    raw = nn_dot(query, keys) * SCALE2
    scores = []
    for i, (_, _, block) in enumerate(pieces):
        hit = (
            (row_block == margin[block, 0])
            | (row_block == margin[block, 1])
            | (row_block == margin[block, 2])
        )
        scores.append(jnp.where(hit, raw[:, i * VBLK : (i + 1) * VBLK], NEG))
    scores = jnp.concatenate(scores, axis=1)
    return weighted(scores, values)


def cross_kernel(place, margin, q_ref, *refs):
    mains, halos, (own, sibling, third, out) = refs[:4], refs[4:8], refs[8:]
    main = functools.reduce(
        jnp.add, [ref[...] for ref in mains[1:]], jnp.where(place[1] == place[2], mains[0][...], 0)
    )
    halo = functools.reduce(
        jnp.add, [ref[...] for ref in halos[1:]], jnp.where(place[1] == place[3], halos[0][...], 0)
    )
    ctx = place[0]
    phase = lax.rem(ctx, 4)
    base = (ctx - phase) * 4
    lane = lax.broadcasted_iota(jnp.int32, (1, 256), 1)
    halo_base = jnp.where(phase == 0, base - 2, jnp.where(phase == 3, base + 16, -100))
    main_base = base + lax.div(main_first(ctx), ABLK)
    ids = jnp.where(lane < WIN, lane // ABLK + main_base, lane // ABLK - WIN // ABLK + halo_base)
    ids = jnp.where(lane < WIN + HALO, ids, -100)
    spare = jnp.zeros((256 - WIN - HALO, HD), jnp.bfloat16)
    keys = jnp.concatenate([main[:WIN], halo[:HALO], spare], axis=0)
    values = jnp.concatenate(
        [main[WIN:QAT], halo[HALO:], spare], axis=0
    )
    scores = nt_dot(rows_of(q_ref, 0), keys) * SCALE2
    parts = []
    for r in range(TOWERS):
        block = ctx * 4 + r
        hit = (ids == margin[block, 0]) | (ids == margin[block, 1]) | (ids == margin[block, 2])
        parts.append(jnp.where(hit, scores[r * VBLK : (r + 1) * VBLK], NEG))
    scores = jnp.concatenate(parts, axis=0)
    result = weighted(scores, values).astype(jnp.bfloat16)
    mixed = audio_rows(place, margin, main, own, sibling, third)
    for r in range(TOWERS):
        out[r, pl.ds(0, VBLK), :] = result[r * VBLK : (r + 1) * VBLK]
        padded = jnp.concatenate(
            [mixed[r * ABLK : (r + 1) * ABLK], jnp.zeros((AUDIO_ROWS - ABLK, HD), jnp.float32)], axis=0
        )
        out[r, pl.ds(VBLK, AUDIO_ROWS), :] = padded.astype(jnp.bfloat16)


def cross(place, margin, query, mains, halos, here, behind):
    rows = TOWERS * VBLK
    return pl.pallas_call(
        cross_kernel,
        out_shape=jax.ShapeDtypeStruct((TOWERS, BOTH, GW), jnp.bfloat16),
        grid_spec=pltpu.PrefetchScalarGridSpec(
            num_scalar_prefetch=2,
            grid=(LOCAL,),
            in_specs=[
                QUERY,
            ]
            + [pl.BlockSpec((HAT, HD), lambda h, *_: (0, h))] * TOWERS
            + [pl.BlockSpec((2 * HALO, HD), lambda h, *_: (0, h))] * TOWERS
            + [shard_spec(0), shard_spec(1), shard_spec(1)],
            out_specs=pl.BlockSpec((TOWERS, BOTH, HD), lambda h, *_: (0, 0, h)),
        ),
        compiler_params=pltpu.CompilerParams(vmem_limit_bytes=60 * MIB),
        cost_estimate=BRIEF,
        name="cross",
    )(place, margin, query, *mains, *halos, here, here, behind)


def weight_rows(pieces):
    return jnp.concatenate([piece(h) for h in range(LOCAL) for piece in pieces], axis=0)


def project_cross_kernel(place, own, sibling, w_ref, _, __, mine, up, down, up_first, down_first):
    towers = [lax.rem(place[1] + step, TOWERS) for step in range(TOWERS)]
    targets = (
        (mine, 0),
        (mine, BOTH),
        (up, 0),
        (up, BOTH),
        (up_first, 0),
        (down_first, 0),
        (down, 0),
        (down, BOTH),
    )
    ws = [
        weight_rows([functools.partial(lambda b, h: w_ref[b, kind, h], b) for b in range(4)])
        for kind in range(2)
    ]
    for step in range(TOWERS):
        for w, (first, count) in zip(ws, ((0, VBLK), (VBLK, AUDIO_ROWS))):
            both = [ref[towers[step], pl.ds(first, count), :] for ref in (own, sibling)]
            y = nn_dot(jnp.concatenate(both, axis=0), w).astype(jnp.bfloat16)
            for i in range(2):
                out, at = targets[2 * step + i]
                out[pl.ds(at + first, count), :] = y[i * count : (i + 1) * count]


def project_cross(place, own, sibling, w, after):
    width = w.shape[-1]
    tile = width // 3
    return pl.pallas_call(
        project_cross_kernel,
        out_shape=[jax.ShapeDtypeStruct((n * BOTH, width), jnp.bfloat16) for n in (2, 2, 2, 1, 1)],
        grid_spec=pltpu.PrefetchScalarGridSpec(
            num_scalar_prefetch=1,
            grid=(3,),
            in_specs=[
                full(own.shape),
                full(own.shape),
                pl.BlockSpec(w.shape[:-1] + (tile,), lambda i, place: (0, 0, 0, 0, i)),
                ANY,
                ANY,
            ],
            out_specs=[
                pl.BlockSpec((n * BOTH, tile), lambda i, place: (0, i)) for n in (2, 2, 2, 1, 1)
            ],
        ),
        compiler_params=pltpu.CompilerParams(vmem_limit_bytes=60 * MIB),
        cost_estimate=BRIEF,
        name="project_cross",
    )(place, own, sibling, w, *after)


def project_self_kernel(place, own, sibling, w_ref, *refs):
    mine, up, down, gain, video_out, audio_out, sibling_out = refs
    a = jnp.concatenate(
        [jnp.concatenate([ref[t] for t in range(TOWERS)], axis=1) for ref in (own, sibling)], axis=0
    )
    w = jnp.concatenate(
        [
            weight_rows([functools.partial(lambda b, h: w_ref[b * TOWERS + t, h], b) for b in range(4)])
            for t in range(TOWERS)
        ],
        axis=0,
    )
    acc = nn_dot(a, w)
    base = functools.reduce(jnp.add, [ref[...].astype(jnp.float32) for ref in (mine, up, down)])
    video, audio = [], []
    for i in range(2):
        video.append(gain[0:1] * (acc[i * VBLK : (i + 1) * VBLK] + base[i * BOTH : i * BOTH + VBLK]))
        audio.append(gain[1:2] * base[i * BOTH + VBLK : (i + 1) * BOTH])
    video_out[...] = video[0].astype(jnp.bfloat16)
    audio_out[...] = audio[0][:ABLK].astype(jnp.bfloat16)
    sibling_out[pl.ds(0, VBLK), :] = video[1].astype(jnp.bfloat16)
    sibling_out[pl.ds(VBLK, AUDIO_ROWS), :] = audio[1].astype(jnp.bfloat16)


def project_self(place, own, sibling, w, base, gains):
    width = w.shape[-1]
    tile = width // 3
    out = lambda rows: pl.BlockSpec((rows, tile), lambda i, place: (0, place[4] * 3 + i))
    return pl.pallas_call(
        project_self_kernel,
        out_shape=[
            jax.ShapeDtypeStruct((VBLK, 2 * width), jnp.bfloat16),
            jax.ShapeDtypeStruct((ABLK, 2 * width), jnp.bfloat16),
            jax.ShapeDtypeStruct((BOTH, width), jnp.bfloat16),
        ],
        grid_spec=pltpu.PrefetchScalarGridSpec(
            num_scalar_prefetch=1,
            grid=(3,),
            in_specs=[
                full(own.shape),
                full(own.shape),
                pl.BlockSpec(w.shape[:-1] + (tile,), lambda i, place: (0, 0, 0, i)),
            ]
            + [pl.BlockSpec((2 * BOTH, tile), lambda i, place: (0, i))] * 3
            + [pl.BlockSpec((2, tile), lambda i, place: (0, place[4] * 3 + i))],
            out_specs=[out(VBLK), out(ABLK), pl.BlockSpec((BOTH, tile), lambda i, place: (0, i))],
        ),
        compiler_params=pltpu.CompilerParams(vmem_limit_bytes=60 * MIB),
        cost_estimate=BRIEF,
        name="project_self",
    )(place, own, sibling, w, *base, gains)


def assemble_kernel(place, video_in, audio_in, theirs, video, audio):
    video[...] = theirs[pl.ds(0, VBLK), :]
    audio[...] = theirs[pl.ds(VBLK, AUDIO_ROWS), :].astype(jnp.float32)[:ABLK].astype(jnp.bfloat16)


def assemble(place, video, audio, theirs):
    width = theirs.shape[1]

    def column(i, place):
        return (0, 1 - place[4])

    return pl.pallas_call(
        assemble_kernel,
        out_shape=[jax.ShapeDtypeStruct(x.shape, x.dtype) for x in (video, audio)],
        grid_spec=pltpu.PrefetchScalarGridSpec(
            num_scalar_prefetch=1,
            grid=(1,),
            in_specs=[ANY, ANY, full(theirs.shape)],
            out_specs=[pl.BlockSpec((VBLK, width), column), pl.BlockSpec((ABLK, width), column)],
        ),
        input_output_aliases={1: 0, 2: 1},
        compiler_params=pltpu.CompilerParams(vmem_limit_bytes=16 * MIB),
        name="assemble",
    )(place, video, audio, theirs)


def gate_kernel(*refs):
    pass


def gate(value, *after):
    return pl.pallas_call(
        gate_kernel,
        out_shape=jax.ShapeDtypeStruct(value.shape, value.dtype),
        in_specs=[ANY] * (1 + len(after)),
        out_specs=ANY,
        input_output_aliases={0: 0},
        compiler_params=pltpu.CompilerParams(vmem_limit_bytes=60 * MIB),
        name="gate",
    )(value, *after)


def exchange_towers(value):
    return lax.all_to_all(value, "tower", split_axis=0, concat_axis=0, tiled=True)


def add_kernel(up, down, up_first, down_first, up_out, down_out):
    for a, b, out in ((up, up_first, up_out), (down, down_first, down_out)):
        out[...] = (a[...].astype(jnp.float32) + b[...].astype(jnp.float32)).astype(jnp.bfloat16)


def add_halves(up, down, up_first, down_first):
    rows, width = up_first.shape
    tile = width // 3
    first = pl.BlockSpec((rows, tile), lambda i: (0, i))
    second = pl.BlockSpec((rows, tile), lambda i: (1, i))
    return pl.pallas_call(
        add_kernel,
        out_shape=[jax.ShapeDtypeStruct(up.shape, up.dtype)] * 2,
        grid=(3,),
        in_specs=[first, second, first, first],
        out_specs=[first, second],
        input_output_aliases={0: 0, 1: 1},
        compiler_params=pltpu.CompilerParams(vmem_limit_bytes=60 * MIB),
        cost_estimate=BRIEF,
        name="add_halves",
    )(up, down, up_first, down_first)


def shift_tower(value, step):
    return lax.ppermute(value, "tower", [(i, (i + step) % TOWERS) for i in range(TOWERS)])


def hop(value):
    total = 2 * CHIPS
    return lax.ppermute(value, "ctx", [(i, (i + 2 - 4 * (i % 2)) % total) for i in range(total)])


def swap_core(value):
    return lax.ppermute(value, "ctx", [(i, i ^ 1) for i in range(2 * CHIPS)])


def shards(video_q, video_k, video_v, audio_q, audio_k, audio_v, margin, out_weight, gate_gains):
    ctx = lax.axis_index("ctx")
    tower = lax.axis_index("tower")
    core = lax.rem(ctx, 2)
    place = jnp.stack([ctx, tower, ctx // 4, edge_tower(ctx), core]).astype(jnp.int32)
    gains = gate_gains[0]
    margins = margin[0]

    parts, w_self, w_rest, *audio = pack(
        place, video_k[0], video_v[0], video_q[0], audio_k[0], audio_v[0], audio_q[0], out_weight
    )
    w_rest = lax.all_gather(w_rest, "batch", axis=0, tiled=False)
    w_self = lax.all_gather(w_self, ("batch", "tower"), axis=0, tiled=False)
    query = exchange_towers(parts)
    own = query[:, :2]
    sibling = swap_core(own)
    here = jnp.stack([own, sibling])
    ahead = hop(here)
    mains = [audio[0]] + [send_main(gate(audio[step], sibling), step) for step in (1, 2, 3)]

    acc, top, total, token = flash(query, [here], None, False)
    halos = [audio[4]] + [send_halo(gate(audio[4 + step], token), step) for step in (1, 2, 3)]
    ahead = gate(ahead, token, *mains[1:], *halos[1:])
    crossed = cross(place, margins, query, mains, halos, here, ahead)
    rest, up, down, up_first, down_first = project_cross(
        place, crossed, swap_core(crossed), w_rest, (token, token)
    )
    up_first, down_first = shift_tower(up_first, 1), shift_tower(down_first, -1)

    behind = [rest]
    after = (rest,)
    for step in range(1, 4):
        if step == 3:
            up, down = add_halves(up, down, up_first, down_first)
            after = (up, down)
        now = [ahead, swap_core(ahead)]
        ahead = hop(ahead if step < 3 else ahead[:1])
        acc, top, total, token = flash(query, now, (acc, top, total), False, after)
        behind.append(token)
        after = ()
        ahead = gate(ahead, behind[step - 1])
    video_self = flash(query, [ahead, swap_core(ahead)], (acc, top, total), True)
    base = (rest, shift_tower(up, 1), shift_tower(down, -1))

    self_all = exchange_towers(video_self.reshape(TOWERS, VBLK, GW))
    video_out, audio_out, theirs = project_self(place, self_all, swap_core(self_all), w_self, base, gains)
    video_out, audio_out = assemble(place, video_out, audio_out, swap_core(theirs))
    return (video_out[None], audio_out[None])


def solution(mesh):
    return jax.shard_map(
        shards,
        mesh=mesh,
        in_specs=(
            P("batch", ("ctx", "tower"), None),
            P("batch", ("ctx", "tower"), None),
            P("batch", ("ctx", "tower"), None),
            P("batch", "tower", None),
            P("batch", "tower", None),
            P("batch", "tower", None),
            P("batch", None, None),
            P(None, "tower", "batch", None),
            P("batch", None, None),
        ),
        out_specs=(P("batch", ("ctx", "tower"), None), P("batch", ("ctx", "tower"), None)),
        check_vma=False,
    )
```

```python
import functools

import jax
import jax.numpy as jnp
from jax import lax
from jax.experimental import pallas as pl
from jax.experimental.pallas import tpu as pltpu
from jax.sharding import PartitionSpec as P

H = 12
HD = 128
VBLK = 128
ABLK = 24
TOWERS = 4
CHIPS = 8
LOCAL = H // TOWERS
GW = LOCAL * HD
NEG = -1e30
SCALE2 = HD**-0.5 * 1.4426950408889634
MIB = 1024 * 1024


def nt_dot(a, b):
    return lax.dot_general(a, b, (((1,), (1,)), ((), ())), preferred_element_type=jnp.float32)


def nn_dot(a, b):
    return jnp.dot(a, b, preferred_element_type=jnp.float32)


def full(shape):
    return pl.BlockSpec(shape, lambda *_: (0,) * len(shape))


BRIEF = pl.CostEstimate(flops=1, bytes_accessed=1, transcendentals=0)
ANY = pl.BlockSpec(memory_space=pl.ANY)


def start_copies(pairs, sem, first):
    copies = [pltpu.make_async_copy(a, b, sem.at[first + i]) for i, (a, b) in enumerate(pairs)]
    for copy in copies:
        copy.start()
    return copies


WIN = 192
HALO = 48
QROWS = 96
QAT = 2 * WIN
HAT = QAT + QROWS
AROWS = HAT + 2 * HALO


def main_first(ctx):
    return jnp.clip(lax.rem(ctx, 4) * QROWS - HALO, 0, 384 - WIN)


def edge_tower(ctx):
    phase = lax.rem(ctx, 4)
    edge = jnp.where(phase == 0, ctx // 4 - 1, ctx // 4 + 1)
    return jnp.where(((phase == 0) | (phase == 3)) & (edge >= 0) & (edge < TOWERS), edge, -1)


def pack_kernel(
    place, k_ref, v_ref, q_ref, ak_ref, av_ref, aq_ref, w_ref,
    out, self_out, rest_out, main0, main1, main2, main3, halo0, halo1, halo2, halo3,
    rows, turned, audio, w_rows, sem,
):
    ctx, tower = place[0], place[1]
    phase = lax.rem(ctx, 4)
    main = pl.ds(pl.multiple_of(main_first(ctx), 16), WIN)
    mine = pl.ds(pl.multiple_of(phase * QROWS, 16), QROWS)
    halo = pl.ds(pl.multiple_of(jnp.where(phase == 0, 384 - HALO, 0), 16), HALO)
    half = w_ref.shape[3] // 2
    columns = pl.ds(pl.multiple_of(place[4] * half, 128), half)
    coming = start_copies([(ref, rows.at[i]) for i, ref in enumerate((k_ref, v_ref, q_ref))], sem, 0)
    coming_w = start_copies([(w_ref.at[:, :, :, columns], w_rows)], sem, 3)
    coming_audio = start_copies(
        [
            (ak_ref.at[main], audio.at[pl.ds(0, WIN)]),
            (av_ref.at[main], audio.at[pl.ds(WIN, WIN)]),
            (aq_ref.at[mine], audio.at[pl.ds(QAT, QROWS)]),
            (ak_ref.at[halo], audio.at[pl.ds(HAT, HALO)]),
            (av_ref.at[halo], audio.at[pl.ds(HAT + HALO, HALO)]),
        ],
        sem,
        4,
    )
    heads = [(g, h) for g in range(TOWERS) for h in range(LOCAL)]
    going = []
    for i in (1, 2):
        coming[i].wait()
        pairs = [
            (rows.at[i, :, pl.ds((g * LOCAL + h) * HD, HD)], out.at[g, i, h]) for g, h in heads
        ]
        going += start_copies(pairs, sem, 9 + (i - 1) * H)
    coming[0].wait()
    for g, h in heads:
        block = rows[0, :, pl.ds((g * LOCAL + h) * HD, HD)]
        turned[g, h] = block.astype(jnp.float32).T.astype(jnp.bfloat16)
    going += start_copies([(turned.at[g], out.at[g, 0]) for g in range(TOWERS)], sem, 33)
    coming_w[0].wait()
    going += start_copies([(w_rows.at[0], self_out), (w_rows.at[pl.ds(1, 2)], rest_out)], sem, 37)
    for copy in coming_audio:
        copy.wait()
    pairs = []
    for step, (main_out, halo_out) in enumerate(
        ((main0, halo0), (main1, halo1), (main2, halo2), (main3, halo3))
    ):
        group = pl.ds(pl.multiple_of(lax.rem(tower + step, TOWERS) * GW, 128), GW)
        pairs.append((audio.at[pl.ds(0, HAT), group], main_out))
        pairs.append((audio.at[pl.ds(HAT, 2 * HALO), group], halo_out))
    going += start_copies(pairs, sem, 39)
    for copy in going:
        copy.wait()


def pack(place, k, v, q, ak, av, aq, w):
    rows = k.shape[0]
    narrow = (LOCAL, w.shape[2], w.shape[3] // 2)
    shapes = [(TOWERS, 3, LOCAL, rows, HD), narrow, (2,) + narrow]
    shapes += [(HAT, GW)] * TOWERS + [(2 * HALO, GW)] * TOWERS
    return pl.pallas_call(
        pack_kernel,
        out_shape=[jax.ShapeDtypeStruct(shape, jnp.bfloat16) for shape in shapes],
        grid_spec=pltpu.PrefetchScalarGridSpec(
            num_scalar_prefetch=1,
            grid=(1,),
            in_specs=[ANY] * 7,
            out_specs=[ANY] * len(shapes),
            scratch_shapes=[
                pltpu.VMEM((3,) + k.shape, jnp.bfloat16),
                pltpu.VMEM((TOWERS, LOCAL, HD, rows), jnp.bfloat16),
                pltpu.VMEM((AROWS, aq.shape[1]), jnp.bfloat16),
                pltpu.VMEM((3,) + narrow, jnp.bfloat16),
                pltpu.SemaphoreType.DMA((47,)),
            ],
        ),
        compiler_params=pltpu.CompilerParams(vmem_limit_bytes=60 * MIB),
        name="pack",
    )(place, k, v, q, ak, av, aq, w)


def ctx_towers(pairs):
    return [(c * TOWERS + s, c * TOWERS + d) for c, s, d in pairs]


def send_main(value, step):
    pairs = [(c, c // 4, (c // 4 + step) % TOWERS) for c in range(16)]
    return lax.ppermute(value, ("ctx", "tower"), ctx_towers(pairs))


def send_halo(value, step):
    pairs = []
    for c in range(16):
        source = c // 4 - 1 if c % 4 == 0 else c // 4 + 1
        if c % 4 in (0, 3) and 0 <= source < TOWERS:
            pairs.append((c, source, (source + step) % TOWERS))
    return lax.ppermute(value, ("ctx", "tower"), ctx_towers(pairs))


def keys_of(kv_ref):
    return jnp.concatenate([kv_ref[r, 0, 0] for r in range(TOWERS)], axis=1)


def rows_of(kv_ref, which):
    return jnp.concatenate([kv_ref[r, which, 0] for r in range(TOWERS)], axis=0)


def lane_tiles(x):
    return [x[:, i : i + HD] for i in range(0, x.shape[1], HD)]


def flash_kernel(kv_count, first, last, after, *refs):
    q_ref = refs[0]
    kv_refs = [ref.at[i] for ref in refs[1 : 1 + kv_count] for i in range(ref.shape[0])]
    rest = refs[1 + kv_count :]
    rest = rest[: len(rest) - (1 if last else 4) - after] + rest[len(rest) - (1 if last else 4) :]
    if first:
        outs = rest
    else:
        acc_in, top_in, total_in = rest[:3]
        outs = rest[3:]
    size = 2 * VBLK
    tiles = [slice(i * size, (i + 1) * size) for i in range(2)]
    query = rows_of(q_ref, 0)
    keys = [keys_of(kv) for kv in kv_refs]
    all_scores = [[nn_dot(query[rows], k) for k in keys] for rows in tiles]
    for rows, scores in zip(tiles, all_scores):
        top = functools.reduce(jnp.maximum, [t for s in scores for t in lane_tiles(s)])
        top = jnp.max(top, axis=1, keepdims=True) * SCALE2
        if first:
            top = jnp.broadcast_to(top, (size, HD))
            acc = total = None
        else:
            top = jnp.maximum(top, top_in[rows])
            factor = jnp.exp2(top_in[rows] - top)
            acc = acc_in[rows] * factor
            total = total_in[rows] * factor
        wide = jnp.concatenate([top] * TOWERS, axis=1)
        for s, kv in zip(scores, kv_refs):
            weights = jnp.exp2(s * SCALE2 - wide)
            part = functools.reduce(jnp.add, lane_tiles(weights))
            total = part if total is None else total + part
            part = nn_dot(weights.astype(jnp.bfloat16), rows_of(kv, 1))
            acc = part if acc is None else acc + part
        if last:
            outs[0][rows] = (acc / jnp.sum(total, axis=1, keepdims=True)).astype(jnp.bfloat16)
        else:
            outs[0][rows] = acc
            outs[1][rows] = top
            outs[2][rows] = total
            outs[3][...] = total[:8]


QUERY = pl.BlockSpec((TOWERS, 1, 1, VBLK, HD), lambda h, *_: (0, 2, h, 0, 0))


def shards_spec(count):
    return pl.BlockSpec((count, TOWERS, 2, 1, VBLK, HD), lambda h, *_: (0, 0, 0, h, 0, 0))


def shard_spec(which):
    return pl.BlockSpec((None, TOWERS, 2, 1, VBLK, HD), lambda h, *_: (which, 0, 0, h, 0, 0))


def flash(query, kvs, state, last, after=()):
    rows = TOWERS * VBLK
    keys = rows * len(kvs)
    wide = jax.ShapeDtypeStruct((rows, GW), jnp.float32)
    head = pl.BlockSpec((rows, HD), lambda h: (0, h))
    if last:
        out_shape = jax.ShapeDtypeStruct((rows, GW), jnp.bfloat16)
        out_specs = head
    else:
        out_shape = [wide, wide, wide, jax.ShapeDtypeStruct((8, HD), jnp.float32)]
        out_specs = [head, head, head, pl.BlockSpec((8, HD), lambda h: (0, 0))]
    return pl.pallas_call(
        functools.partial(flash_kernel, len(kvs), state is None, last, len(after)),
        out_shape=out_shape,
        grid=(LOCAL,),
        in_specs=[QUERY] + [shards_spec(kv.shape[0]) for kv in kvs] + ([] if state is None else [head] * 3) + [ANY] * len(after),
        out_specs=out_specs,
        compiler_params=pltpu.CompilerParams(vmem_limit_bytes=60 * MIB),
        cost_estimate=BRIEF,
        name="flash",
    )(query, *kvs, *(() if state is None else state), *after)


AUDIO_ROWS = 32
BOTH = VBLK + AUDIO_ROWS


def weighted(scores, values):
    weights = jnp.exp2(scores - jnp.max(scores, axis=1, keepdims=True)).astype(jnp.bfloat16)
    result = nn_dot(weights, jnp.concatenate([values, jnp.ones_like(values)], axis=1))
    return result[:, :HD] / result[:, HD:]


def audio_rows(place, margin, main, own, sibling, third):
    ctx = place[0]
    core = lax.rem(ctx, 2)
    row_block = lax.broadcasted_iota(jnp.int32, (QROWS, 1), 0) // ABLK + ctx * 4
    query = main[QAT:]
    pieces = [(own, r, ctx * 4 + r) for r in range(TOWERS)]
    after = lax.rem(ctx + 1, 16) * 4
    before = lax.rem(ctx + 15, 16) * 4 + 2
    for r in range(2):
        pieces.append((sibling, 2 * core + r, jnp.where(core == 0, after, before) + r))
        pieces.append((third, 2 - 2 * core + r, jnp.where(core == 0, before, after) + r))
    keys = jnp.concatenate([ref[r, 0, 0] for ref, r, _ in pieces], axis=1)
    values = jnp.concatenate([ref[r, 1, 0] for ref, r, _ in pieces], axis=0)
    raw = nn_dot(query, keys) * SCALE2
    scores = []
    for i, (_, _, block) in enumerate(pieces):
        hit = (
            (row_block == margin[block, 0])
            | (row_block == margin[block, 1])
            | (row_block == margin[block, 2])
        )
        scores.append(jnp.where(hit, raw[:, i * VBLK : (i + 1) * VBLK], NEG))
    scores = jnp.concatenate(scores, axis=1)
    return weighted(scores, values)


def cross_kernel(place, margin, q_ref, *refs):
    mains, halos, (own, sibling, third, out) = refs[:4], refs[4:8], refs[8:]
    main = functools.reduce(
        jnp.add, [ref[...] for ref in mains[1:]], jnp.where(place[1] == place[2], mains[0][...], 0)
    )
    halo = functools.reduce(
        jnp.add, [ref[...] for ref in halos[1:]], jnp.where(place[1] == place[3], halos[0][...], 0)
    )
    ctx = place[0]
    phase = lax.rem(ctx, 4)
    base = (ctx - phase) * 4
    lane = lax.broadcasted_iota(jnp.int32, (1, 256), 1)
    halo_base = jnp.where(phase == 0, base - 2, jnp.where(phase == 3, base + 16, -100))
    main_base = base + lax.div(main_first(ctx), ABLK)
    ids = jnp.where(lane < WIN, lane // ABLK + main_base, lane // ABLK - WIN // ABLK + halo_base)
    ids = jnp.where(lane < WIN + HALO, ids, -100)
    spare = jnp.zeros((256 - WIN - HALO, HD), jnp.bfloat16)
    keys = jnp.concatenate([main[:WIN], halo[:HALO], spare], axis=0)
    values = jnp.concatenate(
        [main[WIN:QAT], halo[HALO:], spare], axis=0
    )
    scores = nt_dot(rows_of(q_ref, 0), keys) * SCALE2
    parts = []
    for r in range(TOWERS):
        block = ctx * 4 + r
        hit = (ids == margin[block, 0]) | (ids == margin[block, 1]) | (ids == margin[block, 2])
        parts.append(jnp.where(hit, scores[r * VBLK : (r + 1) * VBLK], NEG))
    scores = jnp.concatenate(parts, axis=0)
    result = weighted(scores, values).astype(jnp.bfloat16)
    mixed = audio_rows(place, margin, main, own, sibling, third)
    for r in range(TOWERS):
        out[r, pl.ds(0, VBLK), :] = result[r * VBLK : (r + 1) * VBLK]
        padded = jnp.concatenate(
            [mixed[r * ABLK : (r + 1) * ABLK], jnp.zeros((AUDIO_ROWS - ABLK, HD), jnp.float32)], axis=0
        )
        out[r, pl.ds(VBLK, AUDIO_ROWS), :] = padded.astype(jnp.bfloat16)


def cross(place, margin, query, mains, halos, here, behind):
    rows = TOWERS * VBLK
    return pl.pallas_call(
        cross_kernel,
        out_shape=jax.ShapeDtypeStruct((TOWERS, BOTH, GW), jnp.bfloat16),
        grid_spec=pltpu.PrefetchScalarGridSpec(
            num_scalar_prefetch=2,
            grid=(LOCAL,),
            in_specs=[
                QUERY,
            ]
            + [pl.BlockSpec((HAT, HD), lambda h, *_: (0, h))] * TOWERS
            + [pl.BlockSpec((2 * HALO, HD), lambda h, *_: (0, h))] * TOWERS
            + [shard_spec(0), shard_spec(1), shard_spec(1)],
            out_specs=pl.BlockSpec((TOWERS, BOTH, HD), lambda h, *_: (0, 0, h)),
        ),
        compiler_params=pltpu.CompilerParams(vmem_limit_bytes=60 * MIB),
        cost_estimate=BRIEF,
        name="cross",
    )(place, margin, query, *mains, *halos, here, here, behind)


def weight_rows(pieces):
    return jnp.concatenate([piece(h) for h in range(LOCAL) for piece in pieces], axis=0)


def project_cross_kernel(place, own, sibling, w_ref, _, __, mine, up, down, up_first, down_first):
    towers = [lax.rem(place[1] + step, TOWERS) for step in range(TOWERS)]
    targets = (
        (mine, 0),
        (mine, BOTH),
        (up, 0),
        (up, BOTH),
        (up_first, 0),
        (down_first, 0),
        (down, 0),
        (down, BOTH),
    )
    ws = [
        weight_rows([functools.partial(lambda b, h: w_ref[b, kind, h], b) for b in range(4)])
        for kind in range(2)
    ]
    for step in range(TOWERS):
        for w, (first, count) in zip(ws, ((0, VBLK), (VBLK, AUDIO_ROWS))):
            both = [ref[towers[step], pl.ds(first, count), :] for ref in (own, sibling)]
            y = nn_dot(jnp.concatenate(both, axis=0), w).astype(jnp.bfloat16)
            for i in range(2):
                out, at = targets[2 * step + i]
                out[pl.ds(at + first, count), :] = y[i * count : (i + 1) * count]


def project_cross(place, own, sibling, w, after):
    width = w.shape[-1]
    tile = width // 3
    return pl.pallas_call(
        project_cross_kernel,
        out_shape=[jax.ShapeDtypeStruct((n * BOTH, width), jnp.bfloat16) for n in (2, 2, 2, 1, 1)],
        grid_spec=pltpu.PrefetchScalarGridSpec(
            num_scalar_prefetch=1,
            grid=(3,),
            in_specs=[
                full(own.shape),
                full(own.shape),
                pl.BlockSpec(w.shape[:-1] + (tile,), lambda i, place: (0, 0, 0, 0, i)),
                ANY,
                ANY,
            ],
            out_specs=[
                pl.BlockSpec((n * BOTH, tile), lambda i, place: (0, i)) for n in (2, 2, 2, 1, 1)
            ],
        ),
        compiler_params=pltpu.CompilerParams(vmem_limit_bytes=60 * MIB),
        cost_estimate=BRIEF,
        name="project_cross",
    )(place, own, sibling, w, *after)


def project_self_kernel(place, own, sibling, w_ref, *refs):
    mine, up, down, gain, video_out, audio_out, sibling_out = refs
    a = jnp.concatenate(
        [jnp.concatenate([ref[t] for t in range(TOWERS)], axis=1) for ref in (own, sibling)], axis=0
    )
    w = jnp.concatenate(
        [
            weight_rows([functools.partial(lambda b, h: w_ref[b * TOWERS + t, h], b) for b in range(4)])
            for t in range(TOWERS)
        ],
        axis=0,
    )
    acc = nn_dot(a, w)
    base = functools.reduce(jnp.add, [ref[...].astype(jnp.float32) for ref in (mine, up, down)])
    video, audio = [], []
    for i in range(2):
        video.append(gain[0:1] * (acc[i * VBLK : (i + 1) * VBLK] + base[i * BOTH : i * BOTH + VBLK]))
        audio.append(gain[1:2] * base[i * BOTH + VBLK : (i + 1) * BOTH])
    video_out[...] = video[0].astype(jnp.bfloat16)
    audio_out[...] = audio[0][:ABLK].astype(jnp.bfloat16)
    sibling_out[pl.ds(0, VBLK), :] = video[1].astype(jnp.bfloat16)
    sibling_out[pl.ds(VBLK, AUDIO_ROWS), :] = audio[1].astype(jnp.bfloat16)


def project_self(place, own, sibling, w, base, gains):
    width = w.shape[-1]
    tile = width // 3
    out = lambda rows: pl.BlockSpec((rows, tile), lambda i, place: (0, place[4] * 3 + i))
    return pl.pallas_call(
        project_self_kernel,
        out_shape=[
            jax.ShapeDtypeStruct((VBLK, 2 * width), jnp.bfloat16),
            jax.ShapeDtypeStruct((ABLK, 2 * width), jnp.bfloat16),
            jax.ShapeDtypeStruct((BOTH, width), jnp.bfloat16),
        ],
        grid_spec=pltpu.PrefetchScalarGridSpec(
            num_scalar_prefetch=1,
            grid=(3,),
            in_specs=[
                full(own.shape),
                full(own.shape),
                pl.BlockSpec(w.shape[:-1] + (tile,), lambda i, place: (0, 0, 0, i)),
            ]
            + [pl.BlockSpec((2 * BOTH, tile), lambda i, place: (0, i))] * 3
            + [pl.BlockSpec((2, tile), lambda i, place: (0, place[4] * 3 + i))],
            out_specs=[out(VBLK), out(ABLK), pl.BlockSpec((BOTH, tile), lambda i, place: (0, i))],
        ),
        compiler_params=pltpu.CompilerParams(vmem_limit_bytes=60 * MIB),
        cost_estimate=BRIEF,
        name="project_self",
    )(place, own, sibling, w, *base, gains)


def assemble_kernel(place, video_in, audio_in, theirs, video, audio):
    video[...] = theirs[pl.ds(0, VBLK), :]
    audio[...] = theirs[pl.ds(VBLK, AUDIO_ROWS), :].astype(jnp.float32)[:ABLK].astype(jnp.bfloat16)


def assemble(place, video, audio, theirs):
    width = theirs.shape[1]

    def column(i, place):
        return (0, 1 - place[4])

    return pl.pallas_call(
        assemble_kernel,
        out_shape=[jax.ShapeDtypeStruct(x.shape, x.dtype) for x in (video, audio)],
        grid_spec=pltpu.PrefetchScalarGridSpec(
            num_scalar_prefetch=1,
            grid=(1,),
            in_specs=[ANY, ANY, full(theirs.shape)],
            out_specs=[pl.BlockSpec((VBLK, width), column), pl.BlockSpec((ABLK, width), column)],
        ),
        input_output_aliases={1: 0, 2: 1},
        compiler_params=pltpu.CompilerParams(vmem_limit_bytes=16 * MIB),
        name="assemble",
    )(place, video, audio, theirs)


def gate_kernel(*refs):
    pass


def gate(value, *after):
    return pl.pallas_call(
        gate_kernel,
        out_shape=jax.ShapeDtypeStruct(value.shape, value.dtype),
        in_specs=[ANY] * (1 + len(after)),
        out_specs=ANY,
        input_output_aliases={0: 0},
        compiler_params=pltpu.CompilerParams(vmem_limit_bytes=60 * MIB),
        name="gate",
    )(value, *after)


def exchange_towers(value):
    return lax.all_to_all(value, "tower", split_axis=0, concat_axis=0, tiled=True)


def add_kernel(up, down, up_first, down_first, up_out, down_out):
    for a, b, out in ((up, up_first, up_out), (down, down_first, down_out)):
        out[...] = (a[...].astype(jnp.float32) + b[...].astype(jnp.float32)).astype(jnp.bfloat16)


def add_halves(up, down, up_first, down_first):
    rows, width = up_first.shape
    tile = width // 3
    first = pl.BlockSpec((rows, tile), lambda i: (0, i))
    second = pl.BlockSpec((rows, tile), lambda i: (1, i))
    return pl.pallas_call(
        add_kernel,
        out_shape=[jax.ShapeDtypeStruct(up.shape, up.dtype)] * 2,
        grid=(3,),
        in_specs=[first, second, first, first],
        out_specs=[first, second],
        input_output_aliases={0: 0, 1: 1},
        compiler_params=pltpu.CompilerParams(vmem_limit_bytes=60 * MIB),
        cost_estimate=BRIEF,
        name="add_halves",
    )(up, down, up_first, down_first)


def shift_tower(value, step):
    return lax.ppermute(value, "tower", [(i, (i + step) % TOWERS) for i in range(TOWERS)])


def hop(value):
    total = 2 * CHIPS
    return lax.ppermute(value, "ctx", [(i, (i + 2 - 4 * (i % 2)) % total) for i in range(total)])


def swap_core(value):
    return lax.ppermute(value, "ctx", [(i, i ^ 1) for i in range(2 * CHIPS)])


def shards(video_q, video_k, video_v, audio_q, audio_k, audio_v, margin, out_weight, gate_gains):
    ctx = lax.axis_index("ctx")
    tower = lax.axis_index("tower")
    core = lax.rem(ctx, 2)
    place = jnp.stack([ctx, tower, ctx // 4, edge_tower(ctx), core]).astype(jnp.int32)
    gains = gate_gains[0]
    margins = margin[0]

    parts, w_self, w_rest, *audio = pack(
        place, video_k[0], video_v[0], video_q[0], audio_k[0], audio_v[0], audio_q[0], out_weight
    )
    w_rest = lax.all_gather(w_rest, "batch", axis=0, tiled=False)
    w_self = lax.all_gather(w_self, ("batch", "tower"), axis=0, tiled=False)
    query = exchange_towers(parts)
    own = query[:, :2]
    sibling = swap_core(own)
    here = jnp.stack([own, sibling])
    ahead = hop(here)
    mains = [audio[0]] + [send_main(gate(audio[step], sibling), step) for step in (1, 2, 3)]

    acc, top, total, token = flash(query, [here], None, False)
    halos = [audio[4]] + [send_halo(gate(audio[4 + step], token), step) for step in (1, 2, 3)]
    ahead = gate(ahead, token, *mains[1:], *halos[1:])
    crossed = cross(place, margins, query, mains, halos, here, ahead)
    rest, up, down, up_first, down_first = project_cross(
        place, crossed, swap_core(crossed), w_rest, (token, token)
    )
    up_first, down_first = shift_tower(up_first, 1), shift_tower(down_first, -1)

    behind = [rest]
    after = (rest,)
    for step in range(1, 4):
        if step == 3:
            up, down = add_halves(up, down, up_first, down_first)
            after = (up, down)
        now = [ahead, swap_core(ahead)]
        ahead = hop(ahead if step < 3 else ahead[:1])
        acc, top, total, token = flash(query, now, (acc, top, total), False, after)
        behind.append(token)
        after = ()
        ahead = gate(ahead, behind[0] if step == 1 else behind[2])
    video_self = flash(query, [ahead, swap_core(ahead)], (acc, top, total), True)
    base = (rest, shift_tower(up, 1), shift_tower(down, -1))

    self_all = exchange_towers(video_self.reshape(TOWERS, VBLK, GW))
    video_out, audio_out, theirs = project_self(place, self_all, swap_core(self_all), w_self, base, gains)
    video_out, audio_out = assemble(place, video_out, audio_out, swap_core(theirs))
    return (video_out[None], audio_out[None])


def solution(mesh):
    return jax.shard_map(
        shards,
        mesh=mesh,
        in_specs=(
            P("batch", ("ctx", "tower"), None),
            P("batch", ("ctx", "tower"), None),
            P("batch", ("ctx", "tower"), None),
            P("batch", "tower", None),
            P("batch", "tower", None),
            P("batch", "tower", None),
            P("batch", None, None),
            P(None, "tower", "batch", None),
            P("batch", None, None),
        ),
        out_specs=(P("batch", ("ctx", "tower"), None), P("batch", ("ctx", "tower"), None)),
        check_vma=False,
    )
```
